256 devices in a mesh: row: 16 (over y_hi, x, core), col: 16 (over z, y_lo).
Axes of the slice: x: 4, y: 4 (y_hi: 2, y_lo: 2; y = y_hi * 2 + y_lo), z: 8, core: 2. Of those that a mesh axis runs over, the one named last changes fastest.
Arguments:
- homolog_features: bfloat16 [64, 4096, 256], P('row', 'col'), may hold values from -6 to 6
- presence_indicator: int32 [64, 4096], P('row', 'col'), may hold values from 0 to 1
- polymer_label: int32 [4096], P('col'), may hold values from 0 to 3, as said below
- lowering_matrix: bfloat16 [256, 64], replicated, may hold values from -0.375 to 0.375
- lowering_offset: float32 [64], replicated, may hold values from -3 to 3
- outgoing_matrix: bfloat16 [1024, 128], replicated, may hold values from -0.1875 to 0.1875
- outgoing_offset: float32 [128], replicated, may hold values from -4 to 4
- update_adjoint: bfloat16 [256, 4096, 128], P('row', 'col'), may hold values from -6 to 6
Outputs:
- pair_increment: bfloat16 [256, 4096, 128], P('row', 'col')
- alignment_gradient: bfloat16 [64, 4096, 256], P('row', 'col')
- projector_weight_gradient: float32 [256, 64], replicated
- projector_bias_gradient: float32 [64], replicated
- out_weight_grad: float32 [1024, 128], replicated
- out_bias_grad: float32 [128], replicated
The draws below stay inside these ranges and needn't reach their ends.
Inputs may be any that keep to these rules, and one draw needn't show every extreme that they name: `polymer_label`: never falls along the residues: each chain is one contiguous run.
All inputs are finite; a program needn't handle non-finite values.
Results may differ from the reference program's by a relative error of at most 0.0077.
Values may be sent and summed in bfloat16 or wider, within the bound.
No kernel may reach another device: no remote copies, remote signals or barrier semaphores. Data moves between devices by JAX's collectives and lax.ppermute only.
A program may use at most 64 MiB of HBM per device.

```python
import jax
import jax.numpy as jnp
from jax import lax

FEATURE_DEPTH = 256
HALF_DEPTH = 32
PAIR_CHANNELS = 128
PAIRED = 16
CHAINS = 4
HOMOLOG_TOTAL = 64
BAND = 256
MONOMER_TOTAL = 4096


def draw_presence_indicator(key, part):
    key = jax.random.fold_in(key, 11)
    rolls = jax.random.randint(key, (HOMOLOG_TOTAL, MONOMER_TOTAL), 0, 100)
    limits = 95 - 60 * jnp.arange(HOMOLOG_TOTAL, dtype=jnp.int32) // HOMOLOG_TOTAL
    return (rolls < limits[:, None]).astype(jnp.int32)


def draw_polymer_label(key, part):
    key = jax.random.fold_in(key, 23)
    bounds = jax.random.randint(key, (CHAINS - 1,), 1, MONOMER_TOTAL)
    places = jnp.arange(MONOMER_TOTAL, dtype=jnp.int32)
    return jnp.sum((places[:, None] >= bounds[None, :]).astype(jnp.int32), axis=1).astype(jnp.int32)


def level_of(rng, dims, pieces, smallest, top_value):
    def one(axis_at, parts):
        steps = jax.random.uniform(jax.random.fold_in(jax.random.fold_in(rng, 6), axis_at), (parts,), jnp.float32, smallest / len(pieces), top_value / len(pieces))
        return jnp.repeat(jnp.exp(steps), dims[axis_at] // parts).reshape((-1,) + (1,) * (len(dims) - axis_at - 1))

    factor_of = one(*pieces[0])
    for cut in pieces[1:]:
        factor_of = factor_of * one(*cut)
    return factor_of


def noise(key, extent, scale, limit, pieces=(), held_as=jnp.bfloat16):
    result = scale * jax.random.normal(key, extent, jnp.float32)
    if pieces:
        result = result * level_of(key, extent, pieces, -0.22, 0.18)
    return jnp.clip(result, -limit, limit).astype(held_as)


def setup_inputs(seed: int = 0) -> dict:
    key_of = jax.random.split(jax.random.key(seed), 9)
    return {
        "homolog_features": noise(key_of[0], (HOMOLOG_TOTAL, MONOMER_TOTAL, FEATURE_DEPTH), 1.0, 6.0, ((0, 16), (1, 16))),
        "presence_indicator": draw_presence_indicator(jax.random.fold_in(key_of[8], 71), 0),
        "polymer_label": draw_polymer_label(jax.random.fold_in(key_of[8], 71), 0),
        "lowering_matrix": noise(key_of[3], (FEATURE_DEPTH, 2 * HALF_DEPTH), FEATURE_DEPTH ** -0.5, 0.375),
        "lowering_offset": noise(key_of[4], (2 * HALF_DEPTH,), 0.5, 3.0, (), jnp.float32),
        "outgoing_matrix": noise(key_of[5], (HALF_DEPTH * HALF_DEPTH, PAIR_CHANNELS), (HALF_DEPTH * HALF_DEPTH) ** -0.5, 0.1875),
        "outgoing_offset": noise(key_of[6], (PAIR_CHANNELS,), 1.0, 4.0, (), jnp.float32),
        "update_adjoint": noise(key_of[7], (BAND, MONOMER_TOTAL, PAIR_CHANNELS), 1.0, 6.0, ((0, 16), (1, 16))),
    }


def layer_normalize(values):
    center = values - lax.optimization_barrier(jnp.mean(values, axis=-1, keepdims=True))
    spread = lax.optimization_barrier(jnp.mean(center * center, axis=-1, keepdims=True))
    return center * lax.rsqrt(spread + 1e-05)

def reference(homolog_features, presence_indicator, polymer_label, lowering_matrix, lowering_offset, outgoing_matrix, outgoing_offset, update_adjoint):
    presence_real = homolog_features.astype(jnp.float32)
    normalized_alignment = layer_normalize(presence_real).astype(jnp.bfloat16)
    seq_index = jnp.arange(HOMOLOG_TOTAL, dtype=jnp.int32)
    seq_chain = (seq_index - PAIRED) % CHAINS
    permitted_pairs = (seq_index[:, None] < PAIRED) | (seq_chain[:, None] == polymer_label[None, :])
    active_mask = jnp.where(permitted_pairs & (presence_indicator == 1), 1.0, 0.0).astype(jnp.float32)
    weight_float = lowering_matrix.astype(jnp.float32)
    projected = jnp.einsum('src,ch->shr', normalized_alignment.astype(jnp.float32), weight_float) + lowering_offset[None, :, None]
    proj_pair = (projected * active_mask[:, None, :]).astype(jnp.bfloat16)
    left_all = proj_pair[:, :HALF_DEPTH, :BAND].astype(jnp.float32)
    right_all = proj_pair[:, HALF_DEPTH:, :].astype(jnp.float32)
    counts = jnp.dot(active_mask[:, :BAND].T, active_mask, precision=lax.Precision.HIGHEST)
    divisor = jnp.maximum(counts, 1.0)
    out_tensor = outgoing_matrix.astype(jnp.float32).reshape(HALF_DEPTH, HALF_DEPTH, PAIR_CHANNELS)

    def block_step(carry, block_index):
        right_grad, weight_gradient, bias_gradient = carry
        start = (block_index * 8).astype(jnp.int32)
        left_block = lax.dynamic_slice_in_dim(left_all, start, 8, 2)
        div_block = lax.dynamic_slice_in_dim(divisor, start, 8, 0)[..., None]
        grad_block = lax.dynamic_slice_in_dim(update_adjoint, start, 8, 0).astype(jnp.float32)
        outer = jnp.einsum('sci,sej->icej', left_block, right_all).astype(jnp.bfloat16).astype(jnp.float32)
        before = jnp.einsum('icej,ceo->ijo', outer, out_tensor) + outgoing_offset
        pair_block = (before / div_block).astype(jnp.bfloat16)
        scaled = (grad_block / div_block).astype(jnp.bfloat16).astype(jnp.float32)
        bias_gradient = bias_gradient + lax.optimization_barrier(jnp.sum(scaled, axis=(0, 1)))
        weight_gradient = weight_gradient + jnp.einsum('icej,ijo->ceo', outer, scaled)
        outer_grad = jnp.einsum('ijo,ceo->icej', scaled, out_tensor).astype(jnp.bfloat16).astype(jnp.float32)
        left_grad = jnp.einsum('icej,sej->sci', outer_grad, right_all)
        right_grad = right_grad + jnp.einsum('icej,sci->sej', outer_grad, left_block)
        return ((right_grad, weight_gradient, bias_gradient), (pair_block, left_grad))
    initial = (jnp.zeros((HOMOLOG_TOTAL, HALF_DEPTH, MONOMER_TOTAL), jnp.float32), jnp.zeros((HALF_DEPTH, HALF_DEPTH, PAIR_CHANNELS), jnp.float32), jnp.zeros((PAIR_CHANNELS,), jnp.float32))
    (right_grad, weight_gradient, bias_gradient), (pair_blocks, left_blocks) = lax.scan(block_step, initial, jnp.arange(BAND // 8, dtype=jnp.int32))
    pair_increment = pair_blocks.reshape(BAND, MONOMER_TOTAL, PAIR_CHANNELS)
    left_grad = jnp.transpose(left_blocks, (1, 2, 0, 3)).reshape(HOMOLOG_TOTAL, HALF_DEPTH, BAND)
    left_full = jnp.pad(left_grad, ((0, 0), (0, 0), (0, MONOMER_TOTAL - BAND)))
    both = jnp.concatenate([left_full, right_grad], axis=1)
    proj_grad = (both * active_mask[:, None, :]).astype(jnp.bfloat16).astype(jnp.float32)
    projector_weight_gradient = jnp.einsum('src,shr->ch', normalized_alignment.astype(jnp.float32), proj_grad)
    projector_bias_gradient = lax.optimization_barrier(jnp.sum(proj_grad, axis=(0, 2)))
    normalized_gradient = jnp.einsum('shr,ch->src', proj_grad, weight_float)
    discarded_value, backward_function = jax.vjp(layer_normalize, presence_real)
    alignment_gradient = backward_function(normalized_gradient)[0].astype(jnp.bfloat16)
    return (pair_increment, alignment_gradient, projector_weight_gradient, projector_bias_gradient, weight_gradient.reshape(HALF_DEPTH * HALF_DEPTH, PAIR_CHANNELS), bias_gradient)
```

```python
import jax
import jax.numpy as jnp
from jax import lax
from jax.sharding import PartitionSpec as P

PAIRED = 16
CHAINS = 4
BF = jnp.bfloat16
F32 = jnp.float32
STEP = 4


def layer_normalize(values):
    center = values - jnp.mean(values, axis=-1, keepdims=True)
    spread = jnp.mean(center * center, axis=-1, keepdims=True)
    return center * lax.rsqrt(spread + 1e-05)


def column_spread(block, col_index, cols):
    far = [lax.ppermute(block, "col", [(0, d)]) for d in range(STEP, cols, STEP)]
    block = jnp.where(col_index == 0, block, sum(far[1:], far[0]))
    near = [
        lax.ppermute(block, "col", [(a, a + d) for a in range(0, cols, STEP)])
        for d in range(1, STEP)
    ]
    return jnp.where(col_index % STEP == 0, block, sum(near[1:], near[0]))


def column_collect(block, cols):
    sent = block.astype(BF)
    for d in range(1, STEP):
        block = block + lax.ppermute(
            sent, "col", [(a + d, a) for a in range(0, cols, STEP)]
        ).astype(F32)
    sent = block.astype(BF)
    for d in range(STEP, cols, STEP):
        block = block + lax.ppermute(sent, "col", [(d, 0)]).astype(F32)
    return block


def high_low(values):
    high = values.astype(BF)
    return high, (values - high.astype(F32)).astype(BF)


def per_device(
    homolog_features,
    presence_indicator,
    polymer_label,
    lowering_matrix,
    lowering_offset,
    outgoing_matrix,
    outgoing_offset,
    update_adjoint,
):
    seqs, places, depth = homolog_features.shape
    hidden = lowering_matrix.shape[1] // 2
    channels = outgoing_matrix.shape[1]
    row_dev = update_adjoint.shape[0]
    rows, cols = lax.axis_size("row"), lax.axis_size("col")
    row_index, col_index = lax.axis_index("row"), lax.axis_index("col")

    presence_real = homolog_features.astype(F32)
    normalized_alignment = layer_normalize(presence_real).astype(BF)
    seq_index = row_index * seqs + jnp.arange(seqs, dtype=jnp.int32)
    seq_chain = (seq_index - PAIRED) % CHAINS
    permitted_pairs = (seq_index[:, None] < PAIRED) | (seq_chain[:, None] == polymer_label[None, :])
    active_mask = jnp.where(permitted_pairs & (presence_indicator == 1), 1.0, 0.0).astype(F32)
    projected = (
        jnp.einsum("src,ch->hsr", normalized_alignment, lowering_matrix, preferred_element_type=F32)
        + lowering_offset[:, None, None]
    )
    proj_pair = (projected * active_mask[None]).astype(BF)
    live_own = active_mask.astype(BF)

    pieces = hidden * seqs
    spread = column_spread(
        jnp.concatenate([proj_pair[:hidden].reshape(pieces, places), live_own], axis=0),
        col_index,
        cols,
    )
    per_row = spread.reshape(pieces + seqs, rows, row_dev).transpose(1, 0, 2)
    left_part = per_row[:, :pieces].reshape(rows, pieces * row_dev // places, places)
    live_part = per_row[:, pieces:].reshape(rows, 1, seqs * row_dev)
    live_part = jnp.pad(live_part, ((0, 0), (0, 0), (0, places - seqs * row_dev)))
    lines = left_part.shape[1]
    packed = jnp.concatenate(
        [
            jnp.broadcast_to(proj_pair[hidden:].reshape(1, pieces, places), (rows, pieces, places)),
            left_part,
            jnp.broadcast_to(live_own[None], (rows, seqs, places)),
            live_part,
            jnp.zeros((rows, 16 - lines - seqs - 1, places), BF),
        ],
        axis=1,
    )
    arrived = lax.all_to_all(packed, "row", 0, 0, tiled=True)
    right_cols = (
        arrived[:, :pieces].reshape(rows, hidden, seqs, places).transpose(0, 2, 1, 3)
    ).reshape(rows * seqs, hidden, places)
    left_rows = (
        arrived[:, pieces : pieces + lines]
        .reshape(rows, hidden, seqs, row_dev)
        .transpose(0, 2, 1, 3)
        .reshape(rows * seqs, hidden, row_dev)
    )
    at = pieces + lines
    mask_whole = arrived[:, at : at + seqs].reshape(rows * seqs, places)
    mask_rows = arrived[:, at + seqs, : seqs * row_dev].reshape(rows * seqs, row_dev)
    seq_total = rows * seqs
    counts = jnp.dot(mask_rows.T, mask_whole, preferred_element_type=F32)
    divisor = jnp.maximum(counts, 1.0)
    out_tensor = outgoing_matrix.reshape(hidden, hidden, channels)

    def block_step(carry, block_index):
        right_grad, weight_gradient, bias_gradient = carry
        start = block_index * 8
        left_block = lax.dynamic_slice_in_dim(left_rows, start, 8, 2)
        div_block = lax.dynamic_slice_in_dim(divisor, start, 8, 0)[..., None]
        grad_block = lax.dynamic_slice_in_dim(update_adjoint, start, 8, 0)
        outer = jnp.einsum(
            "sci,sej->icej", left_block, right_cols, preferred_element_type=F32
        ).astype(BF)
        before = (
            jnp.einsum("icej,ceo->ijo", outer, out_tensor, preferred_element_type=F32)
            + outgoing_offset
        )
        pair_block = (before / div_block).astype(BF)
        scaled = (grad_block.astype(F32) / div_block).astype(BF)
        bias_gradient = bias_gradient + jnp.sum(scaled.astype(F32), axis=(0, 1))
        weight_gradient = weight_gradient + jnp.einsum(
            "icej,ijo->ceo", outer, scaled, preferred_element_type=F32
        )
        outer_grad = jnp.einsum(
            "ijo,ceo->icej", scaled, out_tensor, preferred_element_type=F32
        ).astype(BF)
        left_grad = jnp.einsum("icej,sej->sci", outer_grad, right_cols, preferred_element_type=F32)
        right_grad = right_grad + jnp.einsum(
            "icej,sci->sej", outer_grad, left_block, preferred_element_type=F32
        )
        return ((right_grad, weight_gradient, bias_gradient), (pair_block, left_grad))

    initial = (
        jnp.zeros((seq_total, hidden, places), F32),
        jnp.zeros((hidden, hidden, channels), F32),
        jnp.zeros((channels,), F32),
    )
    (right_grad, weight_gradient, bias_gradient), (pair_blocks, left_blocks) = lax.scan(
        block_step, initial, jnp.arange(row_dev // 8, dtype=jnp.int32)
    )
    pair_increment = pair_blocks.reshape(row_dev, places, channels)
    left_grad = jnp.transpose(left_blocks, (1, 2, 0, 3)).reshape(seq_total * hidden * row_dev // places, places)
    left_total = column_collect(left_grad, cols)

    weight_gradient = weight_gradient.reshape(places // channels, -1, channels)
    weight_lines = weight_gradient.shape[1] // rows
    weight_pack = jnp.concatenate(list(weight_gradient), axis=1).reshape(rows, weight_lines, places)
    packed = jnp.concatenate(
        [
            right_grad.astype(BF).reshape(rows, pieces, places),
            weight_pack.astype(BF),
            left_total.astype(BF).reshape(rows, lines, places),
            jnp.zeros((rows, 16 - lines, places), BF),
        ],
        axis=1,
    )
    arrived = lax.all_to_all(packed, "row", 0, 0, tiled=True)
    added = jnp.sum(arrived[:, : pieces + weight_lines].astype(F32), axis=0)
    right_local = added[:pieces].reshape(seqs, hidden, places)
    weight_chunk = added[pieces:].astype(BF)
    at = pieces + weight_lines
    left_local = (
        arrived[:, at : at + lines]
        .reshape(rows, seqs, hidden, row_dev)
        .transpose(1, 2, 0, 3)
        .reshape(seqs, hidden, places)
        .astype(F32)
    )
    left_local = jnp.where(col_index == 0, left_local, 0.0)
    both = jnp.concatenate([left_local, right_local], axis=1)
    proj_grad = (both * active_mask[:, None, :]).astype(BF)
    projector_weight_gradient = jnp.einsum(
        "src,shr->hc", normalized_alignment, proj_grad, preferred_element_type=F32
    )
    projector_bias_gradient = jnp.sum(proj_grad.astype(F32), axis=(0, 2))

    bias_rows = jnp.concatenate(
        list(high_low(bias_gradient)) + list(high_low(projector_bias_gradient)), axis=0
    )
    bias_rows = jnp.pad(bias_rows, (0, 16 * places - bias_rows.shape[0])).reshape(16, places)
    own = jnp.concatenate([projector_weight_gradient.astype(BF), weight_chunk, bias_rows], axis=0)
    count = own.shape[0]
    arrived = lax.all_to_all(
        jnp.broadcast_to(own[None], (cols, count, places)), "col", 0, 0, tiled=True
    )
    added = jnp.sum(arrived.astype(F32), axis=0)
    bias_at = 2 * hidden + weight_lines

    def split_bias(lines_of):
        flat = lines_of.reshape(-1)
        out = flat[:channels] + flat[channels : 2 * channels]
        flat = flat[2 * channels :]
        return out, flat[: 2 * hidden] + flat[2 * hidden : 4 * hidden]

    first, second = split_bias(added[bias_at:])
    bias_rows = jnp.concatenate(list(high_low(first)) + list(high_low(second)), axis=0)
    bias_rows = jnp.pad(bias_rows, (0, 16 * places - bias_rows.shape[0])).reshape(16, places)
    own = jnp.concatenate([added[:bias_at].astype(BF), bias_rows], axis=0)
    arrived = lax.all_to_all(
        jnp.broadcast_to(own[None], (rows, count, places)), "row", 0, 0, tiled=True
    ).astype(F32)
    weight_total = arrived[:, 2 * hidden : bias_at].reshape(rows * weight_lines, places)
    weight_total = jnp.concatenate(
        [weight_total[:, i : i + channels] for i in range(0, places, channels)], axis=0
    )
    projector_total = jnp.sum(arrived[:, : 2 * hidden], axis=0).T
    first, second = split_bias(jnp.sum(arrived[:, bias_at:], axis=0))

    normalized_gradient = jnp.einsum(
        "shr,ch->src", proj_grad, lowering_matrix, preferred_element_type=F32
    )
    discarded_value, backward_function = jax.vjp(layer_normalize, presence_real)
    alignment_gradient = backward_function(normalized_gradient)[0].astype(BF)
    return (
        pair_increment,
        alignment_gradient,
        projector_total,
        second,
        weight_total,
        first,
    )


def solution(mesh):
    in_specs = (
        P("row", "col", None),
        P("row", "col"),
        P("col"),
        P(),
        P(),
        P(),
        P(),
        P("row", "col", None),
    )
    out_specs = (P("row", "col", None), P("row", "col", None), P(), P(), P(), P())
    return jax.shard_map(
        per_device, mesh=mesh, in_specs=in_specs, out_specs=out_specs, check_vma=False
    )
```

```python
import functools

import jax
import jax.numpy as jnp
from jax import lax
from jax.experimental import pallas as pl
from jax.experimental.pallas import tpu as pltpu
from jax.sharding import PartitionSpec as P

PAIRED = 16
CHAINS = 4
BF = jnp.bfloat16
F32 = jnp.float32
STEP = 4


def layer_normalize(values):
    center = values - jnp.mean(values, axis=-1, keepdims=True)
    spread = jnp.mean(center * center, axis=-1, keepdims=True)
    return center * lax.rsqrt(spread + 1e-05)


def column_spread(block, col_index, cols):
    far = [lax.ppermute(block, "col", [(0, d)]) for d in range(STEP, cols, STEP)]
    block = jnp.where(col_index == 0, block, sum(far[1:], far[0]))
    near = [
        lax.ppermute(block, "col", [(a, a + d) for a in range(0, cols, STEP)])
        for d in range(1, STEP)
    ]
    return jnp.where(col_index % STEP == 0, block, sum(near[1:], near[0]))


def column_near(block, cols):
    sent = block.astype(BF)
    parts = [
        lax.ppermute(sent, "col", [(a + d, a) for a in range(0, cols, STEP)])
        for d in range(1, STEP)
    ]
    return block + sum(p.astype(F32) for p in parts)


def column_far(block, cols):
    sent = block.astype(BF)
    parts = [lax.ppermute(sent, "col", [(d, 0)]) for d in range(STEP, cols, STEP)]
    return block + sum(p.astype(F32) for p in parts)


def dot(a, b, lhs, rhs):
    return lax.dot_general(a, b, (((lhs,), (rhs,)), ((), ())), preferred_element_type=F32)


def first_kernel(shape, arrived, adjoint, weights, g_ref, s_ref, d_ref, r_ref, left_ref, bias_ref, r_all, tiles, total):
    src, seqs, hidden, row_dev, places, channels, e_block = shape
    step = pl.program_id(0)
    pieces = seqs * hidden

    @pl.when(step == 0)
    def _():
        lines = src * pieces
        spans = [(h, pl.ds(h * channels, channels)) for h in range(places // channels)]
        for d in range(src):
            for h, span in spans:
                r_all[pl.ds(h * lines + d * pieces, pieces), :] = arrived[d, :pieces, span].astype(F32)
            tiles[pl.ds(d * row_dev, row_dev), :] = arrived[d, pieces : pieces + row_dev, channels:].astype(F32)
        for e in range(hidden):
            for h, span in spans:
                rows = [r_all[pl.ds(h * lines + s * hidden + e, src, stride=pieces), :] for s in range(seqs)]
                r_ref[e, :, span] = jnp.concatenate(rows, axis=0).astype(BF)
        for h, span in spans:
            for d in range(src):
                r_all[pl.ds((h * src + d) * 16, 16), :] = arrived[d, pieces + row_dev :, span].astype(F32)
        live_t = []
        for h, span in spans:
            rows = [r_all[pl.ds(h * src * 16 + s, src, stride=16), :] for s in range(seqs)]
            live_t.append(jnp.concatenate(rows, axis=0).T)
        live_t = jnp.concatenate(live_t, axis=0).astype(BF)
        bias = jnp.zeros((1, channels), F32)
        for i in range(row_dev):
            tile = tiles[pl.ds(i, src, stride=row_dev), :]
            column = jnp.concatenate([tile[:, s * hidden : s * hidden + 1] for s in range(seqs)], axis=0)
            column = jnp.broadcast_to(column, (src * seqs, channels)).astype(BF)
            divisor = jnp.maximum(dot(live_t, column, 1, 0), 1.0)
            scaled = (adjoint[i].astype(F32) / divisor).astype(BF)
            d_ref[i] = divisor.astype(BF)
            s_ref[i] = scaled
            bias = bias + jnp.sum(scaled.astype(F32), axis=0, keepdims=True)
        bias_ref[...] = bias
        total[...] = jnp.zeros_like(total)

    part = weights[pl.ds(step * e_block * hidden, e_block * hidden), :]
    for i in range(row_dev):
        g = dot(part, s_ref[i], 1, 1).astype(BF)
        g_ref[:, pl.ds(i * hidden, hidden), :] = g.reshape(e_block, hidden, places)
    acc = total[...]
    for e in range(e_block):
        acc = acc + dot(r_ref[step * e_block + e], g_ref[e], 1, 1)
    total[...] = acc

    @pl.when(step == pl.num_programs(0) - 1)
    def _():
        for i in range(row_dev):
            block = acc[:, i * hidden : (i + 1) * hidden]
            left_ref[pl.ds(i, src, stride=row_dev), :] = jnp.concatenate(
                [block[s * src : (s + 1) * src] for s in range(seqs)], axis=1
            )


def unpack_left(shape, arrived, tiles, left_ref, left_t_ref):
    src, seqs, hidden, row_dev, places, channels, e_block = shape
    pieces = seqs * hidden
    for d in range(src):
        tiles[pl.ds(d * row_dev, row_dev), :] = arrived[d, pieces : pieces + row_dev, :channels].astype(F32)
    blocks = []
    for i in range(row_dev):
        tile = tiles[pl.ds(i, src, stride=row_dev), :]
        blocks.append(jnp.concatenate([tile[:, s * hidden : (s + 1) * hidden] for s in range(seqs)], axis=0))
    left = jnp.concatenate(blocks, axis=1)
    left_ref[...] = left.astype(BF)
    left_t_ref[...] = left.T.astype(BF)


def second_kernel(shape, arrived, r_ref, s_ref, d_ref, weights_t, offset, pair_ref, wgrad_ref, left_out, tiles, left_t, outer, before):
    src, seqs, hidden, row_dev, places, channels, e_block = shape
    step = pl.program_id(0)

    @pl.when(step == 0)
    def _():
        unpack_left(shape, arrived, tiles, left_out, left_t)
        before[...] = jnp.zeros_like(before)

    for e in range(e_block):
        outer[e] = dot(left_t[...], r_ref[e], 1, 0).astype(BF)
    acc = jnp.zeros((e_block * hidden, channels), F32)
    for i in range(row_dev):
        block = outer[:, pl.ds(i * hidden, hidden), :].reshape(e_block * hidden, places)
        before[i] = before[i] + dot(weights_t[...], block, 1, 0)
        acc = acc + dot(block, s_ref[i], 1, 0)
    wgrad_ref[...] = acc

    @pl.when(step == pl.num_programs(0) - 1)
    def _():
        for i in range(row_dev):
            pair_ref[i] = ((before[i].T + offset[...]) / d_ref[i].astype(F32)).astype(BF)


def third_kernel(shape, left, g_ref, out_ref, held):
    src, seqs, hidden, row_dev, places, channels, e_block = shape
    step = pl.program_id(0)
    for e in range(e_block):
        grad = dot(left[...], g_ref[e], 1, 0)
        for h in range(places // channels):
            for s in range(seqs):
                at = h * src * seqs * hidden + s * hidden + step * e_block + e
                held[pl.ds(at, src, stride=seqs * hidden), :] = grad[
                    s * src : (s + 1) * src, h * channels : (h + 1) * channels
                ]

    @pl.when(step == pl.num_programs(0) - 1)
    def _():
        lines = src * seqs * hidden
        for h in range(places // channels):
            out_ref[:, pl.ds(h * channels, channels)] = held[pl.ds(h * lines, lines), :].astype(BF)


def vmem(*block):
    return pl.BlockSpec(block, lambda t: (0,) * len(block))


def params():
    return pltpu.CompilerParams(dimension_semantics=("arbitrary",), vmem_limit_bytes=52 * 2**20)


def main_first(shape, arrived, adjoint, weights):
    src, seqs, hidden, row_dev, places, channels, e_block = shape
    total, lines = src * seqs, row_dev * hidden
    S = jax.ShapeDtypeStruct
    return pl.pallas_call(
        functools.partial(first_kernel, shape),
        grid=(hidden // e_block,),
        in_specs=[vmem(*arrived.shape), vmem(*adjoint.shape), vmem(*weights.shape)],
        out_specs=[
            pl.BlockSpec((e_block, lines, places), lambda t: (t, 0, 0)),
            vmem(row_dev, places, channels),
            vmem(row_dev, places, channels),
            vmem(hidden, total, places),
            vmem(src * row_dev, channels),
            vmem(1, channels),
        ],
        out_shape=[
            S((hidden, lines, places), BF),
            S((row_dev, places, channels), BF),
            S((row_dev, places, channels), BF),
            S((hidden, total, places), BF),
            S((src * row_dev, channels), F32),
            S((1, channels), F32),
        ],
        scratch_shapes=[
            pltpu.VMEM((total * hidden * places // channels, channels), F32),
            pltpu.VMEM((src * row_dev, channels), F32),
            pltpu.VMEM((total, lines), F32),
        ],
        compiler_params=params(),
        cost_estimate=pl.CostEstimate(flops=2 * 800_000_000, bytes_accessed=16 * 2**20, transcendentals=0),
        name="scaled_outer_grad",
    )(arrived, adjoint, weights)


def main_second(shape, arrived, right, scaled, divisor, weights_t, offset):
    src, seqs, hidden, row_dev, places, channels, e_block = shape
    total, lines = src * seqs, row_dev * hidden
    S = jax.ShapeDtypeStruct
    folds = places // channels
    halves = hidden // e_block // folds
    return pl.pallas_call(
        functools.partial(second_kernel, shape),
        grid=(hidden // e_block,),
        in_specs=[
            vmem(*arrived.shape),
            pl.BlockSpec((e_block, total, places), lambda t: (t, 0, 0)),
            vmem(*scaled.shape),
            vmem(*divisor.shape),
            pl.BlockSpec((channels, e_block * hidden), lambda t: (0, t)),
            vmem(1, channels),
        ],
        out_specs=[
            vmem(row_dev, places, channels),
            pl.BlockSpec((e_block * hidden, channels), lambda t: (t % halves, t // halves)),
            vmem(total, lines),
        ],
        out_shape=[
            S((row_dev, places, channels), BF),
            S((hidden * hidden // folds, places), F32),
            S((total, lines), BF),
        ],
        scratch_shapes=[
            pltpu.VMEM((src * row_dev, channels), F32),
            pltpu.VMEM((lines, total), BF),
            pltpu.VMEM((e_block, lines, places), BF),
            pltpu.VMEM((row_dev, channels, places), F32),
        ],
        compiler_params=params(),
        cost_estimate=pl.CostEstimate(flops=2 * 1_300_000_000, bytes_accessed=8 * 2**20, transcendentals=0),
        name="outer_pair",
    )(arrived, right, scaled, divisor, weights_t, offset)


def main_third(shape, left, outer_grad):
    src, seqs, hidden, row_dev, places, channels, e_block = shape
    total, lines = src * seqs, row_dev * hidden
    return pl.pallas_call(
        functools.partial(third_kernel, shape),
        grid=(hidden // e_block,),
        in_specs=[vmem(total, lines), pl.BlockSpec((e_block, lines, places), lambda t: (t, 0, 0))],
        out_specs=vmem(total * hidden, places),
        out_shape=jax.ShapeDtypeStruct((total * hidden, places), BF),
        scratch_shapes=[pltpu.VMEM((total * hidden * places // channels, channels), F32)],
        compiler_params=params(),
        cost_estimate=pl.CostEstimate(flops=2 * 270_000_000, bytes_accessed=10 * 2**20, transcendentals=0),
        name="right_grad",
    )(left, outer_grad)


def high_low(values):
    high = values.astype(BF)
    return high, (values - high.astype(F32)).astype(BF)


def per_device(
    homolog_features,
    presence_indicator,
    polymer_label,
    lowering_matrix,
    lowering_offset,
    outgoing_matrix,
    outgoing_offset,
    update_adjoint,
):
    seqs, places, depth = homolog_features.shape
    hidden = lowering_matrix.shape[1] // 2
    channels = outgoing_matrix.shape[1]
    row_dev = update_adjoint.shape[0]
    rows, cols = lax.axis_size("row"), lax.axis_size("col")
    row_index, col_index = lax.axis_index("row"), lax.axis_index("col")

    presence_real = homolog_features.astype(F32)
    normalized_alignment = layer_normalize(presence_real).astype(BF)
    seq_index = row_index * seqs + jnp.arange(seqs, dtype=jnp.int32)
    seq_chain = (seq_index - PAIRED) % CHAINS
    permitted_pairs = (seq_index[:, None] < PAIRED) | (seq_chain[:, None] == polymer_label[None, :])
    active_mask = jnp.where(permitted_pairs & (presence_indicator == 1), 1.0, 0.0).astype(F32)
    pieces = seqs * hidden
    tile = row_dev
    right_own = (
        jnp.einsum(
            "src,ch->shr", normalized_alignment, lowering_matrix[:, hidden:], preferred_element_type=F32
        )
        + lowering_offset[hidden:, None]
    )
    right_own = (right_own * active_mask[:, None, :]).astype(BF).reshape(pieces, places)
    live_t = active_mask.T[:, :, None]
    left_own = (
        jnp.einsum(
            "src,ch->rsh", normalized_alignment, lowering_matrix[:, :hidden], preferred_element_type=F32
        )
        + lowering_offset[:hidden]
    )
    left_own = jnp.concatenate(
        [
            (left_own * live_t).astype(BF).reshape(places, pieces),
            jnp.broadcast_to(live_t, left_own.shape).astype(BF).reshape(places, pieces),
        ],
        axis=1,
    )
    spread = column_spread(left_own, col_index, cols)
    live_own = jnp.pad(active_mask.astype(BF), ((0, 16 - seqs), (0, 0)))
    packed = jnp.concatenate(
        [
            jnp.broadcast_to(right_own[None], (rows, pieces, places)),
            spread.reshape(rows, tile, places),
            jnp.broadcast_to(live_own[None], (rows, 16, places)),
        ],
        axis=1,
    )
    arrived = lax.all_to_all(packed, "row", 0, 0, tiled=True)

    shape = (rows, seqs, hidden, row_dev, places, channels, 8)
    weights = outgoing_matrix.reshape(hidden, hidden, channels).transpose(1, 0, 2)
    weights = weights.reshape(hidden * hidden, channels)
    outer_grad, scaled, divisor, right_cols, left_grad, bias_gradient = main_first(
        shape, arrived, update_adjoint, weights
    )
    bias_gradient = bias_gradient[0]

    left_grad = column_near(left_grad, cols)
    pair_increment, weight_gradient, left_rows = main_second(
        shape, arrived, right_cols, scaled, divisor, weights.T, outgoing_offset[None]
    )
    left_grad = column_far(left_grad, cols)
    right_grad = main_third(shape, left_rows, outer_grad)

    weight_lines = weight_gradient.shape[0] // rows
    left_lines = jnp.pad(
        left_grad.astype(BF).reshape(rows, tile, channels), ((0, 0), (0, 0), (0, places - channels))
    )
    packed = jnp.concatenate(
        [
            right_grad.reshape(rows, pieces, places),
            weight_gradient.astype(BF).reshape(rows, weight_lines, places),
            left_lines,
        ],
        axis=1,
    )
    arrived = lax.all_to_all(packed, "row", 0, 0, tiled=True)
    added = jnp.sum(arrived[:, : pieces + weight_lines].astype(F32), axis=0)
    right_local = added[:pieces].reshape(seqs, hidden, places)
    weight_chunk = added[pieces:].astype(BF)
    left_local = arrived[:, pieces + weight_lines :, :channels].reshape(places, seqs, hidden)
    left_local = left_local.transpose(1, 2, 0).astype(F32)
    left_local = jnp.where(col_index == 0, left_local, 0.0)
    both = jnp.concatenate([left_local, right_local], axis=1)
    proj_grad = (both * active_mask[:, None, :]).astype(BF)
    projector_weight_gradient = jnp.einsum(
        "src,shr->hc", normalized_alignment, proj_grad, preferred_element_type=F32
    )
    projector_bias_gradient = jnp.sum(proj_grad.astype(F32), axis=(0, 2))

    bias_rows = jnp.concatenate(
        list(high_low(bias_gradient)) + list(high_low(projector_bias_gradient)), axis=0
    )
    bias_rows = jnp.pad(bias_rows, (0, 16 * places - bias_rows.shape[0])).reshape(16, places)
    own = jnp.concatenate([projector_weight_gradient.astype(BF), weight_chunk, bias_rows], axis=0)
    count = own.shape[0]
    arrived = lax.all_to_all(
        jnp.broadcast_to(own[None], (cols, count, places)), "col", 0, 0, tiled=True
    )
    added = jnp.sum(arrived.astype(F32), axis=0)
    bias_at = 2 * hidden + weight_lines

    def split_bias(lines_of):
        flat = lines_of.reshape(-1)
        out = flat[:channels] + flat[channels : 2 * channels]
        flat = flat[2 * channels :]
        return out, flat[: 2 * hidden] + flat[2 * hidden : 4 * hidden]

    first, second = split_bias(added[bias_at:])
    bias_rows = jnp.concatenate(list(high_low(first)) + list(high_low(second)), axis=0)
    bias_rows = jnp.pad(bias_rows, (0, 16 * places - bias_rows.shape[0])).reshape(16, places)
    own = jnp.concatenate([added[:bias_at].astype(BF), bias_rows], axis=0)
    arrived = lax.all_to_all(
        jnp.broadcast_to(own[None], (rows, count, places)), "row", 0, 0, tiled=True
    ).astype(F32)
    weight_total = arrived[:, 2 * hidden : bias_at].reshape(rows * weight_lines, places)
    weight_total = jnp.concatenate(
        [weight_total[:, i : i + channels] for i in range(0, places, channels)], axis=0
    )
    weight_total = weight_total.reshape(hidden, hidden, channels).transpose(1, 0, 2)
    weight_total = weight_total.reshape(hidden * hidden, channels)
    projector_total = jnp.sum(arrived[:, : 2 * hidden], axis=0).T
    first, second = split_bias(jnp.sum(arrived[:, bias_at:], axis=0))

    normalized_gradient = jnp.einsum(
        "shr,ch->src", proj_grad, lowering_matrix, preferred_element_type=F32
    )
    discarded_value, backward_function = jax.vjp(layer_normalize, presence_real)
    alignment_gradient = backward_function(normalized_gradient)[0].astype(BF)
    return (
        pair_increment,
        alignment_gradient,
        projector_total,
        second,
        weight_total,
        first,
    )


def solution(mesh):
    in_specs = (
        P("row", "col", None),
        P("row", "col"),
        P("col"),
        P(),
        P(),
        P(),
        P(),
        P("row", "col", None),
    )
    out_specs = (P("row", "col", None), P("row", "col", None), P(), P(), P(), P())
    return jax.shard_map(
        per_device, mesh=mesh, in_specs=in_specs, out_specs=out_specs, check_vma=False
    )
```

```python
import functools

import jax
import jax.numpy as jnp
from jax import lax
from jax.experimental import pallas as pl
from jax.experimental.pallas import tpu as pltpu
from jax.sharding import PartitionSpec as P

PAIRED = 16
CHAINS = 4
BF = jnp.bfloat16
F32 = jnp.float32
STEP = 4
GROUP = 16
E_BLOCK = 8


def dot(a, b, lhs, rhs):
    return lax.dot_general(a, b, (((lhs,), (rhs,)), ((), ())), preferred_element_type=F32)


def rows_at(start, size):
    return pl.ds(pl.multiple_of(start, GROUP), size)


def normal(values):
    center = values - jnp.mean(values, axis=-1, keepdims=True)
    spread = jnp.mean(center * center, axis=-1, keepdims=True)
    scale = lax.rsqrt(spread + 1e-05)
    return center * scale, scale


def project_kernel(dims, info, msa, present, label, weights, offset, normed, live_ref, send, keep, right, left):
    src, seqs, hidden, row_dev, places, half = dims
    pairs = src // 2
    me, core = info[0], lax.rem(info[0], 2)
    first = info[1] == 0
    seq = me * seqs + lax.broadcasted_iota(jnp.int32, (seqs, places), 0)
    chain = lax.rem(seq + (CHAINS - PAIRED % CHAINS), CHAINS)
    permitted = (seq < PAIRED) | (chain == jnp.broadcast_to(label[...], (seqs, places)))
    live = jnp.where(permitted & (present[...] == 1), 1.0, 0.0).astype(F32)
    live = jnp.concatenate([live, jnp.zeros((8 - seqs, places), F32)], axis=0)
    live_ref[...] = live
    weight = weights[...].astype(F32)
    right_w = weight[hidden:].astype(BF)
    left_w = jnp.concatenate([weight[:hidden]] * seqs, axis=0).T.astype(BF)
    lane = lax.broadcasted_iota(jnp.int32, left_w.shape, 1) // hidden
    column = jnp.broadcast_to(offset[...], (8, 2 * hidden)).T[hidden:, :1]
    total = jnp.zeros((places, seqs * hidden), F32)
    for s in range(seqs):
        value = normal(msa[s].astype(F32))[0].astype(BF)
        normed[s] = value
        out = (dot(right_w, value, 1, 1) + column) * live[s : s + 1]
        for h in range(2):
            right[pl.ds(h * seqs * hidden + s * hidden, hidden), :] = out[:, h * half : (h + 1) * half]
        total = total + dot(value, jnp.where(lane == s, left_w, jnp.zeros_like(left_w)), 1, 0)
    total = total + jnp.concatenate([offset[:, :hidden]] * seqs, axis=1)
    spot = lax.broadcasted_iota(jnp.int32, (8, seqs * hidden), 0)
    expand = jnp.where(spot == lax.broadcasted_iota(jnp.int32, (8, seqs * hidden), 1) // hidden, 1.0, 0.0)
    total = total * dot(live.T.astype(BF), expand.astype(BF), 1, 0)
    left[...] = jnp.where(first, total, 0.0)
    place = lax.broadcasted_iota(jnp.int32, (places, half), 0)
    slot = lax.broadcasted_iota(jnp.int32, (places, half), 1)
    base = seqs * hidden
    for ref, to in ((send, 1 - core), (keep, core)):
        pick = jnp.where(place == slot // row_dev * 2 * row_dev + to * row_dev + lax.rem(slot, row_dev), 1.0, 0.0)
        band = dot(live.astype(BF), pick.astype(BF), 1, 0)[:seqs]
        band = jnp.where(first, band, 0.0)
        own = jnp.where(to == 0, live[:seqs, :half], live[:seqs, half:])
        flags = jnp.concatenate([own, band, jnp.zeros((GROUP - 2 * seqs, half), F32)], axis=0)
        ref[pl.ds(0, base), :] = right[rows_at(to * base, base), :].astype(BF)
        ref[pl.ds(base, GROUP), :] = flags.astype(BF)
        for q in range(pairs):
            ref[pl.ds(base + GROUP + q * row_dev, row_dev), :] = left[
                rows_at(q * 2 * row_dev + to * row_dev, row_dev), :
            ].astype(BF)


def pack_right_kernel(dims, info, keep, came, out):
    src, seqs, hidden, row_dev, places, half = dims
    core = lax.rem(info[0], 2)
    base = seqs * hidden
    for ref, who in ((keep, core), (came, 1 - core)):
        value = ref[pl.ds(0, base), :]
        flags = ref[pl.ds(base, GROUP), :]
        for q in range(src // 2):
            out[q, rows_at(who * base, base), :] = value
            out[q, rows_at(2 * base + who * GROUP, GROUP), :] = flags


def pack_left_kernel(dims, info, tree, near_1, near_2, near_3, out):
    src, seqs, hidden, row_dev, places, half = dims
    pairs = src // 2
    core = lax.rem(info[0], 2)
    mixed = GROUP + pairs * row_dev
    for n, who in enumerate((core, 1 - core)):
        span = pl.ds(n * mixed, mixed)
        spread = tree[span, :] + near_1[span, :] + near_2[span, :] + near_3[span, :]
        for q in range(pairs):
            out[q, rows_at(who * row_dev, row_dev), :] = spread[GROUP + q * row_dev : GROUP + (q + 1) * row_dev]
            out[q, rows_at(2 * row_dev + who * GROUP, GROUP), :] = spread[:GROUP]


def unpack_right_kernel(dims, info, mine, other, weights, r_ref, live_t_ref, by_e, by_e_t, r_all, flags, w_all):
    src, seqs, hidden, row_dev, places, half = dims
    base = seqs * hidden
    lines = src * base
    core = lax.rem(info[0], 2)
    for ref, h in ((mine, core), (other, 1 - core)):
        for q in range(src // 2):
            r_all[rows_at(h * lines + q * 2 * base, 2 * base), :] = ref[q, : 2 * base, :].astype(F32)
            flags[rows_at((h * src + 2 * q) * GROUP, 2 * GROUP), :] = ref[q, 2 * base :, :].astype(F32)
    w_all[...] = weights[...].astype(F32)
    for e in range(hidden):
        for h in range(2):
            rows = [r_all[pl.ds(h * lines + s * hidden + e, src, stride=base), :] for s in range(seqs)]
            r_ref[e, :, pl.ds(h * half, half)] = jnp.concatenate(rows, axis=0).astype(BF)
    for e in range(0, hidden, 4):
        rows = [w_all[pl.ds(e + n, hidden, stride=hidden), :] for n in range(4)]
        part = jnp.concatenate(rows, axis=0)
        by_e[pl.ds(e * hidden, 4 * hidden), :] = part.astype(BF)
        by_e_t[:, pl.ds(e * hidden, 4 * hidden)] = part.T.astype(BF)
    for h in range(2):
        rows = [flags[pl.ds(h * src * GROUP + s, src, stride=GROUP), :] for s in range(seqs)]
        live_t_ref[pl.ds(h * half, half), :] = jnp.concatenate(rows, axis=0).T.astype(BF)


def first_kernel(dims, info, arrived, r_ref, live_t, adjoint, weights, g_ref, s_ref, d_ref, left_ref, bias_ref, left_out, left_t, tiles, total):
    src, seqs, hidden, row_dev, places, half = dims
    step = pl.program_id(0)

    @pl.when(step == 0)
    def _():
        pair = info[0] // 2
        for q in range(src // 2):
            tiles[pl.ds(q * 2 * GROUP, 2 * GROUP), :] = arrived[q, 2 * row_dev :, :].astype(F32)
        rows = [tiles[pl.ds(seqs + s, src, stride=GROUP), :] for s in range(seqs)]
        band = jnp.concatenate(rows, axis=0).astype(BF)
        for q in range(src // 2):
            tiles[pl.ds(q * 2 * row_dev, 2 * row_dev), :] = arrived[q, : 2 * row_dev, :].astype(F32)
        blocks = []
        for i in range(row_dev):
            tile = tiles[pl.ds(i, src, stride=row_dev), :]
            blocks.append(jnp.concatenate([tile[:, s * hidden : (s + 1) * hidden] for s in range(seqs)], axis=0))
        left = jnp.concatenate(blocks, axis=1)
        left_out[...] = left.astype(BF)
        left_t[...] = left.T.astype(BF)
        spot = lax.broadcasted_iota(jnp.int32, (half, half), 0) - pair * row_dev
        bias = jnp.zeros((1, half), F32)
        for i in range(row_dev):
            column = dot(band, jnp.where(spot == i, 1.0, 0.0).astype(BF), 1, 0).astype(BF)
            divisor = jnp.maximum(dot(live_t[...], column, 1, 0), 1.0)
            scaled = (adjoint[i].astype(F32) / divisor).astype(BF)
            d_ref[i] = divisor.astype(BF)
            s_ref[i] = scaled
            bias = bias + jnp.sum(scaled.astype(F32), axis=0, keepdims=True)
        bias_ref[...] = bias
        total[...] = jnp.zeros_like(total)

    part = weights[pl.ds(step * E_BLOCK * hidden, E_BLOCK * hidden), :]
    for i in range(row_dev):
        g = dot(part, s_ref[i], 1, 1).astype(BF)
        g_ref[:, pl.ds(i * hidden, hidden), :] = g.reshape(E_BLOCK, hidden, places)
    acc = total[...]
    for e in range(E_BLOCK):
        acc = acc + dot(r_ref[step * E_BLOCK + e], g_ref[e], 1, 1)
    total[...] = acc

    @pl.when(step == pl.num_programs(0) - 1)
    def _():
        for i in range(row_dev):
            block = acc[:, i * hidden : (i + 1) * hidden]
            left_ref[pl.ds(i, src, stride=row_dev), :] = jnp.concatenate(
                [block[s * src : (s + 1) * src] for s in range(seqs)], axis=1
            )


def second_kernel(dims, info, left_t, r_ref, s_ref, d_ref, weights_t, offset, pair_ref, keep, send, outer, before, held):
    src, seqs, hidden, row_dev, places, half = dims
    step = pl.program_id(0)
    block_lines = E_BLOCK * hidden

    @pl.when(step == 0)
    def _():
        before[...] = jnp.zeros_like(before)

    for e in range(E_BLOCK):
        outer[e] = dot(left_t[...], r_ref[e], 1, 0).astype(BF)
    acc = jnp.zeros((block_lines, half), F32)
    for i in range(row_dev):
        block = outer[:, pl.ds(i * hidden, hidden), :].reshape(block_lines, places)
        before[i] = before[i] + dot(weights_t[...], block, 1, 0)
        acc = acc + dot(block, s_ref[i], 1, 0)
    held[rows_at(step * block_lines, block_lines), :] = acc

    @pl.when(step == pl.num_programs(0) - 1)
    def _():
        core = lax.rem(info[0], 2)
        lines = hidden * hidden // 2
        keep[...] = held[rows_at(core * lines, lines), :]
        send[...] = held[rows_at((1 - core) * lines, lines), :].astype(BF)
        for i in range(row_dev):
            pair_ref[i] = ((before[i].T + offset[...]) / d_ref[i].astype(F32)).astype(BF)


def third_kernel(dims, info, left, g_ref, keep, send, held):
    src, seqs, hidden, row_dev, places, half = dims
    step = pl.program_id(0)
    base = seqs * hidden
    lines = src * base
    for e in range(E_BLOCK):
        grad = dot(left[...], g_ref[e], 1, 0)
        for h in range(2):
            for s in range(seqs):
                held[pl.ds(h * lines + s * hidden + step * E_BLOCK + e, src, stride=base), :] = grad[
                    s * src : (s + 1) * src, h * half : (h + 1) * half
                ]

    @pl.when(step == pl.num_programs(0) - 1)
    def _():
        core = lax.rem(info[0], 2)
        keep[...] = held[rows_at(core * lines, lines), :]
        send[...] = held[rows_at((1 - core) * lines, lines), :].astype(BF)


def pack_backward_kernel(dims, info, keep, came, w_keep, w_came, left, far_1, far_2, far_3, out):
    src, seqs, hidden, row_dev, places, half = dims
    pairs = src // 2
    lines = 2 * seqs * hidden
    w_lines = hidden * hidden // src
    total = left[...] + far_1[...].astype(F32) + far_2[...].astype(F32) + far_3[...].astype(F32)
    total = jnp.where(info[1] == 0, total, 0.0).astype(BF)
    for q in range(pairs):
        span = pl.ds(q * lines, lines)
        out[q, pl.ds(0, lines), :] = (keep[span, :] + came[span, :].astype(F32)).astype(BF)
        span = pl.ds(q * w_lines, w_lines)
        out[q, pl.ds(lines, w_lines), :] = (w_keep[span, :] + w_came[span, :].astype(F32)).astype(BF)
        out[q, pl.ds(lines + w_lines, 2 * row_dev), :] = total[q * 2 * row_dev : (q + 1) * 2 * row_dev]


def unpack_backward_kernel(dims, info, arrived, send, keep, chunk, held):
    src, seqs, hidden, row_dev, places, half = dims
    pairs = src // 2
    base = seqs * hidden
    w_lines = hidden * hidden // src
    core = lax.rem(info[0], 2)
    total = arrived[0, : 2 * base + w_lines, :].astype(F32)
    for q in range(1, pairs):
        total = total + arrived[q, : 2 * base + w_lines, :].astype(F32)
    held[...] = total[: 2 * base]
    chunk[...] = total[2 * base :].astype(BF)
    for ref, to in ((send, 1 - core), (keep, core)):
        ref[pl.ds(0, base), :] = held[rows_at(to * base, base), :].astype(BF)
        for q in range(pairs):
            ref[pl.ds(base + q * row_dev, row_dev), :] = arrived[
                q, rows_at(2 * base + w_lines + to * row_dev, row_dev), :
            ]


def projector_kernel(dims, info, keep, came, normed, live, bias, grads, w_keep, w_send, small, right, left):
    src, seqs, hidden, row_dev, places, half = dims
    base = seqs * hidden
    core = lax.rem(info[0], 2)
    for ref, who in ((keep, core), (came, 1 - core)):
        right[rows_at(who * base, base), :] = ref[pl.ds(0, base), :].astype(F32)
        for q in range(src // 2):
            left[rows_at(q * 2 * row_dev + who * row_dev, row_dev), :] = ref[
                pl.ds(base + q * row_dev, row_dev), :
            ].astype(F32)
    left_t = left[...].T
    weight = jnp.zeros((2 * hidden, places), F32)
    sums = jnp.zeros((8, 2 * hidden), F32)
    for s in range(seqs):
        span = slice(s * hidden, (s + 1) * hidden)
        right_s = jnp.concatenate([right[span, :], right[base + s * hidden : base + (s + 1) * hidden, :]], axis=1)
        grad = (jnp.concatenate([left_t[span], right_s], axis=0) * live[s : s + 1, :]).astype(BF)
        grads[pl.ds(s * 2 * hidden, 2 * hidden), :] = grad
        weight = weight + dot(grad, normed[s], 1, 0)
        sums = sums + dot(jnp.ones((8, places), BF), grad, 1, 1)
    low, high = weight[:, :half], weight[:, half:]
    w_keep[...] = jnp.where(core == 0, low, high)
    w_send[...] = jnp.where(core == 0, high, low).astype(BF)
    row = jnp.concatenate([sums[:1], jnp.zeros((1, half - 2 * hidden), F32)], axis=1)
    small[...] = bias_block(bias[...], row, half)


def bias_block(first, second, half):
    first_high, second_high = first.astype(BF).astype(F32), second.astype(BF).astype(F32)
    rows = [first_high, first - first_high, second_high, second - second_high]
    return jnp.concatenate(rows + [jnp.zeros((GROUP - 4, half), F32)], axis=0).astype(BF)


def align_kernel(dims, msa, grads, weights, out):
    src, seqs, hidden, row_dev, places, half = dims
    for s in range(seqs):
        grad = grads[pl.ds(s * 2 * hidden, 2 * hidden), :].astype(F32).T.astype(BF)
        grad = dot(grad, weights[...], 1, 0)
        value, scale = normal(msa[s].astype(F32))
        shift = jnp.mean(grad, axis=-1, keepdims=True)
        slope = jnp.mean(grad * value, axis=-1, keepdims=True)
        out[s] = (scale * (grad - shift - value * slope)).astype(BF)


def pack_column_kernel(dims, w_keep, w_came, chunk, small, out):
    weight = (w_keep[...] + w_came[...].astype(F32)).astype(BF)
    at = weight.shape[0]
    size = chunk.shape[0]
    for c in range(out.shape[0]):
        out[c, pl.ds(0, at), :] = weight
        out[c, pl.ds(at, size), :] = chunk[...]
        out[c, pl.ds(at + size, GROUP), :] = small[...]


def left_sum_kernel(dims, left, near_1, near_2, near_3, total, sent):
    value = left[...] + near_1[...].astype(F32) + near_2[...].astype(F32) + near_3[...].astype(F32)
    total[...] = value
    sent[...] = value.astype(BF)


def pack_row_kernel(dims, arrived, out):
    total = arrived[0].astype(F32)
    for c in range(1, arrived.shape[0]):
        total = total + arrived[c].astype(F32)
    at = total.shape[0] - GROUP
    last = total[at:]
    small = bias_block(last[0:1] + last[1:2], last[2:3] + last[3:4], last.shape[1])
    total = total[:at].astype(BF)
    for q in range(out.shape[0]):
        out[q, pl.ds(0, at), :] = total
        out[q, pl.ds(at, GROUP), :] = small


def finish_kernel(dims, info, mine, other, projector, projector_bias, weight, bias, held):
    src, seqs, hidden, row_dev, places, half = dims
    core = lax.rem(info[0], 2)
    w_lines = hidden * hidden // src
    at = 2 * hidden + w_lines
    sums = []
    small = jnp.zeros((GROUP, half), F32)
    for ref, who in ((mine, core), (other, 1 - core)):
        total = jnp.zeros((2 * hidden, half), F32)
        for q in range(src // 2):
            total = total + ref[q, : 2 * hidden, :].astype(F32)
            small = small + ref[q, at : at + GROUP, :].astype(F32)
            held[rows_at(who * (hidden * hidden // 2) + q * w_lines, w_lines), :] = ref[
                q, 2 * hidden : at, :
            ].astype(F32)
        sums.append(total)
    first = jnp.where(core == 0, sums[0], sums[1])
    second = jnp.where(core == 0, sums[1], sums[0])
    projector[...] = jnp.concatenate([first, second], axis=1)
    bias[...] = small[0:1] + small[1:2]
    projector_bias[...] = (small[2:3] + small[3:4])[:, : 2 * hidden]
    for c in range(hidden):
        weight[pl.ds(c * hidden, hidden), :] = held[pl.ds(c, hidden, stride=hidden), :]


def shape_of(dtype, *shape):
    return jax.ShapeDtypeStruct(shape, dtype)


def whole(*shape):
    return pl.BlockSpec(shape, lambda t: (0,) * len(shape))


SCALARS = pl.BlockSpec(memory_space=pltpu.SMEM)


def call(kernel, dims, name, args, outs, scratch=(), steps=1, in_specs=None, out_specs=None, macs=0, room=24):
    in_specs, out_specs = in_specs or {}, out_specs or {}
    specs = [
        SCALARS if a.dtype == jnp.int32 and a.ndim == 1 else in_specs.get(n, whole(*a.shape))
        for n, a in enumerate(args)
    ]
    size = sum(a.size * a.dtype.itemsize for a in args)
    size += sum(o.size * jnp.dtype(o.dtype).itemsize for o in outs)
    result = pl.pallas_call(
        functools.partial(kernel, dims),
        grid=(steps,),
        in_specs=specs,
        out_specs=[out_specs.get(n, whole(*o.shape)) for n, o in enumerate(outs)],
        out_shape=list(outs),
        scratch_shapes=[pltpu.VMEM(s, t) for s, t in scratch],
        compiler_params=pltpu.CompilerParams(
            dimension_semantics=("arbitrary",), vmem_limit_bytes=room * 2**20
        ),
        cost_estimate=pl.CostEstimate(flops=40 * macs, bytes_accessed=size, transcendentals=0),
        name=name,
    )(*args)
    return result


def near_parts(block, cols):
    return [
        lax.ppermute(block, "col", [(a, a + d) for a in range(0, cols, STEP)])
        for d in range(1, STEP)
    ]


def per_device(
    homolog_features,
    presence_indicator,
    polymer_label,
    lowering_matrix,
    lowering_offset,
    outgoing_matrix,
    outgoing_offset,
    update_adjoint,
):
    seqs, places, depth = homolog_features.shape
    hidden = lowering_matrix.shape[1] // 2
    channels = outgoing_matrix.shape[1]
    row_dev = update_adjoint.shape[0]
    rows, cols = lax.axis_size("row"), lax.axis_size("col")
    pairs, half = rows // 2, channels
    dims = (rows, seqs, hidden, row_dev, places, half)
    base = seqs * hidden
    total = rows * seqs
    lines = row_dev * hidden
    w_lines = hidden * hidden // rows
    info = jnp.stack([lax.axis_index("row"), lax.axis_index("col")]).astype(jnp.int32)
    swap = [(i, i ^ 1) for i in range(rows)]
    same_core = [list(range(c, rows, 2)) for c in range(2)]

    def partner(block):
        return lax.ppermute(block, "row", swap)

    def over_pairs(block):
        return lax.all_to_all(block, "row", 0, 0, axis_index_groups=same_core, tiled=True)

    size = base + GROUP + pairs * row_dev
    normed, live, send, keep = call(
        project_kernel,
        dims,
        "project",
        (info, homolog_features, presence_indicator, polymer_label[None], lowering_matrix.T, lowering_offset[None]),
        (
            shape_of(BF, seqs, places, depth),
            shape_of(F32, 8, places),
            shape_of(BF, size, half),
            shape_of(BF, size, half),
        ),
        [((2 * base, half), F32), ((places, base), F32)],
        macs=100_000_000,
    )
    came = partner(send)

    tree = jnp.concatenate([keep[base:], came[base:]], axis=0)
    far = [lax.ppermute(tree, "col", [(0, d)]) for d in range(STEP, cols, STEP)]
    tree = sum(far, tree)
    near = near_parts(tree, cols)
    packed = call(
        pack_right_kernel,
        dims,
        "pack_right",
        (info, keep, came),
        (shape_of(BF, pairs, 2 * (base + GROUP), half),),
    )[0]
    mine = over_pairs(packed)
    mine, *near = lax.optimization_barrier((mine, *near))
    packed = call(
        pack_left_kernel,
        dims,
        "pack_left",
        (info, tree, *near),
        (shape_of(BF, pairs, 2 * (GROUP + row_dev), half),),
    )[0]
    arrived = over_pairs(packed)
    other = partner(mine)
    right_cols, live_t, by_e, by_e_t = call(
        unpack_right_kernel,
        dims,
        "unpack_right",
        (info, mine, other, outgoing_matrix),
        (
            shape_of(BF, hidden, total, places),
            shape_of(BF, places, total),
            shape_of(BF, hidden * hidden, channels),
            shape_of(BF, channels, hidden * hidden),
        ),
        [
            ((2 * rows * base, half), F32),
            ((2 * rows * GROUP, half), F32),
            ((hidden * hidden, channels), F32),
        ],
        macs=300_000_000,
    )

    by_block = lambda *block: pl.BlockSpec((E_BLOCK, *block), lambda t: (t, 0, 0))
    outer_grad, scaled, divisor, left_grad, bias_grad, left_rows, left_t = call(
        first_kernel,
        dims,
        "scaled_outer_grad",
        (info, arrived, right_cols, live_t, update_adjoint, by_e),
        (
            shape_of(BF, hidden, lines, places),
            shape_of(BF, row_dev, places, channels),
            shape_of(BF, row_dev, places, channels),
            shape_of(F32, rows * row_dev, half),
            shape_of(F32, 1, channels),
            shape_of(BF, total, lines),
            shape_of(BF, lines, total),
        ),
        [((rows * GROUP, half), F32), ((total, lines), F32)],
        steps=hidden // E_BLOCK,
        out_specs={0: by_block(lines, places)},
        macs=800_000_000,
        room=32,
    )

    sent = left_grad.astype(BF)
    near = [
        lax.ppermute(sent, "col", [(a + d, a) for a in range(0, cols, STEP)])
        for d in range(1, STEP)
    ]
    right_keep, right_send = call(
        third_kernel,
        dims,
        "right_grad",
        (info, left_rows, outer_grad),
        (shape_of(F32, rows * base, half), shape_of(BF, rows * base, half)),
        [((2 * rows * base, half), F32)],
        steps=hidden // E_BLOCK,
        in_specs={2: by_block(lines, places)},
        macs=270_000_000,
        room=32,
    )
    *near, right_send = lax.optimization_barrier((*near, right_send))
    left_grad, sent = call(
        left_sum_kernel,
        dims,
        "left_sum",
        (left_grad, *near),
        (shape_of(F32, rows * row_dev, half), shape_of(BF, rows * row_dev, half)),
    )
    left_t, sent = lax.optimization_barrier((left_t, sent))
    far = [lax.ppermute(sent, "col", [(d, 0)]) for d in range(STEP, cols, STEP)]
    pair_increment, w_keep, w_send = call(
        second_kernel,
        dims,
        "outer_pair",
        (info, left_t, right_cols, scaled, divisor, by_e_t, outgoing_offset[None]),
        (
            shape_of(BF, row_dev, places, channels),
            shape_of(F32, hidden * hidden // 2, channels),
            shape_of(BF, hidden * hidden // 2, channels),
        ),
        [
            ((E_BLOCK, lines, places), BF),
            ((row_dev, channels, places), F32),
            ((hidden * hidden, channels), F32),
        ],
        steps=hidden // E_BLOCK,
        in_specs={
            2: by_block(total, places),
            5: pl.BlockSpec((channels, E_BLOCK * hidden), lambda t: (0, t)),
        },
        macs=1_300_000_000,
        room=32,
    )
    w_send, *far = lax.optimization_barrier((w_send, *far))
    w_came = partner(w_send)
    right_came = partner(right_send)
    packed = call(
        pack_backward_kernel,
        dims,
        "pack_backward",
        (info, right_keep, right_came, w_keep, w_came, left_grad, *far),
        (shape_of(BF, pairs, 2 * base + w_lines + 2 * row_dev, half),),
    )[0]
    arrived = over_pairs(packed)

    send, keep, chunk = call(
        unpack_backward_kernel,
        dims,
        "unpack_backward",
        (info, arrived),
        (
            shape_of(BF, base + pairs * row_dev, half),
            shape_of(BF, base + pairs * row_dev, half),
            shape_of(BF, w_lines, half),
        ),
        [((2 * base, half), F32)],
    )
    came = partner(send)
    grads, w_keep, w_send, small = call(
        projector_kernel,
        dims,
        "projector_grad",
        (info, keep, came, normed, live, bias_grad),
        (
            shape_of(BF, seqs * 2 * hidden, places),
            shape_of(F32, 2 * hidden, half),
            shape_of(BF, 2 * hidden, half),
            shape_of(BF, GROUP, half),
        ),
        [((2 * base, half), F32), ((places, base), F32)],
        macs=20_000_000,
    )
    w_came = partner(w_send)
    size = 2 * hidden + w_lines + GROUP
    packed = call(
        pack_column_kernel, dims, "pack_column", (w_keep, w_came, chunk, small), (shape_of(BF, cols, size, half),)
    )[0]
    arrived = lax.all_to_all(packed, "col", 0, 0, tiled=True)
    alignment_gradient = call(
        align_kernel,
        dims,
        "alignment",
        (homolog_features, grads, lowering_matrix.T),
        (shape_of(BF, seqs, places, depth),),
        macs=200_000_000,
    )[0]
    arrived, alignment_gradient = lax.optimization_barrier((arrived, alignment_gradient))
    packed = call(pack_row_kernel, dims, "pack_row", (arrived,), (shape_of(BF, pairs, size, half),))[0]
    mine = over_pairs(packed)
    other = partner(mine)
    projector, projector_bias, weight, bias = call(
        finish_kernel,
        dims,
        "finish",
        (info, mine, other),
        (
            shape_of(F32, 2 * hidden, depth),
            shape_of(F32, 1, 2 * hidden),
            shape_of(F32, hidden * hidden, channels),
            shape_of(F32, 1, channels),
        ),
        [((hidden * hidden, channels), F32)],
    )
    return (
        pair_increment,
        alignment_gradient,
        projector.T,
        projector_bias[0],
        weight,
        bias[0],
    )


def solution(mesh):
    in_specs = (
        P("row", "col", None),
        P("row", "col"),
        P("col"),
        P(),
        P(),
        P(),
        P(),
        P("row", "col", None),
    )
    out_specs = (P("row", "col", None), P("row", "col", None), P(), P(), P(), P())
    return jax.shard_map(
        per_device, mesh=mesh, in_specs=in_specs, out_specs=out_specs, check_vma=False
    )
```

```python
import functools

import jax
import jax.numpy as jnp
from jax import lax
from jax.experimental import pallas as pl
from jax.experimental.pallas import tpu as pltpu
from jax.sharding import PartitionSpec as P

PAIRED = 16
CHAINS = 4
BF = jnp.bfloat16
F32 = jnp.float32
STEP = 4
GROUP = 16
E_BLOCK = 8
E_WIDE = 16
FUSE = 4


def dot(a, b, lhs, rhs):
    return lax.dot_general(a, b, (((lhs,), (rhs,)), ((), ())), preferred_element_type=F32)


def rows_at(start, size):
    return pl.ds(pl.multiple_of(start, GROUP), size)


def normal(values):
    center = values - jnp.mean(values, axis=-1, keepdims=True)
    spread = jnp.mean(center * center, axis=-1, keepdims=True)
    scale = lax.rsqrt(spread + 1e-05)
    return center * scale, scale


def project_kernel(dims, info, msa, present, label, weights, offset, normed, live_ref, send, keep, right, left):
    src, seqs, hidden, row_dev, places, half = dims
    pairs = src // 2
    me, core = info[0], lax.rem(info[0], 2)
    first = info[1] == 0
    seq = me * seqs + lax.broadcasted_iota(jnp.int32, (seqs, places), 0)
    chain = lax.rem(seq + (CHAINS - PAIRED % CHAINS), CHAINS)
    permitted = (seq < PAIRED) | (chain == jnp.broadcast_to(label[...], (seqs, places)))
    live = jnp.where(permitted & (present[...] == 1), 1.0, 0.0).astype(F32)
    live = jnp.concatenate([live, jnp.zeros((8 - seqs, places), F32)], axis=0)
    live_ref[...] = live
    weight = weights[...].astype(F32)
    right_w = weight[hidden:].astype(BF)
    left_w = jnp.concatenate([weight[:hidden]] * seqs, axis=0).T.astype(BF)
    lane = lax.broadcasted_iota(jnp.int32, left_w.shape, 1) // hidden
    column = jnp.broadcast_to(offset[...], (8, 2 * hidden)).T[hidden:, :1]
    total = jnp.zeros((places, seqs * hidden), F32)
    for s in range(seqs):
        value = normal(msa[s].astype(F32))[0].astype(BF)
        normed[s] = value
        out = (dot(right_w, value, 1, 1) + column) * live[s : s + 1]
        for h in range(2):
            right[pl.ds(h * seqs * hidden + s * hidden, hidden), :] = out[:, h * half : (h + 1) * half]
        total = total + dot(value, jnp.where(lane == s, left_w, jnp.zeros_like(left_w)), 1, 0)
    total = total + jnp.concatenate([offset[:, :hidden]] * seqs, axis=1)
    spot = lax.broadcasted_iota(jnp.int32, (8, seqs * hidden), 0)
    expand = jnp.where(spot == lax.broadcasted_iota(jnp.int32, (8, seqs * hidden), 1) // hidden, 1.0, 0.0)
    total = total * dot(live.T.astype(BF), expand.astype(BF), 1, 0)
    left[...] = jnp.where(first, total, 0.0)
    place = lax.broadcasted_iota(jnp.int32, (places, half), 0)
    slot = lax.broadcasted_iota(jnp.int32, (places, half), 1)
    base = seqs * hidden
    for ref, to in ((send, 1 - core), (keep, core)):
        pick = jnp.where(place == slot // row_dev * 2 * row_dev + to * row_dev + lax.rem(slot, row_dev), 1.0, 0.0)
        band = dot(live.astype(BF), pick.astype(BF), 1, 0)[:seqs]
        band = jnp.where(first, band, 0.0)
        own = jnp.where(to == 0, live[:seqs, :half], live[:seqs, half:])
        flags = jnp.concatenate([own, band, jnp.zeros((GROUP - 2 * seqs, half), F32)], axis=0)
        ref[pl.ds(0, base), :] = right[rows_at(to * base, base), :].astype(BF)
        ref[pl.ds(base, GROUP), :] = flags.astype(BF)
        for q in range(pairs):
            ref[pl.ds(base + GROUP + q * row_dev, row_dev), :] = left[
                rows_at(q * 2 * row_dev + to * row_dev, row_dev), :
            ].astype(BF)


def pack_forward_kernel(dims, info, keep, came, out):
    src, seqs, hidden, row_dev, places, half = dims
    core = lax.rem(info[0], 2)
    base = seqs * hidden
    for ref, who in ((keep, core), (came, 1 - core)):
        value = ref[pl.ds(0, base), :]
        flags = ref[pl.ds(base, GROUP), :]
        for q in range(src // 2):
            out[q, rows_at(who * base, base), :] = value
            out[q, rows_at(2 * base + who * GROUP, GROUP), :] = flags
            out[q, rows_at(2 * base + 2 * GROUP + who * row_dev, row_dev), :] = ref[
                pl.ds(base + GROUP + q * row_dev, row_dev), :
            ]


def left_rows_kernel(dims, mine, out, tiles):
    src, seqs, hidden, row_dev, places, half = dims
    first = 2 * seqs * hidden
    for q in range(src // 2):
        tiles[pl.ds(q * 2 * GROUP, 2 * GROUP), :] = mine[q, first : first + 2 * GROUP, :].astype(F32)
    rows = [tiles[pl.ds(seqs + s, src, stride=GROUP), :] for s in range(seqs)]
    blocks = [jnp.concatenate(rows, axis=0)]
    for q in range(src // 2):
        tiles[pl.ds(q * 2 * row_dev, 2 * row_dev), :] = mine[q, first + 2 * GROUP :, :].astype(F32)
    for i in range(row_dev):
        tile = tiles[pl.ds(i, src, stride=row_dev), :]
        blocks.append(jnp.concatenate([tile[:, s * hidden : (s + 1) * hidden] for s in range(seqs)], axis=0))
    out[...] = jnp.concatenate(blocks, axis=1).astype(BF)


def unpack_right_kernel(dims, info, mine, other, weights, r_ref, live_t_ref, by_e, by_e_t, r_all, flags, w_all):
    src, seqs, hidden, row_dev, places, half = dims
    base = seqs * hidden
    lines = src * base
    core = lax.rem(info[0], 2)
    for ref, h in ((mine, core), (other, 1 - core)):
        for q in range(src // 2):
            r_all[rows_at(h * lines + q * 2 * base, 2 * base), :] = ref[q, : 2 * base, :].astype(F32)
            flags[rows_at((h * src + 2 * q) * GROUP, 2 * GROUP), :] = ref[
                q, 2 * base : 2 * base + 2 * GROUP, :
            ].astype(F32)
    w_all[...] = weights[...].astype(F32)
    for e in range(hidden):
        for h in range(2):
            rows = [r_all[pl.ds(h * lines + s * hidden + e, src, stride=base), :] for s in range(seqs)]
            r_ref[e, :, pl.ds(h * half, half)] = jnp.concatenate(rows, axis=0).astype(BF)
    for e in range(0, hidden, 4):
        rows = [w_all[pl.ds(e + n, hidden, stride=hidden), :] for n in range(4)]
        part = jnp.concatenate(rows, axis=0)
        by_e[pl.ds(e * hidden, 4 * hidden), :] = part.astype(BF)
        by_e_t[:, pl.ds(e * hidden, 4 * hidden)] = part.T.astype(BF)
    for h in range(2):
        rows = [flags[pl.ds(h * src * GROUP + s, src, stride=GROUP), :] for s in range(seqs)]
        live_t_ref[pl.ds(h * half, half), :] = jnp.concatenate(rows, axis=0).T.astype(BF)


def first_kernel(dims, info, tree, near_1, near_2, near_3, r_ref, live_t, adjoint, weights, g_ref, s_ref, d_ref, left_ref, bias_ref, left_out, left_t, total):
    src, seqs, hidden, row_dev, places, half = dims
    step = pl.program_id(0)

    @pl.when(step == 0)
    def _():
        pair = info[0] // 2
        spread = tree[...].astype(F32) + near_1[...].astype(F32) + near_2[...].astype(F32) + near_3[...].astype(F32)
        band = spread[:, :half].astype(BF)
        left = spread[:, half:]
        left_out[...] = left.astype(BF)
        left_t[...] = left.T.astype(BF)
        spot = lax.broadcasted_iota(jnp.int32, (half, half), 0) - pair * row_dev
        bias = jnp.zeros((1, half), F32)
        for i in range(row_dev):
            column = dot(band, jnp.where(spot == i, 1.0, 0.0).astype(BF), 1, 0).astype(BF)
            divisor = jnp.maximum(dot(live_t[...], column, 1, 0), 1.0)
            scaled = (adjoint[i].astype(F32) / divisor).astype(BF)
            d_ref[i] = divisor.astype(BF)
            s_ref[i] = scaled
            bias = bias + jnp.sum(scaled.astype(F32), axis=0, keepdims=True)
        bias_ref[...] = bias
        total[...] = jnp.zeros_like(total)

    part = weights[pl.ds(step * E_WIDE * hidden, E_WIDE * hidden), :]
    for i in range(row_dev):
        g = dot(part, s_ref[i], 1, 1).astype(BF)
        g_ref[:, pl.ds(i * hidden, hidden), :] = g.reshape(E_WIDE, hidden, places)
    acc = total[...]
    for e in range(0, E_WIDE, FUSE):
        right = jnp.concatenate([r_ref[step * E_WIDE + e + n] for n in range(FUSE)], axis=1)
        grad = jnp.concatenate([g_ref[e + n] for n in range(FUSE)], axis=1)
        acc = acc + dot(right, grad, 1, 1)
    total[...] = acc

    @pl.when(step == pl.num_programs(0) - 1)
    def _():
        for i in range(row_dev):
            block = acc[:, i * hidden : (i + 1) * hidden]
            left_ref[pl.ds(i, src, stride=row_dev), :] = jnp.concatenate(
                [block[s * src : (s + 1) * src] for s in range(seqs)], axis=1
            )


def second_kernel(dims, info, left_t, r_ref, s_ref, d_ref, weights_t, offset, pair_ref, keep, send, outer, before, held):
    src, seqs, hidden, row_dev, places, half = dims
    step = pl.program_id(0)
    block_lines = E_BLOCK * hidden

    @pl.when(step == 0)
    def _():
        before[...] = jnp.zeros_like(before)

    for e in range(E_BLOCK):
        outer[e] = dot(left_t[...], r_ref[e], 1, 0).astype(BF)
    acc = jnp.zeros((block_lines, half), F32)
    for i in range(row_dev):
        block = outer[:, pl.ds(i * hidden, hidden), :].reshape(block_lines, places)
        before[i] = before[i] + dot(weights_t[...], block, 1, 0)
    for i in range(0, row_dev, FUSE):
        blocks = [
            outer[:, pl.ds((i + n) * hidden, hidden), :].reshape(block_lines, places) for n in range(FUSE)
        ]
        scaled = s_ref[pl.ds(i, FUSE)].reshape(FUSE * places, half)
        acc = acc + dot(jnp.concatenate(blocks, axis=1), scaled, 1, 0)
    held[rows_at(step * block_lines, block_lines), :] = acc

    @pl.when(step == pl.num_programs(0) - 1)
    def _():
        core = lax.rem(info[0], 2)
        lines = hidden * hidden // 2
        keep[...] = held[rows_at(core * lines, lines), :]
        send[...] = held[rows_at((1 - core) * lines, lines), :].astype(BF)
        for i in range(row_dev):
            pair_ref[i] = ((before[i].T + offset[...]) / d_ref[i].astype(F32)).astype(BF)


def third_kernel(dims, info, left, g_ref, keep, send, held):
    src, seqs, hidden, row_dev, places, half = dims
    step = pl.program_id(0)
    base = seqs * hidden
    lines = src * base
    for e in range(E_WIDE):
        grad = dot(left[...], g_ref[e], 1, 0)
        for h in range(2):
            for s in range(seqs):
                held[pl.ds(h * lines + s * hidden + step * E_WIDE + e, src, stride=base), :] = grad[
                    s * src : (s + 1) * src, h * half : (h + 1) * half
                ]

    @pl.when(step == pl.num_programs(0) - 1)
    def _():
        core = lax.rem(info[0], 2)
        keep[...] = held[rows_at(core * lines, lines), :]
        send[...] = held[rows_at((1 - core) * lines, lines), :].astype(BF)


def pack_backward_kernel(dims, info, keep, came, w_keep, w_came, left, far_1, far_2, far_3, out):
    src, seqs, hidden, row_dev, places, half = dims
    pairs = src // 2
    lines = 2 * seqs * hidden
    w_lines = hidden * hidden // src
    total = left[...] + far_1[...].astype(F32) + far_2[...].astype(F32) + far_3[...].astype(F32)
    total = jnp.where(info[1] == 0, total, 0.0).astype(BF)
    for q in range(pairs):
        span = pl.ds(q * lines, lines)
        out[q, pl.ds(0, lines), :] = (keep[span, :] + came[span, :].astype(F32)).astype(BF)
        span = pl.ds(q * w_lines, w_lines)
        out[q, pl.ds(lines, w_lines), :] = (w_keep[span, :] + w_came[span, :].astype(F32)).astype(BF)
        out[q, pl.ds(lines + w_lines, 2 * row_dev), :] = total[q * 2 * row_dev : (q + 1) * 2 * row_dev]


def unpack_backward_kernel(dims, info, arrived, send, keep, chunk, held):
    src, seqs, hidden, row_dev, places, half = dims
    pairs = src // 2
    base = seqs * hidden
    w_lines = hidden * hidden // src
    core = lax.rem(info[0], 2)
    total = arrived[0, : 2 * base + w_lines, :].astype(F32)
    for q in range(1, pairs):
        total = total + arrived[q, : 2 * base + w_lines, :].astype(F32)
    held[...] = total[: 2 * base]
    chunk[...] = total[2 * base :].astype(BF)
    for ref, to in ((send, 1 - core), (keep, core)):
        ref[pl.ds(0, base), :] = held[rows_at(to * base, base), :].astype(BF)
        for q in range(pairs):
            ref[pl.ds(base + q * row_dev, row_dev), :] = arrived[
                q, rows_at(2 * base + w_lines + to * row_dev, row_dev), :
            ]


def projector_kernel(dims, info, keep, came, normed, live, bias, grads, w_keep, w_send, small, right, left):
    src, seqs, hidden, row_dev, places, half = dims
    base = seqs * hidden
    core = lax.rem(info[0], 2)
    for ref, who in ((keep, core), (came, 1 - core)):
        right[rows_at(who * base, base), :] = ref[pl.ds(0, base), :].astype(F32)
        for q in range(src // 2):
            left[rows_at(q * 2 * row_dev + who * row_dev, row_dev), :] = ref[
                pl.ds(base + q * row_dev, row_dev), :
            ].astype(F32)
    left_t = left[...].T
    weight = jnp.zeros((2 * hidden, places), F32)
    sums = jnp.zeros((8, 2 * hidden), F32)
    for s in range(seqs):
        span = slice(s * hidden, (s + 1) * hidden)
        right_s = jnp.concatenate([right[span, :], right[base + s * hidden : base + (s + 1) * hidden, :]], axis=1)
        grad = (jnp.concatenate([left_t[span], right_s], axis=0) * live[s : s + 1, :]).astype(BF)
        grads[pl.ds(s * 2 * hidden, 2 * hidden), :] = grad
        weight = weight + dot(grad, normed[s], 1, 0)
        sums = sums + dot(jnp.ones((8, places), BF), grad, 1, 1)
    low, high = weight[:, :half], weight[:, half:]
    w_keep[...] = jnp.where(core == 0, low, high)
    w_send[...] = jnp.where(core == 0, high, low).astype(BF)
    row = jnp.concatenate([sums[:1], jnp.zeros((1, half - 2 * hidden), F32)], axis=1)
    small[...] = bias_block(bias[...], row, half)


def bias_block(first, second, half):
    first_high, second_high = first.astype(BF).astype(F32), second.astype(BF).astype(F32)
    rows = [first_high, first - first_high, second_high, second - second_high]
    return jnp.concatenate(rows + [jnp.zeros((GROUP - 4, half), F32)], axis=0).astype(BF)


def align_kernel(dims, msa, grads, weights, out):
    src, seqs, hidden, row_dev, places, half = dims
    for s in range(seqs):
        grad = grads[pl.ds(s * 2 * hidden, 2 * hidden), :].astype(F32).T.astype(BF)
        grad = dot(grad, weights[...], 1, 0)
        value, scale = normal(msa[s].astype(F32))
        shift = jnp.mean(grad, axis=-1, keepdims=True)
        slope = jnp.mean(grad * value, axis=-1, keepdims=True)
        out[s] = (scale * (grad - shift - value * slope)).astype(BF)


def pack_column_kernel(dims, w_keep, w_came, chunk, small, out):
    weight = (w_keep[...] + w_came[...].astype(F32)).astype(BF)
    at = weight.shape[0]
    size = chunk.shape[0]
    out[pl.ds(0, at), :] = weight
    out[pl.ds(at, size), :] = chunk[...]
    out[pl.ds(at + size, GROUP), :] = small[...]


def sum_of_four(part_0, part_1, part_2, part_3):
    parts = [p[...].astype(F32) for p in (part_0, part_1, part_2, part_3)]
    total = (parts[0] + parts[1]) + (parts[2] + parts[3])
    at = total.shape[0] - GROUP
    last = total[at:]
    small = bias_block(last[0:1] + last[1:2], last[2:3] + last[3:4], last.shape[1])
    return total[:at].astype(BF), small


def column_sum_kernel(dims, part_0, part_1, part_2, part_3, out):
    total, small = sum_of_four(part_0, part_1, part_2, part_3)
    out[pl.ds(0, total.shape[0]), :] = total
    out[pl.ds(total.shape[0], GROUP), :] = small


def left_sum_kernel(dims, left, near_1, near_2, near_3, total, sent):
    value = left[...] + near_1[...].astype(F32) + near_2[...].astype(F32) + near_3[...].astype(F32)
    total[...] = value
    sent[...] = value.astype(BF)


def pack_row_kernel(dims, part_0, part_1, part_2, part_3, out):
    total, small = sum_of_four(part_0, part_1, part_2, part_3)
    for q in range(out.shape[0]):
        out[q, pl.ds(0, total.shape[0]), :] = total
        out[q, pl.ds(total.shape[0], GROUP), :] = small


def finish_kernel(dims, info, mine, other, projector, projector_bias, weight, bias, held):
    src, seqs, hidden, row_dev, places, half = dims
    core = lax.rem(info[0], 2)
    w_lines = hidden * hidden // src
    at = 2 * hidden + w_lines
    sums = []
    small = jnp.zeros((GROUP, half), F32)
    for ref, who in ((mine, core), (other, 1 - core)):
        total = jnp.zeros((2 * hidden, half), F32)
        for q in range(src // 2):
            total = total + ref[q, : 2 * hidden, :].astype(F32)
            small = small + ref[q, at : at + GROUP, :].astype(F32)
            held[rows_at(who * (hidden * hidden // 2) + q * w_lines, w_lines), :] = ref[
                q, 2 * hidden : at, :
            ].astype(F32)
        sums.append(total)
    first = jnp.where(core == 0, sums[0], sums[1])
    second = jnp.where(core == 0, sums[1], sums[0])
    projector[...] = jnp.concatenate([first, second], axis=1)
    bias[...] = small[0:1] + small[1:2]
    projector_bias[...] = (small[2:3] + small[3:4])[:, : 2 * hidden]
    for c in range(hidden):
        weight[pl.ds(c * hidden, hidden), :] = held[pl.ds(c, hidden, stride=hidden), :]


def shape_of(dtype, *shape):
    return jax.ShapeDtypeStruct(shape, dtype)


def whole(*shape):
    return pl.BlockSpec(shape, lambda t: (0,) * len(shape))


SCALARS = pl.BlockSpec(memory_space=pltpu.SMEM)


def call(kernel, dims, name, args, outs, scratch=(), steps=1, in_specs=None, out_specs=None, macs=0, room=16):
    in_specs, out_specs = in_specs or {}, out_specs or {}
    specs = [
        SCALARS if a.dtype == jnp.int32 and a.ndim == 1 else in_specs.get(n, whole(*a.shape))
        for n, a in enumerate(args)
    ]
    size = sum(a.size * a.dtype.itemsize for a in args)
    size += sum(o.size * jnp.dtype(o.dtype).itemsize for o in outs)
    result = pl.pallas_call(
        functools.partial(kernel, dims),
        grid=(steps,),
        in_specs=specs,
        out_specs=[out_specs.get(n, whole(*o.shape)) for n, o in enumerate(outs)],
        out_shape=list(outs),
        scratch_shapes=[pltpu.VMEM(s, t) for s, t in scratch],
        compiler_params=pltpu.CompilerParams(
            dimension_semantics=("arbitrary",), vmem_limit_bytes=room * 2**20
        ),
        cost_estimate=pl.CostEstimate(flops=40 * macs, bytes_accessed=size, transcendentals=0),
        name=name,
    )(*args)
    return result


def near_parts(block, cols):
    return [
        lax.ppermute(block, "col", [(a, a + d) for a in range(0, cols, STEP)])
        for d in range(1, STEP)
    ]


def swap_parts(block, cols, unit):
    swaps = [lax.ppermute(block, "col", [(i, i ^ d * unit) for i in range(cols)]) for d in range(1, STEP)]
    return [block, *swaps]


def per_device(
    homolog_features,
    presence_indicator,
    polymer_label,
    lowering_matrix,
    lowering_offset,
    outgoing_matrix,
    outgoing_offset,
    update_adjoint,
):
    seqs, places, depth = homolog_features.shape
    hidden = lowering_matrix.shape[1] // 2
    channels = outgoing_matrix.shape[1]
    row_dev = update_adjoint.shape[0]
    rows, cols = lax.axis_size("row"), lax.axis_size("col")
    pairs, half = rows // 2, channels
    dims = (rows, seqs, hidden, row_dev, places, half)
    base = seqs * hidden
    total = rows * seqs
    lines = row_dev * hidden
    w_lines = hidden * hidden // rows
    info = jnp.stack([lax.axis_index("row"), lax.axis_index("col")]).astype(jnp.int32)
    swap = [(i, i ^ 1) for i in range(rows)]
    same_core = [list(range(c, rows, 2)) for c in range(2)]

    def partner(block):
        return lax.ppermute(block, "row", swap)

    def over_pairs(block):
        return lax.all_to_all(block, "row", 0, 0, axis_index_groups=same_core, tiled=True)

    size = base + GROUP + pairs * row_dev
    normed, live, send, keep = call(
        project_kernel,
        dims,
        "project",
        (info, homolog_features, presence_indicator, polymer_label[None], lowering_matrix.T, lowering_offset[None]),
        (
            shape_of(BF, seqs, places, depth),
            shape_of(F32, 8, places),
            shape_of(BF, size, half),
            shape_of(BF, size, half),
        ),
        [((2 * base, half), F32), ((places, base), F32)],
        macs=100_000_000,
        room=62,
    )
    came = partner(send)

    packed = call(
        pack_forward_kernel,
        dims,
        "pack_forward",
        (info, keep, came),
        (shape_of(BF, pairs, 2 * (base + GROUP + row_dev), half),),
    )[0]
    mine = over_pairs(packed)
    tree = call(
        left_rows_kernel,
        dims,
        "left_rows",
        (mine,),
        (shape_of(BF, total, half + lines),),
        [((rows * GROUP, half), F32)],
    )[0]
    far = [lax.ppermute(tree, "col", [(0, d)]) for d in range(STEP, cols, STEP)]
    tree = sum(far, tree)
    near = near_parts(tree, cols)
    mine, tree = lax.optimization_barrier((mine, tree))
    other = partner(mine)
    right_cols, live_t, by_e, by_e_t = call(
        unpack_right_kernel,
        dims,
        "unpack_right",
        (info, mine, other, outgoing_matrix),
        (
            shape_of(BF, hidden, total, places),
            shape_of(BF, places, total),
            shape_of(BF, hidden * hidden, channels),
            shape_of(BF, channels, hidden * hidden),
        ),
        [
            ((2 * rows * base, half), F32),
            ((2 * rows * GROUP, half), F32),
            ((hidden * hidden, channels), F32),
        ],
        macs=300_000_000,
    )

    by_block = lambda size, *block: pl.BlockSpec((size, *block), lambda t: (t, 0, 0))
    outer_grad, scaled, divisor, left_grad, bias_grad, left_rows, left_t = call(
        first_kernel,
        dims,
        "scaled_outer_grad",
        (info, tree, *near, right_cols, live_t, update_adjoint, by_e),
        (
            shape_of(BF, hidden, lines, places),
            shape_of(BF, row_dev, places, channels),
            shape_of(BF, row_dev, places, channels),
            shape_of(F32, rows * row_dev, half),
            shape_of(F32, 1, channels),
            shape_of(BF, total, lines),
            shape_of(BF, lines, total),
        ),
        [((total, lines), F32)],
        steps=hidden // E_WIDE,
        out_specs={0: by_block(E_WIDE, lines, places)},
        macs=800_000_000,
        room=24,
    )

    sent = left_grad.astype(BF)
    near = [
        lax.ppermute(sent, "col", [(a + d, a) for a in range(0, cols, STEP)])
        for d in range(1, STEP)
    ]
    right_keep, right_send = call(
        third_kernel,
        dims,
        "right_grad",
        (info, left_rows, outer_grad),
        (shape_of(F32, rows * base, half), shape_of(BF, rows * base, half)),
        [((2 * rows * base, half), F32)],
        steps=hidden // E_WIDE,
        in_specs={2: by_block(E_WIDE, lines, places)},
        macs=270_000_000,
        room=24,
    )
    *near, right_send = lax.optimization_barrier((*near, right_send))
    left_grad, sent = call(
        left_sum_kernel,
        dims,
        "left_sum",
        (left_grad, *near),
        (shape_of(F32, rows * row_dev, half), shape_of(BF, rows * row_dev, half)),
    )
    left_t, sent = lax.optimization_barrier((left_t, sent))
    far = [lax.ppermute(sent, "col", [(d, 0)]) for d in range(STEP, cols, STEP)]
    pair_increment, w_keep, w_send = call(
        second_kernel,
        dims,
        "outer_pair",
        (info, left_t, right_cols, scaled, divisor, by_e_t, outgoing_offset[None]),
        (
            shape_of(BF, row_dev, places, channels),
            shape_of(F32, hidden * hidden // 2, channels),
            shape_of(BF, hidden * hidden // 2, channels),
        ),
        [
            ((E_BLOCK, lines, places), BF),
            ((row_dev, channels, places), F32),
            ((hidden * hidden, channels), F32),
        ],
        steps=hidden // E_BLOCK,
        in_specs={
            2: by_block(E_BLOCK, total, places),
            5: pl.BlockSpec((channels, E_BLOCK * hidden), lambda t: (0, t)),
        },
        macs=1_300_000_000,
        room=20,
    )
    w_send, *far = lax.optimization_barrier((w_send, *far))
    w_came = partner(w_send)
    right_came = partner(right_send)
    packed = call(
        pack_backward_kernel,
        dims,
        "pack_backward",
        (info, right_keep, right_came, w_keep, w_came, left_grad, *far),
        (shape_of(BF, pairs, 2 * base + w_lines + 2 * row_dev, half),),
    )[0]
    arrived = over_pairs(packed)

    send, keep, chunk = call(
        unpack_backward_kernel,
        dims,
        "unpack_backward",
        (info, arrived),
        (
            shape_of(BF, base + pairs * row_dev, half),
            shape_of(BF, base + pairs * row_dev, half),
            shape_of(BF, w_lines, half),
        ),
        [((2 * base, half), F32)],
    )
    came = partner(send)
    grads, w_keep, w_send, small = call(
        projector_kernel,
        dims,
        "projector_grad",
        (info, keep, came, normed, live, bias_grad),
        (
            shape_of(BF, seqs * 2 * hidden, places),
            shape_of(F32, 2 * hidden, half),
            shape_of(BF, 2 * hidden, half),
            shape_of(BF, GROUP, half),
        ),
        [((2 * base, half), F32), ((places, base), F32)],
        macs=20_000_000,
    )
    w_came = partner(w_send)
    size = 2 * hidden + w_lines + GROUP
    own = call(
        pack_column_kernel, dims, "pack_column", (w_keep, w_came, chunk, small), (shape_of(BF, size, half),)
    )[0]
    parts = swap_parts(own, cols, STEP)
    alignment_gradient = call(
        align_kernel,
        dims,
        "alignment",
        (homolog_features, grads, lowering_matrix.T),
        (shape_of(BF, seqs, places, depth),),
        macs=200_000_000,
    )[0]
    *parts, alignment_gradient = lax.optimization_barrier((*parts, alignment_gradient))
    own = call(column_sum_kernel, dims, "column_sum", parts, (shape_of(BF, size, half),))[0]
    parts = swap_parts(own, cols, 1)
    packed = call(pack_row_kernel, dims, "pack_row", parts, (shape_of(BF, pairs, size, half),))[0]
    mine = over_pairs(packed)
    other = partner(mine)
    projector, projector_bias, weight, bias = call(
        finish_kernel,
        dims,
        "finish",
        (info, mine, other),
        (
            shape_of(F32, 2 * hidden, depth),
            shape_of(F32, 1, 2 * hidden),
            shape_of(F32, hidden * hidden, channels),
            shape_of(F32, 1, channels),
        ),
        [((hidden * hidden, channels), F32)],
    )
    return (
        pair_increment,
        alignment_gradient,
        projector.T,
        projector_bias[0],
        weight,
        bias[0],
    )


def solution(mesh):
    in_specs = (
        P("row", "col", None),
        P("row", "col"),
        P("col"),
        P(),
        P(),
        P(),
        P(),
        P("row", "col", None),
    )
    out_specs = (P("row", "col", None), P("row", "col", None), P(), P(), P(), P())
    return jax.shard_map(
        per_device, mesh=mesh, in_specs=in_specs, out_specs=out_specs, check_vma=False
    )
```

```python
import functools

import jax
import jax.numpy as jnp
from jax import lax
from jax.experimental import pallas as pl
from jax.experimental.pallas import tpu as pltpu
from jax.sharding import PartitionSpec as P

PAIRED = 16
CHAINS = 4
BF = jnp.bfloat16
F32 = jnp.float32
STEP = 4
GROUP = 16
E_BLOCK = 8
E_WIDE = 16
FUSE = 4


def dot(a, b, lhs, rhs):
    return lax.dot_general(a, b, (((lhs,), (rhs,)), ((), ())), preferred_element_type=F32)


def rows_at(start, size):
    return pl.ds(pl.multiple_of(start, GROUP), size)


def normal(values):
    center = values - jnp.mean(values, axis=-1, keepdims=True)
    spread = jnp.mean(center * center, axis=-1, keepdims=True)
    scale = lax.rsqrt(spread + 1e-05)
    return center * scale, scale


def project_kernel(dims, msa, present, label, weights, offset, normed, live_ref, send, keep, right, left):
    src, seqs, hidden, row_dev, places, half = dims
    pairs = src // 2
    me = lax.axis_index("row")
    core = lax.rem(me, 2)
    first = lax.axis_index("col") == 0
    seq = me * seqs + lax.broadcasted_iota(jnp.int32, (seqs, places), 0)
    chain = lax.rem(seq + (CHAINS - PAIRED % CHAINS), CHAINS)
    permitted = (seq < PAIRED) | (chain == jnp.broadcast_to(label[...], (seqs, places)))
    live = jnp.where(permitted & (present[...] == 1), 1.0, 0.0).astype(F32)
    live = jnp.concatenate([live, jnp.zeros((8 - seqs, places), F32)], axis=0)
    live_ref[...] = live
    weight = weights[...].astype(F32)
    right_w = weight[hidden:].astype(BF)
    left_w = jnp.concatenate([weight[:hidden]] * seqs, axis=0).T.astype(BF)
    lane = lax.broadcasted_iota(jnp.int32, left_w.shape, 1) // hidden
    column = jnp.broadcast_to(offset[...], (8, 2 * hidden)).T[hidden:, :1]
    total = jnp.zeros((places, seqs * hidden), F32)
    for s in range(seqs):
        value = normal(msa[s].astype(F32))[0].astype(BF)
        normed[s] = value
        out = (dot(right_w, value, 1, 1) + column) * live[s : s + 1]
        for h in range(2):
            right[pl.ds(h * seqs * hidden + s * hidden, hidden), :] = out[:, h * half : (h + 1) * half]
        total = total + dot(value, jnp.where(lane == s, left_w, jnp.zeros_like(left_w)), 1, 0)
    total = total + jnp.concatenate([offset[:, :hidden]] * seqs, axis=1)
    spot = lax.broadcasted_iota(jnp.int32, (8, seqs * hidden), 0)
    expand = jnp.where(spot == lax.broadcasted_iota(jnp.int32, (8, seqs * hidden), 1) // hidden, 1.0, 0.0)
    total = total * dot(live.T.astype(BF), expand.astype(BF), 1, 0)
    left[...] = jnp.where(first, total, 0.0)
    place = lax.broadcasted_iota(jnp.int32, (places, half), 0)
    slot = lax.broadcasted_iota(jnp.int32, (places, half), 1)
    base = seqs * hidden
    for ref, to in ((send, 1 - core), (keep, core)):
        pick = jnp.where(place == slot // row_dev * 2 * row_dev + to * row_dev + lax.rem(slot, row_dev), 1.0, 0.0)
        band = dot(live.astype(BF), pick.astype(BF), 1, 0)[:seqs]
        band = jnp.where(first, band, 0.0)
        own = jnp.where(to == 0, live[:seqs, :half], live[:seqs, half:])
        flags = jnp.concatenate([own, band, jnp.zeros((GROUP - 2 * seqs, half), F32)], axis=0)
        ref[pl.ds(0, base), :] = right[rows_at(to * base, base), :].astype(BF)
        ref[pl.ds(base, GROUP), :] = flags.astype(BF)
        for q in range(pairs):
            ref[pl.ds(base + GROUP + q * row_dev, row_dev), :] = left[
                rows_at(q * 2 * row_dev + to * row_dev, row_dev), :
            ].astype(BF)


def pack_forward_kernel(dims, keep, came, out):
    src, seqs, hidden, row_dev, places, half = dims
    core = lax.rem(lax.axis_index("row"), 2)
    base = seqs * hidden
    for ref, who in ((keep, core), (came, 1 - core)):
        value = ref[pl.ds(0, base), :]
        flags = ref[pl.ds(base, GROUP), :]
        for q in range(src // 2):
            out[q, rows_at(who * base, base), :] = value
            out[q, rows_at(2 * base + who * GROUP, GROUP), :] = flags
            out[q, rows_at(2 * base + 2 * GROUP + who * row_dev, row_dev), :] = ref[
                pl.ds(base + GROUP + q * row_dev, row_dev), :
            ]


def left_rows_kernel(dims, mine, out, tiles):
    src, seqs, hidden, row_dev, places, half = dims
    first = 2 * seqs * hidden
    for q in range(src // 2):
        tiles[pl.ds(q * 2 * GROUP, 2 * GROUP), :] = mine[q, first : first + 2 * GROUP, :].astype(F32)
    rows = [tiles[pl.ds(seqs + s, src, stride=GROUP), :] for s in range(seqs)]
    blocks = [jnp.concatenate(rows, axis=0)]
    for q in range(src // 2):
        tiles[pl.ds(q * 2 * row_dev, 2 * row_dev), :] = mine[q, first + 2 * GROUP :, :].astype(F32)
    for i in range(row_dev):
        tile = tiles[pl.ds(i, src, stride=row_dev), :]
        blocks.append(jnp.concatenate([tile[:, s * hidden : (s + 1) * hidden] for s in range(seqs)], axis=0))
    out[...] = jnp.concatenate(blocks, axis=1).astype(BF)


def unpack_right_kernel(dims, mine, other, weights, r_ref, live_t_ref, by_e, by_e_t, r_all, flags, w_all):
    src, seqs, hidden, row_dev, places, half = dims
    base = seqs * hidden
    lines = src * base
    core = lax.rem(lax.axis_index("row"), 2)
    for ref, h in ((mine, core), (other, 1 - core)):
        for q in range(src // 2):
            r_all[rows_at(h * lines + q * 2 * base, 2 * base), :] = ref[q, : 2 * base, :].astype(F32)
            flags[rows_at((h * src + 2 * q) * GROUP, 2 * GROUP), :] = ref[
                q, 2 * base : 2 * base + 2 * GROUP, :
            ].astype(F32)
    w_all[...] = weights[...].astype(F32)
    for e in range(hidden):
        for h in range(2):
            rows = [r_all[pl.ds(h * lines + s * hidden + e, src, stride=base), :] for s in range(seqs)]
            r_ref[e, :, pl.ds(h * half, half)] = jnp.concatenate(rows, axis=0).astype(BF)
    for e in range(0, hidden, 4):
        rows = [w_all[pl.ds(e + n, hidden, stride=hidden), :] for n in range(4)]
        part = jnp.concatenate(rows, axis=0)
        by_e[pl.ds(e * hidden, 4 * hidden), :] = part.astype(BF)
        by_e_t[:, pl.ds(e * hidden, 4 * hidden)] = part.T.astype(BF)
    for h in range(2):
        rows = [flags[pl.ds(h * src * GROUP + s, src, stride=GROUP), :] for s in range(seqs)]
        live_t_ref[pl.ds(h * half, half), :] = jnp.concatenate(rows, axis=0).T.astype(BF)


def first_kernel(dims, tree, near_1, near_2, near_3, r_ref, live_t, adjoint, weights, g_ref, s_ref, d_ref, left_ref, bias_ref, left_out, left_t, total):
    src, seqs, hidden, row_dev, places, half = dims
    step = pl.program_id(0)

    @pl.when(step == 0)
    def _():
        pair = lax.axis_index("row") // 2
        spread = tree[...].astype(F32) + near_1[...].astype(F32) + near_2[...].astype(F32) + near_3[...].astype(F32)
        band = spread[:, :half].astype(BF)
        left = spread[:, half:]
        left_out[...] = left.astype(BF)
        left_t[...] = left.T.astype(BF)
        spot = lax.broadcasted_iota(jnp.int32, (half, half), 0) - pair * row_dev
        bias = jnp.zeros((1, half), F32)
        for i in range(row_dev):
            column = dot(band, jnp.where(spot == i, 1.0, 0.0).astype(BF), 1, 0).astype(BF)
            divisor = jnp.maximum(dot(live_t[...], column, 1, 0), 1.0)
            scaled = (adjoint[i].astype(F32) / divisor).astype(BF)
            d_ref[i] = divisor.astype(BF)
            s_ref[i] = scaled
            bias = bias + jnp.sum(scaled.astype(F32), axis=0, keepdims=True)
        bias_ref[...] = bias
        total[...] = jnp.zeros_like(total)

    part = weights[pl.ds(step * E_WIDE * hidden, E_WIDE * hidden), :]
    for i in range(row_dev):
        g = dot(part, s_ref[i], 1, 1).astype(BF)
        g_ref[:, pl.ds(i * hidden, hidden), :] = g.reshape(E_WIDE, hidden, places)
    acc = total[...]
    for e in range(0, E_WIDE, FUSE):
        right = jnp.concatenate([r_ref[step * E_WIDE + e + n] for n in range(FUSE)], axis=1)
        grad = jnp.concatenate([g_ref[e + n] for n in range(FUSE)], axis=1)
        acc = acc + dot(right, grad, 1, 1)
    total[...] = acc

    @pl.when(step == pl.num_programs(0) - 1)
    def _():
        for i in range(row_dev):
            block = acc[:, i * hidden : (i + 1) * hidden]
            left_ref[pl.ds(i, src, stride=row_dev), :] = jnp.concatenate(
                [block[s * src : (s + 1) * src] for s in range(seqs)], axis=1
            )


def outer_of(left_t, r_ref, outer):
    for e in range(E_BLOCK):
        outer[e] = dot(left_t[...], r_ref[e], 1, 0).astype(BF)


def outer_row(outer, i, hidden):
    return outer[:, pl.ds(i * hidden, hidden), :].reshape(E_BLOCK * hidden, outer.shape[2])


def second_kernel(dims, left_t, r_ref, s_ref, keep, send, outer, held):
    src, seqs, hidden, row_dev, places, half = dims
    step = pl.program_id(0)
    block_lines = E_BLOCK * hidden
    outer_of(left_t, r_ref, outer)
    acc = jnp.zeros((block_lines, half), F32)
    for i in range(0, row_dev, FUSE):
        blocks = [outer_row(outer, i + n, hidden) for n in range(FUSE)]
        scaled = s_ref[pl.ds(i, FUSE)].reshape(FUSE * places, half)
        acc = acc + dot(jnp.concatenate(blocks, axis=1), scaled, 1, 0)
    held[rows_at(step * block_lines, block_lines), :] = acc

    @pl.when(step == pl.num_programs(0) - 1)
    def _():
        core = lax.rem(lax.axis_index("row"), 2)
        lines = hidden * hidden // 2
        keep[...] = held[rows_at(core * lines, lines), :]
        send[...] = held[rows_at((1 - core) * lines, lines), :].astype(BF)


def pair_kernel(dims, left_t, r_ref, d_ref, weights_t, offset, pair_ref, outer, before):
    src, seqs, hidden, row_dev, places, half = dims
    step = pl.program_id(0)

    @pl.when(step == 0)
    def _():
        before[...] = jnp.zeros_like(before)

    outer_of(left_t, r_ref, outer)
    for i in range(row_dev):
        before[i] = before[i] + dot(weights_t[...], outer_row(outer, i, hidden), 1, 0)

    @pl.when(step == pl.num_programs(0) - 1)
    def _():
        for i in range(row_dev):
            pair_ref[i] = ((before[i].T + offset[...]) / d_ref[i].astype(F32)).astype(BF)


def third_kernel(dims, left, g_ref, keep, send, held):
    src, seqs, hidden, row_dev, places, half = dims
    step = pl.program_id(0)
    base = seqs * hidden
    lines = src * base
    for e in range(E_WIDE):
        grad = dot(left[...], g_ref[e], 1, 0)
        for h in range(2):
            for s in range(seqs):
                held[pl.ds(h * lines + s * hidden + step * E_WIDE + e, src, stride=base), :] = grad[
                    s * src : (s + 1) * src, h * half : (h + 1) * half
                ]

    @pl.when(step == pl.num_programs(0) - 1)
    def _():
        core = lax.rem(lax.axis_index("row"), 2)
        keep[...] = held[rows_at(core * lines, lines), :]
        send[...] = held[rows_at((1 - core) * lines, lines), :].astype(BF)


def pack_backward_kernel(dims, keep, came, w_keep, w_came, left, far_1, far_2, far_3, out):
    src, seqs, hidden, row_dev, places, half = dims
    pairs = src // 2
    lines = 2 * seqs * hidden
    w_lines = hidden * hidden // src
    total = left[...] + far_1[...].astype(F32) + far_2[...].astype(F32) + far_3[...].astype(F32)
    total = jnp.where(lax.axis_index("col") == 0, total, 0.0).astype(BF)
    for q in range(pairs):
        span = pl.ds(q * lines, lines)
        out[q, pl.ds(0, lines), :] = (keep[span, :] + came[span, :].astype(F32)).astype(BF)
        span = pl.ds(q * w_lines, w_lines)
        out[q, pl.ds(lines, w_lines), :] = (w_keep[span, :] + w_came[span, :].astype(F32)).astype(BF)
        out[q, pl.ds(lines + w_lines, 2 * row_dev), :] = total[q * 2 * row_dev : (q + 1) * 2 * row_dev]


def unpack_backward_kernel(dims, arrived, send, keep, chunk, held):
    src, seqs, hidden, row_dev, places, half = dims
    pairs = src // 2
    base = seqs * hidden
    w_lines = hidden * hidden // src
    core = lax.rem(lax.axis_index("row"), 2)
    total = arrived[0, : 2 * base + w_lines, :].astype(F32)
    for q in range(1, pairs):
        total = total + arrived[q, : 2 * base + w_lines, :].astype(F32)
    held[...] = total[: 2 * base]
    chunk[...] = total[2 * base :].astype(BF)
    for ref, to in ((send, 1 - core), (keep, core)):
        ref[pl.ds(0, base), :] = held[rows_at(to * base, base), :].astype(BF)
        for q in range(pairs):
            ref[pl.ds(base + q * row_dev, row_dev), :] = arrived[
                q, rows_at(2 * base + w_lines + to * row_dev, row_dev), :
            ]


def projector_kernel(dims, keep, came, normed, live, bias, grads, w_keep, w_send, small, right, left):
    src, seqs, hidden, row_dev, places, half = dims
    base = seqs * hidden
    core = lax.rem(lax.axis_index("row"), 2)
    for ref, who in ((keep, core), (came, 1 - core)):
        right[rows_at(who * base, base), :] = ref[pl.ds(0, base), :].astype(F32)
        for q in range(src // 2):
            left[rows_at(q * 2 * row_dev + who * row_dev, row_dev), :] = ref[
                pl.ds(base + q * row_dev, row_dev), :
            ].astype(F32)
    left_t = left[...].T
    weight = jnp.zeros((2 * hidden, places), F32)
    sums = jnp.zeros((8, 2 * hidden), F32)
    for s in range(seqs):
        span = slice(s * hidden, (s + 1) * hidden)
        right_s = jnp.concatenate([right[span, :], right[base + s * hidden : base + (s + 1) * hidden, :]], axis=1)
        grad = (jnp.concatenate([left_t[span], right_s], axis=0) * live[s : s + 1, :]).astype(BF)
        grads[pl.ds(s * 2 * hidden, 2 * hidden), :] = grad
        weight = weight + dot(grad, normed[s], 1, 0)
        sums = sums + dot(jnp.ones((8, places), BF), grad, 1, 1)
    low, high = weight[:, :half], weight[:, half:]
    w_keep[...] = jnp.where(core == 0, low, high)
    w_send[...] = jnp.where(core == 0, high, low).astype(BF)
    row = jnp.concatenate([sums[:1], jnp.zeros((1, half - 2 * hidden), F32)], axis=1)
    small[...] = bias_block(bias[...], row, half)


def bias_block(first, second, half):
    first_high, second_high = first.astype(BF).astype(F32), second.astype(BF).astype(F32)
    rows = [first_high, first - first_high, second_high, second - second_high]
    return jnp.concatenate(rows + [jnp.zeros((GROUP - 4, half), F32)], axis=0).astype(BF)


def align_kernel(dims, msa, grads, weights, out):
    src, seqs, hidden, row_dev, places, half = dims
    for s in range(seqs):
        grad = grads[pl.ds(s * 2 * hidden, 2 * hidden), :].astype(F32).T.astype(BF)
        grad = dot(grad, weights[...], 1, 0)
        value, scale = normal(msa[s].astype(F32))
        shift = jnp.mean(grad, axis=-1, keepdims=True)
        slope = jnp.mean(grad * value, axis=-1, keepdims=True)
        out[s] = (scale * (grad - shift - value * slope)).astype(BF)


def pack_column_kernel(dims, w_keep, w_came, chunk, small, out):
    weight = (w_keep[...] + w_came[...].astype(F32)).astype(BF)
    at = weight.shape[0]
    size = chunk.shape[0]
    out[pl.ds(0, at), :] = weight
    out[pl.ds(at, size), :] = chunk[...]
    out[pl.ds(at + size, GROUP), :] = small[...]


def sum_of_four(part_0, part_1, part_2, part_3):
    parts = [p[...].astype(F32) for p in (part_0, part_1, part_2, part_3)]
    total = (parts[0] + parts[1]) + (parts[2] + parts[3])
    at = total.shape[0] - GROUP
    last = total[at:]
    small = bias_block(last[0:1] + last[1:2], last[2:3] + last[3:4], last.shape[1])
    return total[:at].astype(BF), small


def column_sum_kernel(dims, part_0, part_1, part_2, part_3, out):
    total, small = sum_of_four(part_0, part_1, part_2, part_3)
    out[pl.ds(0, total.shape[0]), :] = total
    out[pl.ds(total.shape[0], GROUP), :] = small


def left_sum_kernel(dims, left, near_1, near_2, near_3, total, sent):
    value = left[...] + near_1[...].astype(F32) + near_2[...].astype(F32) + near_3[...].astype(F32)
    total[...] = value
    sent[...] = value.astype(BF)


def pack_row_kernel(dims, part_0, part_1, part_2, part_3, out):
    total, small = sum_of_four(part_0, part_1, part_2, part_3)
    for q in range(out.shape[0]):
        out[q, pl.ds(0, total.shape[0]), :] = total
        out[q, pl.ds(total.shape[0], GROUP), :] = small


def finish_kernel(dims, mine, other, projector, projector_bias, weight, bias, held):
    src, seqs, hidden, row_dev, places, half = dims
    core = lax.rem(lax.axis_index("row"), 2)
    w_lines = hidden * hidden // src
    at = 2 * hidden + w_lines
    sums = []
    small = jnp.zeros((GROUP, half), F32)
    for ref, who in ((mine, core), (other, 1 - core)):
        total = jnp.zeros((2 * hidden, half), F32)
        for q in range(src // 2):
            total = total + ref[q, : 2 * hidden, :].astype(F32)
            small = small + ref[q, at : at + GROUP, :].astype(F32)
            held[rows_at(who * (hidden * hidden // 2) + q * w_lines, w_lines), :] = ref[
                q, 2 * hidden : at, :
            ].astype(F32)
        sums.append(total)
    first = jnp.where(core == 0, sums[0], sums[1])
    second = jnp.where(core == 0, sums[1], sums[0])
    projector[...] = jnp.concatenate([first, second], axis=1)
    bias[...] = small[0:1] + small[1:2]
    projector_bias[...] = (small[2:3] + small[3:4])[:, : 2 * hidden]
    for c in range(hidden):
        weight[pl.ds(c * hidden, hidden), :] = held[pl.ds(c, hidden, stride=hidden), :]


def shape_of(dtype, *shape):
    return jax.ShapeDtypeStruct(shape, dtype)


def whole(*shape):
    return pl.BlockSpec(shape, lambda t: (0,) * len(shape))


def call(kernel, dims, name, args, outs, scratch=(), steps=1, in_specs=None, out_specs=None, macs=0, room=16):
    in_specs, out_specs = in_specs or {}, out_specs or {}
    specs = [in_specs.get(n, whole(*a.shape)) for n, a in enumerate(args)]
    size = sum(a.size * a.dtype.itemsize for a in args)
    size += sum(o.size * jnp.dtype(o.dtype).itemsize for o in outs)
    result = pl.pallas_call(
        functools.partial(kernel, dims),
        grid=(steps,),
        in_specs=specs,
        out_specs=[out_specs.get(n, whole(*o.shape)) for n, o in enumerate(outs)],
        out_shape=list(outs),
        scratch_shapes=[pltpu.VMEM(s, t) for s, t in scratch],
        compiler_params=pltpu.CompilerParams(
            dimension_semantics=("arbitrary",), vmem_limit_bytes=room * 2**20
        ),
        cost_estimate=pl.CostEstimate(flops=40 * macs, bytes_accessed=size, transcendentals=0),
        name=name,
    )(*args)
    return result


def near_parts(block, cols):
    return [
        lax.ppermute(block, "col", [(a, a + d) for a in range(0, cols, STEP)])
        for d in range(1, STEP)
    ]


def swap_parts(block, cols, unit):
    swaps = [lax.ppermute(block, "col", [(i, i ^ d * unit) for i in range(cols)]) for d in range(1, STEP)]
    return [block, *swaps]


def per_device(
    homolog_features,
    presence_indicator,
    polymer_label,
    lowering_matrix,
    lowering_offset,
    outgoing_matrix,
    outgoing_offset,
    update_adjoint,
):
    seqs, places, depth = homolog_features.shape
    hidden = lowering_matrix.shape[1] // 2
    channels = outgoing_matrix.shape[1]
    row_dev = update_adjoint.shape[0]
    rows, cols = lax.axis_size("row"), lax.axis_size("col")
    pairs, half = rows // 2, channels
    dims = (rows, seqs, hidden, row_dev, places, half)
    base = seqs * hidden
    total = rows * seqs
    lines = row_dev * hidden
    w_lines = hidden * hidden // rows
    swap = [(i, i ^ 1) for i in range(rows)]
    same_core = [list(range(c, rows, 2)) for c in range(2)]

    def partner(block):
        return lax.ppermute(block, "row", swap)

    def over_pairs(block):
        return lax.all_to_all(block, "row", 0, 0, axis_index_groups=same_core, tiled=True)

    size = base + GROUP + pairs * row_dev
    normed, live, send, keep = call(
        project_kernel,
        dims,
        "project",
        (homolog_features, presence_indicator, polymer_label[None], lowering_matrix.T, lowering_offset[None]),
        (
            shape_of(BF, seqs, places, depth),
            shape_of(F32, 8, places),
            shape_of(BF, size, half),
            shape_of(BF, size, half),
        ),
        [((2 * base, half), F32), ((places, base), F32)],
        macs=100_000_000,
        room=62,
    )
    came = partner(send)

    packed = call(
        pack_forward_kernel,
        dims,
        "pack_forward",
        (keep, came),
        (shape_of(BF, pairs, 2 * (base + GROUP + row_dev), half),),
    )[0]
    mine = over_pairs(packed)
    tree = call(
        left_rows_kernel,
        dims,
        "left_rows",
        (mine,),
        (shape_of(BF, total, half + lines),),
        [((rows * GROUP, half), F32)],
    )[0]
    far = [lax.ppermute(tree, "col", [(0, d)]) for d in range(STEP, cols, STEP)]
    tree = sum(far, tree)
    near = near_parts(tree, cols)
    mine, tree = lax.optimization_barrier((mine, tree))
    other = partner(mine)
    right_cols, live_t, by_e, by_e_t = call(
        unpack_right_kernel,
        dims,
        "unpack_right",
        (mine, other, outgoing_matrix),
        (
            shape_of(BF, hidden, total, places),
            shape_of(BF, places, total),
            shape_of(BF, hidden * hidden, channels),
            shape_of(BF, channels, hidden * hidden),
        ),
        [
            ((2 * rows * base, half), F32),
            ((2 * rows * GROUP, half), F32),
            ((hidden * hidden, channels), F32),
        ],
        macs=300_000_000,
    )

    by_block = lambda size, *block: pl.BlockSpec((size, *block), lambda t: (t, 0, 0))
    outer_grad, scaled, divisor, left_grad, bias_grad, left_rows, left_t = call(
        first_kernel,
        dims,
        "scaled_outer_grad",
        (tree, *near, right_cols, live_t, update_adjoint, by_e),
        (
            shape_of(BF, hidden, lines, places),
            shape_of(BF, row_dev, places, channels),
            shape_of(BF, row_dev, places, channels),
            shape_of(F32, rows * row_dev, half),
            shape_of(F32, 1, channels),
            shape_of(BF, total, lines),
            shape_of(BF, lines, total),
        ),
        [((total, lines), F32)],
        steps=hidden // E_WIDE,
        out_specs={0: by_block(E_WIDE, lines, places)},
        macs=800_000_000,
        room=24,
    )

    sent = left_grad.astype(BF)
    near = [
        lax.ppermute(sent, "col", [(a + d, a) for a in range(0, cols, STEP)])
        for d in range(1, STEP)
    ]
    right_keep, right_send = call(
        third_kernel,
        dims,
        "right_grad",
        (left_rows, outer_grad),
        (shape_of(F32, rows * base, half), shape_of(BF, rows * base, half)),
        [((2 * rows * base, half), F32)],
        steps=hidden // E_WIDE,
        in_specs={1: by_block(E_WIDE, lines, places)},
        macs=270_000_000,
        room=24,
    )
    *near, right_send = lax.optimization_barrier((*near, right_send))
    left_grad, sent = call(
        left_sum_kernel,
        dims,
        "left_sum",
        (left_grad, *near),
        (shape_of(F32, rows * row_dev, half), shape_of(BF, rows * row_dev, half)),
    )
    left_t, sent = lax.optimization_barrier((left_t, sent))
    far = [lax.ppermute(sent, "col", [(d, 0)]) for d in range(STEP, cols, STEP)]
    w_keep, w_send = call(
        second_kernel,
        dims,
        "outer_weight_grad",
        (left_t, right_cols, scaled),
        (shape_of(F32, hidden * hidden // 2, channels), shape_of(BF, hidden * hidden // 2, channels)),
        [((E_BLOCK, lines, places), BF), ((hidden * hidden, channels), F32)],
        steps=hidden // E_BLOCK,
        in_specs={1: by_block(E_BLOCK, total, places)},
        macs=800_000_000,
        room=20,
    )
    w_send, *far = lax.optimization_barrier((w_send, *far))
    w_came = partner(w_send)
    right_came = partner(right_send)
    packed = call(
        pack_backward_kernel,
        dims,
        "pack_backward",
        (right_keep, right_came, w_keep, w_came, left_grad, *far),
        (shape_of(BF, pairs, 2 * base + w_lines + 2 * row_dev, half),),
    )[0]
    arrived = over_pairs(packed)

    send, keep, chunk = call(
        unpack_backward_kernel,
        dims,
        "unpack_backward",
        (arrived,),
        (
            shape_of(BF, base + pairs * row_dev, half),
            shape_of(BF, base + pairs * row_dev, half),
            shape_of(BF, w_lines, half),
        ),
        [((2 * base, half), F32)],
    )
    came = partner(send)
    grads, w_keep, w_send, small = call(
        projector_kernel,
        dims,
        "projector_grad",
        (keep, came, normed, live, bias_grad),
        (
            shape_of(BF, seqs * 2 * hidden, places),
            shape_of(F32, 2 * hidden, half),
            shape_of(BF, 2 * hidden, half),
            shape_of(BF, GROUP, half),
        ),
        [((2 * base, half), F32), ((places, base), F32)],
        macs=20_000_000,
    )
    w_came = partner(w_send)
    size = 2 * hidden + w_lines + GROUP
    own = call(
        pack_column_kernel, dims, "pack_column", (w_keep, w_came, chunk, small), (shape_of(BF, size, half),)
    )[0]
    parts = swap_parts(own, cols, STEP)
    pair_increment = call(
        pair_kernel,
        dims,
        "outer_pair",
        (left_t, right_cols, divisor, by_e_t, outgoing_offset[None]),
        (shape_of(BF, row_dev, places, channels),),
        [((E_BLOCK, lines, places), BF), ((row_dev, channels, places), F32)],
        steps=hidden // E_BLOCK,
        in_specs={
            1: by_block(E_BLOCK, total, places),
            3: pl.BlockSpec((channels, E_BLOCK * hidden), lambda t: (0, t)),
        },
        macs=800_000_000,
        room=20,
    )[0]
    *parts, pair_increment = lax.optimization_barrier((*parts, pair_increment))
    own = call(column_sum_kernel, dims, "column_sum", parts, (shape_of(BF, size, half),))[0]
    parts = swap_parts(own, cols, 1)
    alignment_gradient = call(
        align_kernel,
        dims,
        "alignment",
        (homolog_features, grads, lowering_matrix.T),
        (shape_of(BF, seqs, places, depth),),
        macs=200_000_000,
    )[0]
    *parts, alignment_gradient = lax.optimization_barrier((*parts, alignment_gradient))
    packed = call(pack_row_kernel, dims, "pack_row", parts, (shape_of(BF, pairs, size, half),))[0]
    mine = over_pairs(packed)
    other = partner(mine)
    projector, projector_bias, weight, bias = call(
        finish_kernel,
        dims,
        "finish",
        (mine, other),
        (
            shape_of(F32, 2 * hidden, depth),
            shape_of(F32, 1, 2 * hidden),
            shape_of(F32, hidden * hidden, channels),
            shape_of(F32, 1, channels),
        ),
        [((hidden * hidden, channels), F32)],
    )
    return (
        pair_increment,
        alignment_gradient,
        projector.T,
        projector_bias[0],
        weight,
        bias[0],
    )


def solution(mesh):
    in_specs = (
        P("row", "col", None),
        P("row", "col"),
        P("col"),
        P(),
        P(),
        P(),
        P(),
        P("row", "col", None),
    )
    out_specs = (P("row", "col", None), P("row", "col", None), P(), P(), P(), P())
    return jax.shard_map(
        per_device, mesh=mesh, in_specs=in_specs, out_specs=out_specs, check_vma=False
    )
```

```python
import functools

import jax
import jax.numpy as jnp
from jax import lax
from jax.experimental import pallas as pl
from jax.experimental.pallas import tpu as pltpu
from jax.sharding import PartitionSpec as P

PAIRED = 16
CHAINS = 4
BF = jnp.bfloat16
F32 = jnp.float32
STEP = 4
GROUP = 16
FUSE_E = 8
FUSE_I = 8


def dot(a, b, lhs, rhs):
    return lax.dot_general(a, b, (((lhs,), (rhs,)), ((), ())), preferred_element_type=F32)


def rows_at(start, size):
    return pl.ds(pl.multiple_of(start, GROUP), size)


def normal(values):
    center = values - jnp.mean(values, axis=-1, keepdims=True)
    spread = jnp.mean(center * center, axis=-1, keepdims=True)
    scale = lax.rsqrt(spread + 1e-05)
    return center * scale, scale


def project_kernel(dims, msa, present, label, weights, offset, normed, live_ref, send, keep, right, left):
    src, seqs, hidden, row_dev, places, half = dims
    pairs = src // 2
    me = lax.axis_index("row")
    core = lax.rem(me, 2)
    first = lax.axis_index("col") == 0
    seq = me * seqs + lax.broadcasted_iota(jnp.int32, (seqs, places), 0)
    chain = lax.rem(seq + (CHAINS - PAIRED % CHAINS), CHAINS)
    permitted = (seq < PAIRED) | (chain == jnp.broadcast_to(label[...], (seqs, places)))
    live = jnp.where(permitted & (present[...] == 1), 1.0, 0.0).astype(F32)
    live = jnp.concatenate([live, jnp.zeros((8 - seqs, places), F32)], axis=0)
    live_ref[...] = live
    weight = weights[...].astype(F32)
    right_w = weight[hidden:].astype(BF)
    left_w = jnp.concatenate([weight[:hidden]] * seqs, axis=0).T.astype(BF)
    lane = lax.broadcasted_iota(jnp.int32, left_w.shape, 1) // hidden
    column = jnp.broadcast_to(offset[...], (8, 2 * hidden)).T[hidden:, :1]
    total = jnp.zeros((places, seqs * hidden), F32)
    for s in range(seqs):
        value = normal(msa[s].astype(F32))[0].astype(BF)
        normed[s] = value
        out = (dot(right_w, value, 1, 1) + column) * live[s : s + 1]
        for h in range(2):
            right[pl.ds(h * seqs * hidden + s * hidden, hidden), :] = out[:, h * half : (h + 1) * half]
        total = total + dot(value, jnp.where(lane == s, left_w, jnp.zeros_like(left_w)), 1, 0)
    total = total + jnp.concatenate([offset[:, :hidden]] * seqs, axis=1)
    spot = lax.broadcasted_iota(jnp.int32, (8, seqs * hidden), 0)
    expand = jnp.where(spot == lax.broadcasted_iota(jnp.int32, (8, seqs * hidden), 1) // hidden, 1.0, 0.0)
    total = total * dot(live.T.astype(BF), expand.astype(BF), 1, 0)
    left[...] = jnp.where(first, total, 0.0)
    place = lax.broadcasted_iota(jnp.int32, (places, half), 0)
    slot = lax.broadcasted_iota(jnp.int32, (places, half), 1)
    base = seqs * hidden
    for ref, to in ((send, 1 - core), (keep, core)):
        pick = jnp.where(place == slot // row_dev * 2 * row_dev + to * row_dev + lax.rem(slot, row_dev), 1.0, 0.0)
        band = dot(live.astype(BF), pick.astype(BF), 1, 0)[:seqs]
        band = jnp.where(first, band, 0.0)
        own = jnp.where(to == 0, live[:seqs, :half], live[:seqs, half:])
        flags = jnp.concatenate([own, band, jnp.zeros((GROUP - 2 * seqs, half), F32)], axis=0)
        ref[pl.ds(0, base), :] = right[rows_at(to * base, base), :].astype(BF)
        ref[pl.ds(base, GROUP), :] = flags.astype(BF)
        for q in range(pairs):
            ref[pl.ds(base + GROUP + q * row_dev, row_dev), :] = left[
                rows_at(q * 2 * row_dev + to * row_dev, row_dev), :
            ].astype(BF)


def move_kernel(dims, block, out):
    out[...] = block[...]


def pack_forward_kernel(dims, keep, came, out):
    src, seqs, hidden, row_dev, places, half = dims
    core = lax.rem(lax.axis_index("row"), 2)
    base = seqs * hidden
    for ref, who in ((keep, core), (came, 1 - core)):
        value = ref[pl.ds(0, base), :]
        flags = ref[pl.ds(base, GROUP), :]
        for q in range(src // 2):
            out[q, rows_at(who * base, base), :] = value
            out[q, rows_at(2 * base + who * GROUP, GROUP), :] = flags
            out[q, rows_at(2 * base + 2 * GROUP + who * row_dev, row_dev), :] = ref[
                pl.ds(base + GROUP + q * row_dev, row_dev), :
            ]


def left_rows_kernel(dims, mine, out, tiles):
    src, seqs, hidden, row_dev, places, half = dims
    first = 2 * seqs * hidden
    for q in range(src // 2):
        tiles[pl.ds(q * 2 * GROUP, 2 * GROUP), :] = mine[q, first : first + 2 * GROUP, :].astype(F32)
    rows = [tiles[pl.ds(seqs + s, src, stride=GROUP), :] for s in range(seqs)]
    blocks = [jnp.concatenate(rows, axis=0)]
    for q in range(src // 2):
        tiles[pl.ds(q * 2 * row_dev, 2 * row_dev), :] = mine[q, first + 2 * GROUP :, :].astype(F32)
    for i in range(row_dev):
        tile = tiles[pl.ds(i, src, stride=row_dev), :]
        blocks.append(jnp.concatenate([tile[:, s * hidden : (s + 1) * hidden] for s in range(seqs)], axis=0))
    out[...] = jnp.concatenate(blocks, axis=1).astype(BF)


def unpack_right_kernel(dims, mine, other, weights, r_ref, live_t_ref, by_e, by_e_t, r_all, flags, w_all):
    src, seqs, hidden, row_dev, places, half = dims
    base = seqs * hidden
    lines = src * base
    core = lax.rem(lax.axis_index("row"), 2)
    for ref, h in ((mine, core), (other, 1 - core)):
        for q in range(src // 2):
            r_all[rows_at(h * lines + q * 2 * base, 2 * base), :] = ref[q, : 2 * base, :].astype(F32)
            flags[rows_at((h * src + 2 * q) * GROUP, 2 * GROUP), :] = ref[
                q, 2 * base : 2 * base + 2 * GROUP, :
            ].astype(F32)
    w_all[...] = weights[...].astype(F32)
    for e in range(hidden):
        for h in range(2):
            rows = [r_all[pl.ds(h * lines + s * hidden + e, src, stride=base), :] for s in range(seqs)]
            r_ref[e, :, pl.ds(h * half, half)] = jnp.concatenate(rows, axis=0).astype(BF)
    for e in range(0, hidden, 4):
        rows = [w_all[pl.ds(e + n, hidden, stride=hidden), :] for n in range(4)]
        part = jnp.concatenate(rows, axis=0)
        by_e[pl.ds(e * hidden, 4 * hidden), :] = part.astype(BF)
        by_e_t[:, pl.ds(e * hidden, 4 * hidden)] = part.T.astype(BF)
    for h in range(2):
        rows = [flags[pl.ds(h * src * GROUP + s, src, stride=GROUP), :] for s in range(seqs)]
        live_t_ref[pl.ds(h * half, half), :] = jnp.concatenate(rows, axis=0).T.astype(BF)


def first_kernel(dims, tree, near_1, near_2, near_3, r_ref, live_t, adjoint, weights, g_ref, s_ref, d_ref, left_ref, bias_ref, left_out, left_t):
    src, seqs, hidden, row_dev, places, half = dims
    pair = lax.axis_index("row") // 2
    spread = tree[...].astype(F32) + near_1[...].astype(F32) + near_2[...].astype(F32) + near_3[...].astype(F32)
    band = spread[:, :half].astype(BF)
    left = spread[:, half:]
    left_out[...] = left.astype(BF)
    left_t[...] = left.T.astype(BF)
    spot = lax.broadcasted_iota(jnp.int32, (half, half), 0) - pair * row_dev
    bias = jnp.zeros((1, half), F32)
    for i in range(row_dev):
        column = dot(band, jnp.where(spot == i, 1.0, 0.0).astype(BF), 1, 0).astype(BF)
        divisor = jnp.maximum(dot(live_t[...], column, 1, 0), 1.0)
        scaled = (adjoint[i].astype(F32) / divisor).astype(BF)
        d_ref[i] = divisor.astype(BF)
        s_ref[i] = scaled
        bias = bias + jnp.sum(scaled.astype(F32), axis=0, keepdims=True)
    bias_ref[...] = bias
    for i in range(row_dev):
        g = dot(weights[...], s_ref[i], 1, 1).astype(BF)
        g_ref[:, pl.ds(i * hidden, hidden), :] = g.reshape(hidden, hidden, places)
    acc = jnp.zeros((src * seqs, row_dev * hidden), F32)
    for e in range(0, hidden, FUSE_E):
        right = jnp.concatenate([r_ref[e + n] for n in range(FUSE_E)], axis=1)
        grad = jnp.concatenate([g_ref[e + n] for n in range(FUSE_E)], axis=1)
        acc = acc + dot(right, grad, 1, 1)
    for i in range(row_dev):
        block = acc[:, i * hidden : (i + 1) * hidden]
        left_ref[pl.ds(i, src, stride=row_dev), :] = jnp.concatenate(
            [block[s * src : (s + 1) * src] for s in range(seqs)], axis=1
        )


def outer_of(left_t, r_ref, outer):
    for e in range(outer.shape[0]):
        outer[e] = dot(left_t[...], r_ref[e], 1, 0).astype(BF)


def outer_row(outer, i, hidden):
    return outer[:, pl.ds(i * hidden, hidden), :].reshape(hidden * hidden, outer.shape[2])


def second_kernel(dims, left_t, r_ref, s_ref, keep, send, outer, held):
    src, seqs, hidden, row_dev, places, half = dims
    outer_of(left_t, r_ref, outer)
    acc = jnp.zeros((hidden * hidden, half), F32)
    for i in range(0, row_dev, FUSE_I):
        blocks = [outer_row(outer, i + n, hidden) for n in range(FUSE_I)]
        scaled = s_ref[pl.ds(i, FUSE_I)].reshape(FUSE_I * places, half)
        acc = acc + dot(jnp.concatenate(blocks, axis=1), scaled, 1, 0)
    held[...] = acc
    core = lax.rem(lax.axis_index("row"), 2)
    lines = hidden * hidden // 2
    keep[...] = held[rows_at(core * lines, lines), :]
    send[...] = held[rows_at((1 - core) * lines, lines), :].astype(BF)


def pair_kernel(dims, left_t, r_ref, d_ref, weights_t, offset, pair_ref, outer):
    src, seqs, hidden, row_dev, places, half = dims
    outer_of(left_t, r_ref, outer)
    for i in range(row_dev):
        before = dot(weights_t[...], outer_row(outer, i, hidden), 1, 0)
        pair_ref[i] = ((before.T + offset[...]) / d_ref[i].astype(F32)).astype(BF)


def third_kernel(dims, left, g_ref, keep, send, held):
    src, seqs, hidden, row_dev, places, half = dims
    base = seqs * hidden
    lines = src * base
    for e in range(hidden):
        grad = dot(left[...], g_ref[e], 1, 0)
        for h in range(2):
            for s in range(seqs):
                held[pl.ds(h * lines + s * hidden + e, src, stride=base), :] = grad[
                    s * src : (s + 1) * src, h * half : (h + 1) * half
                ]
    core = lax.rem(lax.axis_index("row"), 2)
    keep[...] = held[rows_at(core * lines, lines), :]
    send[...] = held[rows_at((1 - core) * lines, lines), :].astype(BF)


def pack_backward_kernel(dims, keep, came, w_keep, w_came, left, far_1, far_2, far_3, out):
    src, seqs, hidden, row_dev, places, half = dims
    pairs = src // 2
    lines = 2 * seqs * hidden
    w_lines = hidden * hidden // src
    total = left[...] + far_1[...].astype(F32) + far_2[...].astype(F32) + far_3[...].astype(F32)
    total = jnp.where(lax.axis_index("col") == 0, total, 0.0).astype(BF)
    for q in range(pairs):
        span = pl.ds(q * lines, lines)
        out[q, pl.ds(0, lines), :] = (keep[span, :] + came[span, :].astype(F32)).astype(BF)
        span = pl.ds(q * w_lines, w_lines)
        out[q, pl.ds(lines, w_lines), :] = (w_keep[span, :] + w_came[span, :].astype(F32)).astype(BF)
        out[q, pl.ds(lines + w_lines, 2 * row_dev), :] = total[q * 2 * row_dev : (q + 1) * 2 * row_dev]


def unpack_backward_kernel(dims, arrived, send, keep, chunk, held):
    src, seqs, hidden, row_dev, places, half = dims
    pairs = src // 2
    base = seqs * hidden
    w_lines = hidden * hidden // src
    core = lax.rem(lax.axis_index("row"), 2)
    total = arrived[0, : 2 * base + w_lines, :].astype(F32)
    for q in range(1, pairs):
        total = total + arrived[q, : 2 * base + w_lines, :].astype(F32)
    held[...] = total[: 2 * base]
    chunk[...] = total[2 * base :].astype(BF)
    for ref, to in ((send, 1 - core), (keep, core)):
        ref[pl.ds(0, base), :] = held[rows_at(to * base, base), :].astype(BF)
        for q in range(pairs):
            ref[pl.ds(base + q * row_dev, row_dev), :] = arrived[
                q, rows_at(2 * base + w_lines + to * row_dev, row_dev), :
            ]


def projector_kernel(dims, keep, came, normed, live, bias, grads, w_keep, w_send, small, right, left):
    src, seqs, hidden, row_dev, places, half = dims
    base = seqs * hidden
    core = lax.rem(lax.axis_index("row"), 2)
    for ref, who in ((keep, core), (came, 1 - core)):
        right[rows_at(who * base, base), :] = ref[pl.ds(0, base), :].astype(F32)
        for q in range(src // 2):
            left[rows_at(q * 2 * row_dev + who * row_dev, row_dev), :] = ref[
                pl.ds(base + q * row_dev, row_dev), :
            ].astype(F32)
    left_t = left[...].T
    weight = jnp.zeros((2 * hidden, places), F32)
    sums = jnp.zeros((8, 2 * hidden), F32)
    for s in range(seqs):
        span = slice(s * hidden, (s + 1) * hidden)
        right_s = jnp.concatenate([right[span, :], right[base + s * hidden : base + (s + 1) * hidden, :]], axis=1)
        grad = (jnp.concatenate([left_t[span], right_s], axis=0) * live[s : s + 1, :]).astype(BF)
        grads[pl.ds(s * 2 * hidden, 2 * hidden), :] = grad
        weight = weight + dot(grad, normed[s], 1, 0)
        sums = sums + dot(jnp.ones((8, places), BF), grad, 1, 1)
    low, high = weight[:, :half], weight[:, half:]
    w_keep[...] = jnp.where(core == 0, low, high)
    w_send[...] = jnp.where(core == 0, high, low).astype(BF)
    row = jnp.concatenate([sums[:1], jnp.zeros((1, half - 2 * hidden), F32)], axis=1)
    small[...] = bias_block(bias[...], row, half)


def bias_block(first, second, half):
    first_high, second_high = first.astype(BF).astype(F32), second.astype(BF).astype(F32)
    rows = [first_high, first - first_high, second_high, second - second_high]
    return jnp.concatenate(rows + [jnp.zeros((GROUP - 4, half), F32)], axis=0).astype(BF)


def align_kernel(dims, msa, grads, weights, out):
    src, seqs, hidden, row_dev, places, half = dims
    for s in range(seqs):
        grad = grads[pl.ds(s * 2 * hidden, 2 * hidden), :].astype(F32).T.astype(BF)
        grad = dot(grad, weights[...], 1, 0)
        value, scale = normal(msa[s].astype(F32))
        shift = jnp.mean(grad, axis=-1, keepdims=True)
        slope = jnp.mean(grad * value, axis=-1, keepdims=True)
        out[s] = (scale * (grad - shift - value * slope)).astype(BF)


def pack_column_kernel(dims, w_keep, w_came, chunk, small, out):
    weight = (w_keep[...] + w_came[...].astype(F32)).astype(BF)
    at = weight.shape[0]
    size = chunk.shape[0]
    out[pl.ds(0, at), :] = weight
    out[pl.ds(at, size), :] = chunk[...]
    out[pl.ds(at + size, GROUP), :] = small[...]


def sum_of_four(part_0, part_1, part_2, part_3):
    parts = [p[...].astype(F32) for p in (part_0, part_1, part_2, part_3)]
    total = (parts[0] + parts[1]) + (parts[2] + parts[3])
    at = total.shape[0] - GROUP
    last = total[at:]
    small = bias_block(last[0:1] + last[1:2], last[2:3] + last[3:4], last.shape[1])
    return total[:at].astype(BF), small


def column_sum_kernel(dims, part_0, part_1, part_2, part_3, out):
    total, small = sum_of_four(part_0, part_1, part_2, part_3)
    out[pl.ds(0, total.shape[0]), :] = total
    out[pl.ds(total.shape[0], GROUP), :] = small


def left_sum_kernel(dims, left, near_1, near_2, near_3, total, sent):
    value = left[...] + near_1[...].astype(F32) + near_2[...].astype(F32) + near_3[...].astype(F32)
    total[...] = value
    sent[...] = value.astype(BF)


def pack_row_kernel(dims, part_0, part_1, part_2, part_3, out):
    total, small = sum_of_four(part_0, part_1, part_2, part_3)
    for q in range(out.shape[0]):
        out[q, pl.ds(0, total.shape[0]), :] = total
        out[q, pl.ds(total.shape[0], GROUP), :] = small


def finish_kernel(dims, mine, other, projector, projector_bias, weight, bias, held):
    src, seqs, hidden, row_dev, places, half = dims
    core = lax.rem(lax.axis_index("row"), 2)
    w_lines = hidden * hidden // src
    at = 2 * hidden + w_lines
    sums = []
    small = jnp.zeros((GROUP, half), F32)
    for ref, who in ((mine, core), (other, 1 - core)):
        total = jnp.zeros((2 * hidden, half), F32)
        for q in range(src // 2):
            total = total + ref[q, : 2 * hidden, :].astype(F32)
            small = small + ref[q, at : at + GROUP, :].astype(F32)
            held[rows_at(who * (hidden * hidden // 2) + q * w_lines, w_lines), :] = ref[
                q, 2 * hidden : at, :
            ].astype(F32)
        sums.append(total)
    first = jnp.where(core == 0, sums[0], sums[1])
    second = jnp.where(core == 0, sums[1], sums[0])
    projector[...] = jnp.concatenate([first, second], axis=1)
    bias[...] = small[0:1] + small[1:2]
    projector_bias[...] = (small[2:3] + small[3:4])[:, : 2 * hidden]
    for c in range(hidden):
        weight[pl.ds(c * hidden, hidden), :] = held[pl.ds(c, hidden, stride=hidden), :]


def shape_of(dtype, *shape):
    return jax.ShapeDtypeStruct(shape, dtype)


def whole(*shape):
    return pl.BlockSpec(shape, lambda t: (0,) * len(shape))


def call(kernel, dims, name, args, outs, scratch=(), macs=0, room=16):
    size = sum(a.size * a.dtype.itemsize for a in args)
    size += sum(o.size * jnp.dtype(o.dtype).itemsize for o in outs)
    result = pl.pallas_call(
        functools.partial(kernel, dims),
        grid=(1,),
        in_specs=[whole(*a.shape) for a in args],
        out_specs=[whole(*o.shape) for o in outs],
        out_shape=list(outs),
        scratch_shapes=[pltpu.VMEM(s, t) for s, t in scratch],
        compiler_params=pltpu.CompilerParams(
            dimension_semantics=("arbitrary",), vmem_limit_bytes=room * 2**20
        ),
        cost_estimate=pl.CostEstimate(flops=40 * macs, bytes_accessed=size, transcendentals=0),
        name=name,
    )(*args)
    return result


def near_parts(block, cols):
    return [
        lax.ppermute(block, "col", [(a, a + d) for a in range(0, cols, STEP)])
        for d in range(1, STEP)
    ]


def swap_parts(block, cols, unit):
    swaps = [lax.ppermute(block, "col", [(i, i ^ d * unit) for i in range(cols)]) for d in range(1, STEP)]
    return [block, *swaps]


def per_device(
    homolog_features,
    presence_indicator,
    polymer_label,
    lowering_matrix,
    lowering_offset,
    outgoing_matrix,
    outgoing_offset,
    update_adjoint,
):
    seqs, places, depth = homolog_features.shape
    hidden = lowering_matrix.shape[1] // 2
    channels = outgoing_matrix.shape[1]
    row_dev = update_adjoint.shape[0]
    rows, cols = lax.axis_size("row"), lax.axis_size("col")
    pairs, half = rows // 2, channels
    dims = (rows, seqs, hidden, row_dev, places, half)
    base = seqs * hidden
    total = rows * seqs
    lines = row_dev * hidden
    w_lines = hidden * hidden // rows
    swap = [(i, i ^ 1) for i in range(rows)]
    same_core = [list(range(c, rows, 2)) for c in range(2)]

    def partner(block):
        return lax.ppermute(block, "row", swap)

    def over_pairs(block):
        return lax.all_to_all(block, "row", 0, 0, axis_index_groups=same_core, tiled=True)

    size = base + GROUP + pairs * row_dev
    normed, live, send, keep = call(
        project_kernel,
        dims,
        "project",
        (homolog_features, presence_indicator, polymer_label[None], lowering_matrix.T, lowering_offset[None]),
        (
            shape_of(BF, seqs, places, depth),
            shape_of(F32, 8, places),
            shape_of(BF, size, half),
            shape_of(BF, size, half),
        ),
        [((2 * base, half), F32), ((places, base), F32)],
        macs=100_000_000,
        room=62,
    )
    came = partner(send)
    keep = call(move_kernel, dims, "move", (keep,), (shape_of(BF, size, half),))[0]
    came, keep = lax.optimization_barrier((came, keep))

    packed = call(
        pack_forward_kernel,
        dims,
        "pack_forward",
        (keep, came),
        (shape_of(BF, pairs, 2 * (base + GROUP + row_dev), half),),
    )[0]
    mine = over_pairs(packed)
    tree = call(
        left_rows_kernel,
        dims,
        "left_rows",
        (mine,),
        (shape_of(BF, total, half + lines),),
        [((rows * GROUP, half), F32)],
    )[0]
    far = [lax.ppermute(tree, "col", [(0, d)]) for d in range(STEP, cols, STEP)]
    tree = sum(far, tree)
    near = near_parts(tree, cols)
    mine, tree = lax.optimization_barrier((mine, tree))
    other = partner(mine)
    right_cols, live_t, by_e, by_e_t = call(
        unpack_right_kernel,
        dims,
        "unpack_right",
        (mine, other, outgoing_matrix),
        (
            shape_of(BF, hidden, total, places),
            shape_of(BF, places, total),
            shape_of(BF, hidden * hidden, channels),
            shape_of(BF, channels, hidden * hidden),
        ),
        [
            ((2 * rows * base, half), F32),
            ((2 * rows * GROUP, half), F32),
            ((hidden * hidden, channels), F32),
        ],
        macs=300_000_000,
    )

    outer_grad, scaled, divisor, left_grad, bias_grad, left_rows, left_t = call(
        first_kernel,
        dims,
        "scaled_outer_grad",
        (tree, *near, right_cols, live_t, update_adjoint, by_e),
        (
            shape_of(BF, hidden, lines, places),
            shape_of(BF, row_dev, places, channels),
            shape_of(BF, row_dev, places, channels),
            shape_of(F32, rows * row_dev, half),
            shape_of(F32, 1, channels),
            shape_of(BF, total, lines),
            shape_of(BF, lines, total),
        ),
        macs=800_000_000,
        room=32,
    )

    sent = left_grad.astype(BF)
    near = [
        lax.ppermute(sent, "col", [(a + d, a) for a in range(0, cols, STEP)])
        for d in range(1, STEP)
    ]
    right_keep, right_send = call(
        third_kernel,
        dims,
        "right_grad",
        (left_rows, outer_grad),
        (shape_of(F32, rows * base, half), shape_of(BF, rows * base, half)),
        [((2 * rows * base, half), F32)],
        macs=270_000_000,
        room=32,
    )
    *near, right_send = lax.optimization_barrier((*near, right_send))
    left_grad, sent = call(
        left_sum_kernel,
        dims,
        "left_sum",
        (left_grad, *near),
        (shape_of(F32, rows * row_dev, half), shape_of(BF, rows * row_dev, half)),
    )
    left_t, sent = lax.optimization_barrier((left_t, sent))
    far = [lax.ppermute(sent, "col", [(d, 0)]) for d in range(STEP, cols, STEP)]
    w_keep, w_send = call(
        second_kernel,
        dims,
        "outer_weight_grad",
        (left_t, right_cols, scaled),
        (shape_of(F32, hidden * hidden // 2, channels), shape_of(BF, hidden * hidden // 2, channels)),
        [((hidden, lines, places), BF), ((hidden * hidden, channels), F32)],
        macs=800_000_000,
        room=26,
    )
    w_send, *far = lax.optimization_barrier((w_send, *far))
    w_came = partner(w_send)
    right_came = partner(right_send)
    packed = call(
        pack_backward_kernel,
        dims,
        "pack_backward",
        (right_keep, right_came, w_keep, w_came, left_grad, *far),
        (shape_of(BF, pairs, 2 * base + w_lines + 2 * row_dev, half),),
    )[0]
    arrived = over_pairs(packed)

    send, keep, chunk = call(
        unpack_backward_kernel,
        dims,
        "unpack_backward",
        (arrived,),
        (
            shape_of(BF, base + pairs * row_dev, half),
            shape_of(BF, base + pairs * row_dev, half),
            shape_of(BF, w_lines, half),
        ),
        [((2 * base, half), F32)],
    )
    came = partner(send)
    grads, w_keep, w_send, small = call(
        projector_kernel,
        dims,
        "projector_grad",
        (keep, came, normed, live, bias_grad),
        (
            shape_of(BF, seqs * 2 * hidden, places),
            shape_of(F32, 2 * hidden, half),
            shape_of(BF, 2 * hidden, half),
            shape_of(BF, GROUP, half),
        ),
        [((2 * base, half), F32), ((places, base), F32)],
        macs=20_000_000,
    )
    w_came = partner(w_send)
    size = 2 * hidden + w_lines + GROUP
    own = call(
        pack_column_kernel, dims, "pack_column", (w_keep, w_came, chunk, small), (shape_of(BF, size, half),)
    )[0]
    parts = swap_parts(own, cols, STEP)
    pair_increment = call(
        pair_kernel,
        dims,
        "outer_pair",
        (left_t, right_cols, divisor, by_e_t, outgoing_offset[None]),
        (shape_of(BF, row_dev, places, channels),),
        [((hidden, lines, places), BF)],
        macs=800_000_000,
        room=26,
    )[0]
    *parts, pair_increment = lax.optimization_barrier((*parts, pair_increment))
    own = call(column_sum_kernel, dims, "column_sum", parts, (shape_of(BF, size, half),))[0]
    parts = swap_parts(own, cols, 1)
    alignment_gradient = call(
        align_kernel,
        dims,
        "alignment",
        (homolog_features, grads, lowering_matrix.T),
        (shape_of(BF, seqs, places, depth),),
        macs=200_000_000,
    )[0]
    *parts, alignment_gradient = lax.optimization_barrier((*parts, alignment_gradient))
    packed = call(pack_row_kernel, dims, "pack_row", parts, (shape_of(BF, pairs, size, half),))[0]
    mine = over_pairs(packed)
    other = partner(mine)
    projector, projector_bias, weight, bias = call(
        finish_kernel,
        dims,
        "finish",
        (mine, other),
        (
            shape_of(F32, 2 * hidden, depth),
            shape_of(F32, 1, 2 * hidden),
            shape_of(F32, hidden * hidden, channels),
            shape_of(F32, 1, channels),
        ),
        [((hidden * hidden, channels), F32)],
    )
    return (
        pair_increment,
        alignment_gradient,
        projector.T,
        projector_bias[0],
        weight,
        bias[0],
    )


def solution(mesh):
    in_specs = (
        P("row", "col", None),
        P("row", "col"),
        P("col"),
        P(),
        P(),
        P(),
        P(),
        P("row", "col", None),
    )
    out_specs = (P("row", "col", None), P("row", "col", None), P(), P(), P(), P())
    return jax.shard_map(
        per_device, mesh=mesh, in_specs=in_specs, out_specs=out_specs, check_vma=False
    )
```

```python
import functools

import jax
import jax.numpy as jnp
from jax import lax
from jax.experimental import pallas as pl
from jax.experimental.pallas import tpu as pltpu
from jax.sharding import PartitionSpec as P

PAIRED = 16
CHAINS = 4
BF = jnp.bfloat16
F32 = jnp.float32
STEP = 4
GROUP = 16
FUSE_E = 8
FUSE_I = 8


def dot(a, b, lhs, rhs):
    return lax.dot_general(a, b, (((lhs,), (rhs,)), ((), ())), preferred_element_type=F32)


def rows_at(start, size):
    return pl.ds(pl.multiple_of(start, GROUP), size)


def normal(values):
    center = values - jnp.mean(values, axis=-1, keepdims=True)
    spread = jnp.mean(center * center, axis=-1, keepdims=True)
    scale = lax.rsqrt(spread + 1e-05)
    return center * scale, scale


def project_kernel(dims, msa, present, label, weights, offset, normed, live_ref, send, keep, right, left):
    src, seqs, hidden, row_dev, places, half = dims
    pairs = src // 2
    me = lax.axis_index("row")
    core = lax.rem(me, 2)
    first = lax.axis_index("col") == 0
    seq = me * seqs + lax.broadcasted_iota(jnp.int32, (seqs, places), 0)
    chain = lax.rem(seq + (CHAINS - PAIRED % CHAINS), CHAINS)
    permitted = (seq < PAIRED) | (chain == jnp.broadcast_to(label[...], (seqs, places)))
    live = jnp.where(permitted & (present[...] == 1), 1.0, 0.0).astype(F32)
    live = jnp.concatenate([live, jnp.zeros((8 - seqs, places), F32)], axis=0)
    live_ref[...] = live
    weight = weights[...].astype(F32)
    right_w = weight[hidden:].astype(BF)
    left_w = jnp.concatenate([weight[:hidden]] * seqs, axis=0).T.astype(BF)
    lane = lax.broadcasted_iota(jnp.int32, left_w.shape, 1) // hidden
    column = jnp.broadcast_to(offset[...], (8, 2 * hidden)).T[hidden:, :1]
    total = jnp.zeros((places, seqs * hidden), F32)
    for s in range(seqs):
        value = normal(msa[s].astype(F32))[0].astype(BF)
        normed[s] = value
        out = (dot(right_w, value, 1, 1) + column) * live[s : s + 1]
        for h in range(2):
            right[pl.ds(h * seqs * hidden + s * hidden, hidden), :] = out[:, h * half : (h + 1) * half]
        total = total + dot(value, jnp.where(lane == s, left_w, jnp.zeros_like(left_w)), 1, 0)
    total = total + jnp.concatenate([offset[:, :hidden]] * seqs, axis=1)
    spot = lax.broadcasted_iota(jnp.int32, (8, seqs * hidden), 0)
    expand = jnp.where(spot == lax.broadcasted_iota(jnp.int32, (8, seqs * hidden), 1) // hidden, 1.0, 0.0)
    total = total * dot(live.T.astype(BF), expand.astype(BF), 1, 0)
    left[...] = jnp.where(first, total, 0.0)
    place = lax.broadcasted_iota(jnp.int32, (places, half), 0)
    slot = lax.broadcasted_iota(jnp.int32, (places, half), 1)
    base = seqs * hidden
    for ref, to in ((send, 1 - core), (keep, core)):
        pick = jnp.where(place == slot // row_dev * 2 * row_dev + to * row_dev + lax.rem(slot, row_dev), 1.0, 0.0)
        band = dot(live.astype(BF), pick.astype(BF), 1, 0)[:seqs]
        band = jnp.where(first, band, 0.0)
        own = jnp.where(to == 0, live[:seqs, :half], live[:seqs, half:])
        flags = jnp.concatenate([own, band, jnp.zeros((GROUP - 2 * seqs, half), F32)], axis=0)
        ref[pl.ds(0, base), :] = right[rows_at(to * base, base), :].astype(BF)
        ref[pl.ds(base, GROUP), :] = flags.astype(BF)
        for q in range(pairs):
            ref[pl.ds(base + GROUP + q * row_dev, row_dev), :] = left[
                rows_at(q * 2 * row_dev + to * row_dev, row_dev), :
            ].astype(BF)


def move_kernel(dims, block, out):
    out[...] = block[...]


def pack_forward_kernel(dims, keep, came, out):
    src, seqs, hidden, row_dev, places, half = dims
    core = lax.rem(lax.axis_index("row"), 2)
    base = seqs * hidden
    for ref, who in ((keep, core), (came, 1 - core)):
        value = ref[pl.ds(0, base), :]
        flags = ref[pl.ds(base, GROUP), :]
        for q in range(src // 2):
            out[q, rows_at(who * base, base), :] = value
            out[q, rows_at(2 * base + who * GROUP, GROUP), :] = flags
            out[q, rows_at(2 * base + 2 * GROUP + who * row_dev, row_dev), :] = ref[
                pl.ds(base + GROUP + q * row_dev, row_dev), :
            ]


def left_rows_kernel(dims, mine, out, tiles):
    src, seqs, hidden, row_dev, places, half = dims
    first = 2 * seqs * hidden
    for q in range(src // 2):
        tiles[pl.ds(q * 2 * GROUP, 2 * GROUP), :] = mine[q, first : first + 2 * GROUP, :].astype(F32)
    rows = [tiles[pl.ds(seqs + s, src, stride=GROUP), :] for s in range(seqs)]
    blocks = [jnp.concatenate(rows, axis=0)]
    for q in range(src // 2):
        tiles[pl.ds(q * 2 * row_dev, 2 * row_dev), :] = mine[q, first + 2 * GROUP :, :].astype(F32)
    for i in range(row_dev):
        tile = tiles[pl.ds(i, src, stride=row_dev), :]
        blocks.append(jnp.concatenate([tile[:, s * hidden : (s + 1) * hidden] for s in range(seqs)], axis=0))
    out[...] = jnp.concatenate(blocks, axis=1).astype(BF)


def unpack_right_kernel(dims, mine, other, weights, r_ref, live_t_ref, by_e, by_e_t, r_all, flags, w_all):
    src, seqs, hidden, row_dev, places, half = dims
    base = seqs * hidden
    lines = src * base
    core = lax.rem(lax.axis_index("row"), 2)
    for ref, h in ((mine, core), (other, 1 - core)):
        for q in range(src // 2):
            r_all[rows_at(h * lines + q * 2 * base, 2 * base), :] = ref[q, : 2 * base, :].astype(F32)
            flags[rows_at((h * src + 2 * q) * GROUP, 2 * GROUP), :] = ref[
                q, 2 * base : 2 * base + 2 * GROUP, :
            ].astype(F32)
    w_all[...] = weights[...].astype(F32)
    for e in range(hidden):
        for h in range(2):
            rows = [r_all[pl.ds(h * lines + s * hidden + e, src, stride=base), :] for s in range(seqs)]
            r_ref[e, :, pl.ds(h * half, half)] = jnp.concatenate(rows, axis=0).astype(BF)
    for e in range(0, hidden, 4):
        rows = [w_all[pl.ds(e + n, hidden, stride=hidden), :] for n in range(4)]
        part = jnp.concatenate(rows, axis=0)
        by_e[pl.ds(e * hidden, 4 * hidden), :] = part.astype(BF)
        by_e_t[:, pl.ds(e * hidden, 4 * hidden)] = part.T.astype(BF)
    for h in range(2):
        rows = [flags[pl.ds(h * src * GROUP + s, src, stride=GROUP), :] for s in range(seqs)]
        live_t_ref[pl.ds(h * half, half), :] = jnp.concatenate(rows, axis=0).T.astype(BF)


def first_kernel(dims, tree, near_1, near_2, near_3, r_ref, live_t, adjoint, weights, g_ref, s_ref, d_ref, left_ref, bias_ref, left_out, left_t):
    src, seqs, hidden, row_dev, places, half = dims
    pair = lax.axis_index("row") // 2
    spread = tree[...].astype(F32) + near_1[...].astype(F32) + near_2[...].astype(F32) + near_3[...].astype(F32)
    band = spread[:, :half].astype(BF)
    left = spread[:, half:]
    left_out[...] = left.astype(BF)
    left_t[...] = left.T.astype(BF)
    spot = lax.broadcasted_iota(jnp.int32, (half, half), 0) - pair * row_dev
    bias = jnp.zeros((1, half), F32)
    for i in range(row_dev):
        column = dot(band, jnp.where(spot == i, 1.0, 0.0).astype(BF), 1, 0).astype(BF)
        divisor = jnp.maximum(dot(live_t[...], column, 1, 0), 1.0)
        scaled = (adjoint[i].astype(F32) / divisor).astype(BF)
        d_ref[i] = divisor.astype(BF)
        s_ref[i] = scaled
        bias = bias + jnp.sum(scaled.astype(F32), axis=0, keepdims=True)
    bias_ref[...] = bias
    for i in range(row_dev):
        g = dot(weights[...], s_ref[i], 1, 1).astype(BF)
        g_ref[:, pl.ds(i * hidden, hidden), :] = g.reshape(hidden, hidden, places)
    acc = jnp.zeros((src * seqs, row_dev * hidden), F32)
    for e in range(0, hidden, FUSE_E):
        right = jnp.concatenate([r_ref[e + n] for n in range(FUSE_E)], axis=1)
        grad = jnp.concatenate([g_ref[e + n] for n in range(FUSE_E)], axis=1)
        acc = acc + dot(right, grad, 1, 1)
    for i in range(row_dev):
        block = acc[:, i * hidden : (i + 1) * hidden]
        left_ref[pl.ds(i, src, stride=row_dev), :] = jnp.concatenate(
            [block[s * src : (s + 1) * src] for s in range(seqs)], axis=1
        )


def outer_of(left_t, r_ref, outer):
    for e in range(outer.shape[0]):
        outer[e] = dot(left_t[...], r_ref[e], 1, 0).astype(BF)


def outer_row(outer, i, hidden):
    return outer[:, pl.ds(i * hidden, hidden), :].reshape(hidden * hidden, outer.shape[2])


def second_kernel(dims, left_t, r_ref, s_ref, keep, send, outer, held):
    src, seqs, hidden, row_dev, places, half = dims
    outer_of(left_t, r_ref, outer)
    acc = jnp.zeros((hidden * hidden, half), F32)
    for i in range(0, row_dev, FUSE_I):
        blocks = [outer_row(outer, i + n, hidden) for n in range(FUSE_I)]
        scaled = s_ref[pl.ds(i, FUSE_I)].reshape(FUSE_I * places, half)
        acc = acc + dot(jnp.concatenate(blocks, axis=1), scaled, 1, 0)
    held[...] = acc
    core = lax.rem(lax.axis_index("row"), 2)
    lines = hidden * hidden // 2
    keep[...] = held[rows_at(core * lines, lines), :]
    send[...] = held[rows_at((1 - core) * lines, lines), :].astype(BF)


def pair_kernel(dims, left_t, r_ref, d_ref, weights_t, offset, pair_ref, outer):
    src, seqs, hidden, row_dev, places, half = dims
    outer_of(left_t, r_ref, outer)
    for i in range(row_dev):
        before = dot(weights_t[...], outer_row(outer, i, hidden), 1, 0)
        pair_ref[i] = ((before.T + offset[...]) / d_ref[i].astype(F32)).astype(BF)


def third_kernel(dims, left, g_ref, keep, send, held):
    src, seqs, hidden, row_dev, places, half = dims
    base = seqs * hidden
    lines = src * base
    for e in range(hidden):
        grad = dot(left[...], g_ref[e], 1, 0)
        for h in range(2):
            for s in range(seqs):
                held[pl.ds(h * lines + s * hidden + e, src, stride=base), :] = grad[
                    s * src : (s + 1) * src, h * half : (h + 1) * half
                ]
    core = lax.rem(lax.axis_index("row"), 2)
    keep[...] = held[rows_at(core * lines, lines), :]
    send[...] = held[rows_at((1 - core) * lines, lines), :].astype(BF)


def pack_backward_kernel(dims, keep, came, w_keep, w_came, left, far_1, far_2, far_3, out):
    src, seqs, hidden, row_dev, places, half = dims
    pairs = src // 2
    lines = 2 * seqs * hidden
    w_lines = hidden * hidden // src
    total = left[...] + far_1[...].astype(F32) + far_2[...].astype(F32) + far_3[...].astype(F32)
    total = jnp.where(lax.axis_index("col") == 0, total, 0.0).astype(BF)
    for q in range(pairs):
        span = pl.ds(q * lines, lines)
        out[q, pl.ds(0, lines), :] = (keep[span, :] + came[span, :].astype(F32)).astype(BF)
        span = pl.ds(q * w_lines, w_lines)
        out[q, pl.ds(lines, w_lines), :] = (w_keep[span, :] + w_came[span, :].astype(F32)).astype(BF)
        out[q, pl.ds(lines + w_lines, 2 * row_dev), :] = total[q * 2 * row_dev : (q + 1) * 2 * row_dev]


def unpack_backward_kernel(dims, arrived, send, keep, chunk, held):
    src, seqs, hidden, row_dev, places, half = dims
    pairs = src // 2
    base = seqs * hidden
    w_lines = hidden * hidden // src
    core = lax.rem(lax.axis_index("row"), 2)
    total = arrived[0, : 2 * base + w_lines, :].astype(F32)
    for q in range(1, pairs):
        total = total + arrived[q, : 2 * base + w_lines, :].astype(F32)
    held[...] = total[: 2 * base]
    chunk[...] = total[2 * base :].astype(BF)
    for ref, to in ((send, 1 - core), (keep, core)):
        ref[pl.ds(0, base), :] = held[rows_at(to * base, base), :].astype(BF)
        for q in range(pairs):
            ref[pl.ds(base + q * row_dev, row_dev), :] = arrived[
                q, rows_at(2 * base + w_lines + to * row_dev, row_dev), :
            ]


def projector_kernel(dims, keep, came, normed, live, bias, grads, w_keep, w_send, small, right, left):
    src, seqs, hidden, row_dev, places, half = dims
    base = seqs * hidden
    core = lax.rem(lax.axis_index("row"), 2)
    for ref, who in ((keep, core), (came, 1 - core)):
        right[rows_at(who * base, base), :] = ref[pl.ds(0, base), :].astype(F32)
        for q in range(src // 2):
            left[rows_at(q * 2 * row_dev + who * row_dev, row_dev), :] = ref[
                pl.ds(base + q * row_dev, row_dev), :
            ].astype(F32)
    left_t = left[...].T
    weight = jnp.zeros((2 * hidden, places), F32)
    sums = jnp.zeros((8, 2 * hidden), F32)
    for s in range(seqs):
        span = slice(s * hidden, (s + 1) * hidden)
        right_s = jnp.concatenate([right[span, :], right[base + s * hidden : base + (s + 1) * hidden, :]], axis=1)
        grad = (jnp.concatenate([left_t[span], right_s], axis=0) * live[s : s + 1, :]).astype(BF)
        grads[pl.ds(s * 2 * hidden, 2 * hidden), :] = grad
        weight = weight + dot(grad, normed[s], 1, 0)
        sums = sums + dot(jnp.ones((8, places), BF), grad, 1, 1)
    low, high = weight[:, :half], weight[:, half:]
    w_keep[...] = jnp.where(core == 0, low, high)
    w_send[...] = jnp.where(core == 0, high, low).astype(BF)
    row = jnp.concatenate([sums[:1], jnp.zeros((1, half - 2 * hidden), F32)], axis=1)
    small[...] = bias_block(bias[...], row, half)


def bias_block(first, second, half):
    first_high, second_high = first.astype(BF).astype(F32), second.astype(BF).astype(F32)
    rows = [first_high, first - first_high, second_high, second - second_high]
    return jnp.concatenate(rows + [jnp.zeros((GROUP - 4, half), F32)], axis=0).astype(BF)


def align_kernel(dims, msa, grads, weights, out):
    src, seqs, hidden, row_dev, places, half = dims
    for s in range(seqs):
        grad = grads[pl.ds(s * 2 * hidden, 2 * hidden), :].astype(F32).T.astype(BF)
        grad = dot(grad, weights[...], 1, 0)
        value, scale = normal(msa[s].astype(F32))
        shift = jnp.mean(grad, axis=-1, keepdims=True)
        slope = jnp.mean(grad * value, axis=-1, keepdims=True)
        out[s] = (scale * (grad - shift - value * slope)).astype(BF)


def pack_column_kernel(dims, w_keep, w_came, chunk, small, out):
    weight = (w_keep[...] + w_came[...].astype(F32)).astype(BF)
    at = weight.shape[0]
    size = chunk.shape[0]
    out[pl.ds(0, at), :] = weight
    out[pl.ds(at, size), :] = chunk[...]
    out[pl.ds(at + size, GROUP), :] = small[...]


def sum_of_four(part_0, part_1, part_2, part_3):
    parts = [p[...].astype(F32) for p in (part_0, part_1, part_2, part_3)]
    total = (parts[0] + parts[1]) + (parts[2] + parts[3])
    at = total.shape[0] - GROUP
    last = total[at:]
    small = bias_block(last[0:1] + last[1:2], last[2:3] + last[3:4], last.shape[1])
    return total[:at].astype(BF), small


def column_sum_kernel(dims, part_0, part_1, part_2, part_3, out):
    total, small = sum_of_four(part_0, part_1, part_2, part_3)
    out[pl.ds(0, total.shape[0]), :] = total
    out[pl.ds(total.shape[0], GROUP), :] = small


def left_sum_kernel(dims, left, near_1, near_2, near_3, total, sent):
    value = left[...] + near_1[...].astype(F32) + near_2[...].astype(F32) + near_3[...].astype(F32)
    total[...] = value
    sent[...] = value.astype(BF)


def pack_row_kernel(dims, part_0, part_1, part_2, part_3, out):
    total, small = sum_of_four(part_0, part_1, part_2, part_3)
    for q in range(out.shape[0]):
        out[q, pl.ds(0, total.shape[0]), :] = total
        out[q, pl.ds(total.shape[0], GROUP), :] = small


def finish_kernel(dims, mine, other, projector, projector_bias, weight, bias, held):
    src, seqs, hidden, row_dev, places, half = dims
    core = lax.rem(lax.axis_index("row"), 2)
    w_lines = hidden * hidden // src
    at = 2 * hidden + w_lines
    sums = []
    small = jnp.zeros((GROUP, half), F32)
    for ref, who in ((mine, core), (other, 1 - core)):
        total = jnp.zeros((2 * hidden, half), F32)
        for q in range(src // 2):
            total = total + ref[q, : 2 * hidden, :].astype(F32)
            small = small + ref[q, at : at + GROUP, :].astype(F32)
            held[rows_at(who * (hidden * hidden // 2) + q * w_lines, w_lines), :] = ref[
                q, 2 * hidden : at, :
            ].astype(F32)
        sums.append(total)
    first = jnp.where(core == 0, sums[0], sums[1])
    second = jnp.where(core == 0, sums[1], sums[0])
    projector[...] = jnp.concatenate([first, second], axis=1)
    bias[...] = small[0:1] + small[1:2]
    projector_bias[...] = (small[2:3] + small[3:4])[:, : 2 * hidden]
    for c in range(hidden):
        weight[pl.ds(c * hidden, hidden), :] = held[pl.ds(c, hidden, stride=hidden), :]


def shape_of(dtype, *shape):
    return jax.ShapeDtypeStruct(shape, dtype)


def whole(*shape):
    return pl.BlockSpec(shape, lambda t: (0,) * len(shape))


def call(kernel, dims, name, args, outs, scratch=(), macs=0, room=16):
    size = sum(a.size * a.dtype.itemsize for a in args)
    size += sum(o.size * jnp.dtype(o.dtype).itemsize for o in outs)
    result = pl.pallas_call(
        functools.partial(kernel, dims),
        grid=(1,),
        in_specs=[whole(*a.shape) for a in args],
        out_specs=[whole(*o.shape) for o in outs],
        out_shape=list(outs),
        scratch_shapes=[pltpu.VMEM(s, t) for s, t in scratch],
        compiler_params=pltpu.CompilerParams(
            dimension_semantics=("arbitrary",), vmem_limit_bytes=room * 2**20
        ),
        cost_estimate=pl.CostEstimate(flops=40 * macs, bytes_accessed=size, transcendentals=0),
        name=name,
    )(*args)
    return result


def swap_parts(block, cols, unit):
    swaps = [lax.ppermute(block, "col", [(i, i ^ d * unit) for i in range(cols)]) for d in range(1, STEP)]
    return [block, *swaps]


def per_device(
    homolog_features,
    presence_indicator,
    polymer_label,
    lowering_matrix,
    lowering_offset,
    outgoing_matrix,
    outgoing_offset,
    update_adjoint,
):
    seqs, places, depth = homolog_features.shape
    hidden = lowering_matrix.shape[1] // 2
    channels = outgoing_matrix.shape[1]
    row_dev = update_adjoint.shape[0]
    rows, cols = lax.axis_size("row"), lax.axis_size("col")
    pairs, half = rows // 2, channels
    dims = (rows, seqs, hidden, row_dev, places, half)
    base = seqs * hidden
    total = rows * seqs
    lines = row_dev * hidden
    w_lines = hidden * hidden // rows
    swap = [(i, i ^ 1) for i in range(rows)]
    same_core = [list(range(c, rows, 2)) for c in range(2)]

    def partner(block):
        return lax.ppermute(block, "row", swap)

    def over_pairs(block):
        return lax.all_to_all(block, "row", 0, 0, axis_index_groups=same_core, tiled=True)

    size = base + GROUP + pairs * row_dev
    normed, live, send, keep = call(
        project_kernel,
        dims,
        "project",
        (homolog_features, presence_indicator, polymer_label[None], lowering_matrix.T, lowering_offset[None]),
        (
            shape_of(BF, seqs, places, depth),
            shape_of(F32, 8, places),
            shape_of(BF, size, half),
            shape_of(BF, size, half),
        ),
        [((2 * base, half), F32), ((places, base), F32)],
        macs=100_000_000,
        room=62,
    )
    came = partner(send)
    keep = call(move_kernel, dims, "move", (keep,), (shape_of(BF, size, half),))[0]
    came, keep = lax.optimization_barrier((came, keep))

    packed = call(
        pack_forward_kernel,
        dims,
        "pack_forward",
        (keep, came),
        (shape_of(BF, pairs, 2 * (base + GROUP + row_dev), half),),
    )[0]
    mine = over_pairs(packed)
    tree = call(
        left_rows_kernel,
        dims,
        "left_rows",
        (mine,),
        (shape_of(BF, total, half + lines),),
        [((rows * GROUP, half), F32)],
    )[0]
    leads = sorted(range(STEP, cols, STEP), key=lambda d: min(d, cols - d))
    far = [lax.ppermute(tree, "col", [(0, d)]) for d in leads]
    tree = sum(far, tree)
    near = swap_parts(tree, cols, 1)[1:]
    mine, tree = lax.optimization_barrier((mine, tree))
    other = partner(mine)
    right_cols, live_t, by_e, by_e_t = call(
        unpack_right_kernel,
        dims,
        "unpack_right",
        (mine, other, outgoing_matrix),
        (
            shape_of(BF, hidden, total, places),
            shape_of(BF, places, total),
            shape_of(BF, hidden * hidden, channels),
            shape_of(BF, channels, hidden * hidden),
        ),
        [
            ((2 * rows * base, half), F32),
            ((2 * rows * GROUP, half), F32),
            ((hidden * hidden, channels), F32),
        ],
        macs=300_000_000,
    )

    outer_grad, scaled, divisor, left_grad, bias_grad, left_rows, left_t = call(
        first_kernel,
        dims,
        "scaled_outer_grad",
        (tree, *near, right_cols, live_t, update_adjoint, by_e),
        (
            shape_of(BF, hidden, lines, places),
            shape_of(BF, row_dev, places, channels),
            shape_of(BF, row_dev, places, channels),
            shape_of(F32, rows * row_dev, half),
            shape_of(F32, 1, channels),
            shape_of(BF, total, lines),
            shape_of(BF, lines, total),
        ),
        macs=800_000_000,
        room=32,
    )

    sent = left_grad.astype(BF)
    near = swap_parts(sent, cols, 1)[1:]
    right_keep, right_send = call(
        third_kernel,
        dims,
        "right_grad",
        (left_rows, outer_grad),
        (shape_of(F32, rows * base, half), shape_of(BF, rows * base, half)),
        [((2 * rows * base, half), F32)],
        macs=270_000_000,
        room=32,
    )
    *near, right_send = lax.optimization_barrier((*near, right_send))
    left_grad, sent = call(
        left_sum_kernel,
        dims,
        "left_sum",
        (left_grad, *near),
        (shape_of(F32, rows * row_dev, half), shape_of(BF, rows * row_dev, half)),
    )
    left_t, sent = lax.optimization_barrier((left_t, sent))
    far = [lax.ppermute(sent, "col", [(d, 0)]) for d in leads]
    w_keep, w_send = call(
        second_kernel,
        dims,
        "outer_weight_grad",
        (left_t, right_cols, scaled),
        (shape_of(F32, hidden * hidden // 2, channels), shape_of(BF, hidden * hidden // 2, channels)),
        [((hidden, lines, places), BF), ((hidden * hidden, channels), F32)],
        macs=800_000_000,
        room=26,
    )
    w_send, *far = lax.optimization_barrier((w_send, *far))
    w_came = partner(w_send)
    right_came = partner(right_send)
    packed = call(
        pack_backward_kernel,
        dims,
        "pack_backward",
        (right_keep, right_came, w_keep, w_came, left_grad, *far),
        (shape_of(BF, pairs, 2 * base + w_lines + 2 * row_dev, half),),
    )[0]
    arrived = over_pairs(packed)

    send, keep, chunk = call(
        unpack_backward_kernel,
        dims,
        "unpack_backward",
        (arrived,),
        (
            shape_of(BF, base + pairs * row_dev, half),
            shape_of(BF, base + pairs * row_dev, half),
            shape_of(BF, w_lines, half),
        ),
        [((2 * base, half), F32)],
    )
    came = partner(send)
    grads, w_keep, w_send, small = call(
        projector_kernel,
        dims,
        "projector_grad",
        (keep, came, normed, live, bias_grad),
        (
            shape_of(BF, seqs * 2 * hidden, places),
            shape_of(F32, 2 * hidden, half),
            shape_of(BF, 2 * hidden, half),
            shape_of(BF, GROUP, half),
        ),
        [((2 * base, half), F32), ((places, base), F32)],
        macs=20_000_000,
    )
    w_came = partner(w_send)
    size = 2 * hidden + w_lines + GROUP
    own = call(
        pack_column_kernel, dims, "pack_column", (w_keep, w_came, chunk, small), (shape_of(BF, size, half),)
    )[0]
    parts = swap_parts(own, cols, STEP)
    pair_increment = call(
        pair_kernel,
        dims,
        "outer_pair",
        (left_t, right_cols, divisor, by_e_t, outgoing_offset[None]),
        (shape_of(BF, row_dev, places, channels),),
        [((hidden, lines, places), BF)],
        macs=800_000_000,
        room=26,
    )[0]
    *parts, pair_increment = lax.optimization_barrier((*parts, pair_increment))
    own = call(column_sum_kernel, dims, "column_sum", parts, (shape_of(BF, size, half),))[0]
    parts = swap_parts(own, cols, 1)
    alignment_gradient = call(
        align_kernel,
        dims,
        "alignment",
        (homolog_features, grads, lowering_matrix.T),
        (shape_of(BF, seqs, places, depth),),
        macs=200_000_000,
    )[0]
    *parts, alignment_gradient = lax.optimization_barrier((*parts, alignment_gradient))
    packed = call(pack_row_kernel, dims, "pack_row", parts, (shape_of(BF, pairs, size, half),))[0]
    mine = over_pairs(packed)
    other = partner(mine)
    projector, projector_bias, weight, bias = call(
        finish_kernel,
        dims,
        "finish",
        (mine, other),
        (
            shape_of(F32, 2 * hidden, depth),
            shape_of(F32, 1, 2 * hidden),
            shape_of(F32, hidden * hidden, channels),
            shape_of(F32, 1, channels),
        ),
        [((hidden * hidden, channels), F32)],
    )
    return (
        pair_increment,
        alignment_gradient,
        projector.T,
        projector_bias[0],
        weight,
        bias[0],
    )


def solution(mesh):
    in_specs = (
        P("row", "col", None),
        P("row", "col"),
        P("col"),
        P(),
        P(),
        P(),
        P(),
        P("row", "col", None),
    )
    out_specs = (P("row", "col", None), P("row", "col", None), P(), P(), P(), P())
    return jax.shard_map(
        per_device, mesh=mesh, in_specs=in_specs, out_specs=out_specs, check_vma=False
    )
```

```python
import functools

import jax
import jax.numpy as jnp
from jax import lax
from jax.experimental import pallas as pl
from jax.experimental.pallas import tpu as pltpu
from jax.sharding import PartitionSpec as P

PAIRED = 16
CHAINS = 4
BF = jnp.bfloat16
F32 = jnp.float32
STEP = 4
GROUP = 16
FUSE_E = 8
FUSE_I = 8


def dot(a, b, lhs, rhs):
    return lax.dot_general(a, b, (((lhs,), (rhs,)), ((), ())), preferred_element_type=F32)


def rows_at(start, size):
    return pl.ds(pl.multiple_of(start, GROUP), size)


def normal(values):
    center = values - jnp.mean(values, axis=-1, keepdims=True)
    spread = jnp.mean(center * center, axis=-1, keepdims=True)
    scale = lax.rsqrt(spread + 1e-05)
    return center * scale, scale


def project_kernel(dims, msa, present, label, weights, offset, normed, live_ref, send, keep, right, left):
    src, seqs, hidden, row_dev, places, half = dims
    pairs = src // 2
    me = lax.axis_index("row")
    core = lax.rem(me, 2)
    first = lax.axis_index("col") == 0
    seq = me * seqs + lax.broadcasted_iota(jnp.int32, (seqs, places), 0)
    chain = lax.rem(seq + (CHAINS - PAIRED % CHAINS), CHAINS)
    permitted = (seq < PAIRED) | (chain == jnp.broadcast_to(label[...], (seqs, places)))
    live = jnp.where(permitted & (present[...] == 1), 1.0, 0.0).astype(F32)
    live = jnp.concatenate([live, jnp.zeros((8 - seqs, places), F32)], axis=0)
    live_ref[...] = live
    weight = weights[...].astype(F32)
    right_w = weight[hidden:].astype(BF)
    left_w = jnp.concatenate([weight[:hidden]] * seqs, axis=0).T.astype(BF)
    lane = lax.broadcasted_iota(jnp.int32, left_w.shape, 1) // hidden
    column = jnp.broadcast_to(offset[...], (8, 2 * hidden)).T[hidden:, :1]
    total = jnp.zeros((places, seqs * hidden), F32)
    for s in range(seqs):
        value = normal(msa[s].astype(F32))[0].astype(BF)
        normed[s] = value
        out = (dot(right_w, value, 1, 1) + column) * live[s : s + 1]
        for h in range(2):
            right[pl.ds(h * seqs * hidden + s * hidden, hidden), :] = out[:, h * half : (h + 1) * half]
        total = total + dot(value, jnp.where(lane == s, left_w, jnp.zeros_like(left_w)), 1, 0)
    total = total + jnp.concatenate([offset[:, :hidden]] * seqs, axis=1)
    spot = lax.broadcasted_iota(jnp.int32, (8, seqs * hidden), 0)
    expand = jnp.where(spot == lax.broadcasted_iota(jnp.int32, (8, seqs * hidden), 1) // hidden, 1.0, 0.0)
    total = total * dot(live.T.astype(BF), expand.astype(BF), 1, 0)
    left[...] = jnp.where(first, total, 0.0)
    place = lax.broadcasted_iota(jnp.int32, (places, half), 0)
    slot = lax.broadcasted_iota(jnp.int32, (places, half), 1)
    base = seqs * hidden
    for ref, to in ((send, 1 - core), (keep, core)):
        pick = jnp.where(place == slot // row_dev * 2 * row_dev + to * row_dev + lax.rem(slot, row_dev), 1.0, 0.0)
        band = dot(live.astype(BF), pick.astype(BF), 1, 0)[:seqs]
        band = jnp.where(first, band, 0.0)
        own = jnp.where(to == 0, live[:seqs, :half], live[:seqs, half:])
        flags = jnp.concatenate([own, band, jnp.zeros((GROUP - 2 * seqs, half), F32)], axis=0)
        ref[pl.ds(0, base), :] = right[rows_at(to * base, base), :].astype(BF)
        ref[pl.ds(base, GROUP), :] = flags.astype(BF)
        for q in range(pairs):
            ref[pl.ds(base + GROUP + q * row_dev, row_dev), :] = left[
                rows_at(q * 2 * row_dev + to * row_dev, row_dev), :
            ].astype(BF)


def move_kernel(dims, block, out):
    out[...] = block[...]


def pack_forward_kernel(dims, keep, came, out):
    src, seqs, hidden, row_dev, places, half = dims
    core = lax.rem(lax.axis_index("row"), 2)
    base = seqs * hidden
    own, partner = [ref[pl.ds(base, GROUP), :].astype(F32)[: GROUP // 2] for ref in (keep, came)]
    flags = jnp.where(
        core == 0, jnp.concatenate([own, partner], axis=0), jnp.concatenate([partner, own], axis=0)
    ).astype(BF)
    for q in range(src // 2):
        out[q, pl.ds(2 * base, GROUP), :] = flags
    for ref, who in ((keep, core), (came, 1 - core)):
        value = ref[pl.ds(0, base), :]
        for q in range(src // 2):
            out[q, rows_at(who * base, base), :] = value
            out[q, rows_at(2 * base + GROUP + who * row_dev, row_dev), :] = ref[
                pl.ds(base + GROUP + q * row_dev, row_dev), :
            ]


def left_rows_kernel(dims, mine, out, tiles):
    src, seqs, hidden, row_dev, places, half = dims
    first = 2 * seqs * hidden
    for q in range(src // 2):
        tiles[pl.ds(q * GROUP, GROUP), :] = mine[q, first : first + GROUP, :].astype(F32)
    rows = [tiles[pl.ds(seqs + s, src, stride=GROUP // 2), :] for s in range(seqs)]
    blocks = [jnp.concatenate(rows, axis=0)]
    for q in range(src // 2):
        tiles[pl.ds(q * 2 * row_dev, 2 * row_dev), :] = mine[q, first + GROUP :, :].astype(F32)
    for i in range(row_dev):
        tile = tiles[pl.ds(i, src, stride=row_dev), :]
        blocks.append(jnp.concatenate([tile[:, s * hidden : (s + 1) * hidden] for s in range(seqs)], axis=0))
    out[...] = jnp.concatenate(blocks, axis=1).astype(BF)


def unpack_right_kernel(dims, mine, other, weights, r_ref, live_t_ref, by_e, by_e_t, r_all, flags, w_all):
    src, seqs, hidden, row_dev, places, half = dims
    base = seqs * hidden
    lines = src * base
    core = lax.rem(lax.axis_index("row"), 2)
    for ref, h in ((mine, core), (other, 1 - core)):
        for q in range(src // 2):
            r_all[rows_at(h * lines + q * 2 * base, 2 * base), :] = ref[q, : 2 * base, :].astype(F32)
            flags[rows_at((h * src // 2 + q) * GROUP, GROUP), :] = ref[
                q, 2 * base : 2 * base + GROUP, :
            ].astype(F32)
    w_all[...] = weights[...].astype(F32)
    for e in range(hidden):
        for h in range(2):
            rows = [r_all[pl.ds(h * lines + s * hidden + e, src, stride=base), :] for s in range(seqs)]
            r_ref[e, :, pl.ds(h * half, half)] = jnp.concatenate(rows, axis=0).astype(BF)
    for e in range(0, hidden, 4):
        rows = [w_all[pl.ds(e + n, hidden, stride=hidden), :] for n in range(4)]
        part = jnp.concatenate(rows, axis=0)
        by_e[pl.ds(e * hidden, 4 * hidden), :] = part.astype(BF)
        by_e_t[:, pl.ds(e * hidden, 4 * hidden)] = part.T.astype(BF)
    for h in range(2):
        rows = [flags[pl.ds(h * src * GROUP // 2 + s, src, stride=GROUP // 2), :] for s in range(seqs)]
        live_t_ref[pl.ds(h * half, half), :] = jnp.concatenate(rows, axis=0).T.astype(BF)


def first_kernel(dims, tree, near_1, near_2, near_3, r_ref, live_t, adjoint, weights, g_ref, s_ref, d_ref, left_ref, bias_ref, left_out, left_t):
    src, seqs, hidden, row_dev, places, half = dims
    pair = lax.axis_index("row") // 2
    spread = tree[...].astype(F32) + near_1[...].astype(F32) + near_2[...].astype(F32) + near_3[...].astype(F32)
    band = spread[:, :half].astype(BF)
    left = spread[:, half:]
    left_out[...] = left.astype(BF)
    left_t[...] = left.T.astype(BF)
    spot = lax.broadcasted_iota(jnp.int32, (half, half), 0) - pair * row_dev
    bias = jnp.zeros((1, half), F32)
    for i in range(row_dev):
        column = dot(band, jnp.where(spot == i, 1.0, 0.0).astype(BF), 1, 0).astype(BF)
        divisor = jnp.maximum(dot(live_t[...], column, 1, 0), 1.0)
        scaled = (adjoint[i].astype(F32) / divisor).astype(BF)
        d_ref[i] = divisor.astype(BF)
        s_ref[i] = scaled
        bias = bias + jnp.sum(scaled.astype(F32), axis=0, keepdims=True)
    bias_ref[...] = bias
    for i in range(row_dev):
        g = dot(weights[...], s_ref[i], 1, 1).astype(BF)
        g_ref[:, pl.ds(i * hidden, hidden), :] = g.reshape(hidden, hidden, places)
    acc = jnp.zeros((src * seqs, row_dev * hidden), F32)
    for e in range(0, hidden, FUSE_E):
        right = jnp.concatenate([r_ref[e + n] for n in range(FUSE_E)], axis=1)
        grad = jnp.concatenate([g_ref[e + n] for n in range(FUSE_E)], axis=1)
        acc = acc + dot(right, grad, 1, 1)
    for i in range(row_dev):
        block = acc[:, i * hidden : (i + 1) * hidden]
        left_ref[pl.ds(i, src, stride=row_dev), :] = jnp.concatenate(
            [block[s * src : (s + 1) * src] for s in range(seqs)], axis=1
        )


def outer_of(left_t, r_ref, outer):
    for e in range(outer.shape[0]):
        outer[e] = dot(left_t[...], r_ref[e], 1, 0).astype(BF)


def outer_row(outer, i, hidden):
    return outer[:, pl.ds(i * hidden, hidden), :].reshape(hidden * hidden, outer.shape[2])


def second_kernel(dims, left_t, r_ref, s_ref, keep, send, outer, held):
    src, seqs, hidden, row_dev, places, half = dims
    outer_of(left_t, r_ref, outer)
    acc = jnp.zeros((hidden * hidden, half), F32)
    for i in range(0, row_dev, FUSE_I):
        blocks = [outer_row(outer, i + n, hidden) for n in range(FUSE_I)]
        scaled = s_ref[pl.ds(i, FUSE_I)].reshape(FUSE_I * places, half)
        acc = acc + dot(jnp.concatenate(blocks, axis=1), scaled, 1, 0)
    held[...] = acc
    core = lax.rem(lax.axis_index("row"), 2)
    lines = hidden * hidden // 2
    keep[...] = held[rows_at(core * lines, lines), :]
    send[...] = held[rows_at((1 - core) * lines, lines), :].astype(BF)


def pair_kernel(dims, left_t, r_ref, d_ref, weights_t, offset, pair_ref, outer):
    src, seqs, hidden, row_dev, places, half = dims
    outer_of(left_t, r_ref, outer)
    for i in range(row_dev):
        before = dot(weights_t[...], outer_row(outer, i, hidden), 1, 0)
        pair_ref[i] = ((before.T + offset[...]) / d_ref[i].astype(F32)).astype(BF)


def third_kernel(dims, left, g_ref, keep, send, held):
    src, seqs, hidden, row_dev, places, half = dims
    base = seqs * hidden
    lines = src * base
    for e in range(hidden):
        grad = dot(left[...], g_ref[e], 1, 0)
        for h in range(2):
            for s in range(seqs):
                held[pl.ds(h * lines + s * hidden + e, src, stride=base), :] = grad[
                    s * src : (s + 1) * src, h * half : (h + 1) * half
                ]
    core = lax.rem(lax.axis_index("row"), 2)
    keep[...] = held[rows_at(core * lines, lines), :]
    send[...] = held[rows_at((1 - core) * lines, lines), :].astype(BF)


def pack_backward_kernel(dims, keep, came, w_keep, w_came, left, far_1, far_2, far_3, out):
    src, seqs, hidden, row_dev, places, half = dims
    pairs = src // 2
    lines = 2 * seqs * hidden
    w_lines = hidden * hidden // src
    total = left[...] + far_1[...].astype(F32) + far_2[...].astype(F32) + far_3[...].astype(F32)
    total = jnp.where(lax.axis_index("col") == 0, total, 0.0).astype(BF)
    for q in range(pairs):
        span = pl.ds(q * lines, lines)
        out[q, pl.ds(0, lines), :] = (keep[span, :] + came[span, :].astype(F32)).astype(BF)
        span = pl.ds(q * w_lines, w_lines)
        out[q, pl.ds(lines, w_lines), :] = (w_keep[span, :] + w_came[span, :].astype(F32)).astype(BF)
        out[q, pl.ds(lines + w_lines, 2 * row_dev), :] = total[q * 2 * row_dev : (q + 1) * 2 * row_dev]


def unpack_backward_kernel(dims, arrived, send, keep, chunk, held):
    src, seqs, hidden, row_dev, places, half = dims
    pairs = src // 2
    base = seqs * hidden
    w_lines = hidden * hidden // src
    core = lax.rem(lax.axis_index("row"), 2)
    total = arrived[0, : 2 * base + w_lines, :].astype(F32)
    for q in range(1, pairs):
        total = total + arrived[q, : 2 * base + w_lines, :].astype(F32)
    held[...] = total[: 2 * base]
    chunk[...] = total[2 * base :].astype(BF)
    for ref, to in ((send, 1 - core), (keep, core)):
        ref[pl.ds(0, base), :] = held[rows_at(to * base, base), :].astype(BF)
        for q in range(pairs):
            ref[pl.ds(base + q * row_dev, row_dev), :] = arrived[
                q, rows_at(2 * base + w_lines + to * row_dev, row_dev), :
            ]


def projector_kernel(dims, keep, came, normed, live, bias, grads, w_keep, w_send, small, right, left):
    src, seqs, hidden, row_dev, places, half = dims
    base = seqs * hidden
    core = lax.rem(lax.axis_index("row"), 2)
    for ref, who in ((keep, core), (came, 1 - core)):
        right[rows_at(who * base, base), :] = ref[pl.ds(0, base), :].astype(F32)
        for q in range(src // 2):
            left[rows_at(q * 2 * row_dev + who * row_dev, row_dev), :] = ref[
                pl.ds(base + q * row_dev, row_dev), :
            ].astype(F32)
    left_t = left[...].T
    weight = jnp.zeros((2 * hidden, places), F32)
    sums = jnp.zeros((8, 2 * hidden), F32)
    for s in range(seqs):
        span = slice(s * hidden, (s + 1) * hidden)
        right_s = jnp.concatenate([right[span, :], right[base + s * hidden : base + (s + 1) * hidden, :]], axis=1)
        grad = (jnp.concatenate([left_t[span], right_s], axis=0) * live[s : s + 1, :]).astype(BF)
        grads[pl.ds(s * 2 * hidden, 2 * hidden), :] = grad
        weight = weight + dot(grad, normed[s], 1, 0)
        sums = sums + dot(jnp.ones((8, places), BF), grad, 1, 1)
    low, high = weight[:, :half], weight[:, half:]
    w_keep[...] = jnp.where(core == 0, low, high)
    w_send[...] = jnp.where(core == 0, high, low).astype(BF)
    row = jnp.concatenate([sums[:1], jnp.zeros((1, half - 2 * hidden), F32)], axis=1)
    small[...] = bias_block(bias[...], row, half)


def bias_block(first, second, half):
    first_high, second_high = first.astype(BF).astype(F32), second.astype(BF).astype(F32)
    rows = [first_high, first - first_high, second_high, second - second_high]
    return jnp.concatenate(rows + [jnp.zeros((GROUP - 4, half), F32)], axis=0).astype(BF)


def align_kernel(dims, msa, grads, weights, out):
    src, seqs, hidden, row_dev, places, half = dims
    for s in range(seqs):
        grad = grads[pl.ds(s * 2 * hidden, 2 * hidden), :].astype(F32).T.astype(BF)
        grad = dot(grad, weights[...], 1, 0)
        value, scale = normal(msa[s].astype(F32))
        shift = jnp.mean(grad, axis=-1, keepdims=True)
        slope = jnp.mean(grad * value, axis=-1, keepdims=True)
        out[s] = (scale * (grad - shift - value * slope)).astype(BF)


def pack_column_kernel(dims, w_keep, w_came, chunk, small, out):
    weight = (w_keep[...] + w_came[...].astype(F32)).astype(BF)
    at = weight.shape[0]
    size = chunk.shape[0]
    out[pl.ds(0, at), :] = weight
    out[pl.ds(at, size), :] = chunk[...]
    out[pl.ds(at + size, GROUP), :] = small[...]


def sum_of_four(part_0, part_1, part_2, part_3):
    parts = [p[...].astype(F32) for p in (part_0, part_1, part_2, part_3)]
    total = (parts[0] + parts[1]) + (parts[2] + parts[3])
    at = total.shape[0] - GROUP
    last = total[at:]
    small = bias_block(last[0:1] + last[1:2], last[2:3] + last[3:4], last.shape[1])
    return total[:at].astype(BF), small


def column_sum_kernel(dims, part_0, part_1, part_2, part_3, out):
    total, small = sum_of_four(part_0, part_1, part_2, part_3)
    out[pl.ds(0, total.shape[0]), :] = total
    out[pl.ds(total.shape[0], GROUP), :] = small


def left_sum_kernel(dims, left, near_1, near_2, near_3, total, sent):
    value = left[...] + near_1[...].astype(F32) + near_2[...].astype(F32) + near_3[...].astype(F32)
    total[...] = value
    sent[...] = value.astype(BF)


def pack_row_kernel(dims, part_0, part_1, part_2, part_3, out):
    total, small = sum_of_four(part_0, part_1, part_2, part_3)
    for q in range(out.shape[0]):
        out[q, pl.ds(0, total.shape[0]), :] = total
        out[q, pl.ds(total.shape[0], GROUP), :] = small


def finish_kernel(dims, mine, other, projector, projector_bias, weight, bias):
    src, seqs, hidden, row_dev, places, half = dims
    core = lax.rem(lax.axis_index("row"), 2)
    w_lines = hidden * hidden // src
    at = 2 * hidden + w_lines
    sums = []
    small = jnp.zeros((GROUP, half), F32)
    for ref, who in ((mine, core), (other, 1 - core)):
        total = jnp.zeros((2 * hidden, half), F32)
        for q in range(src // 2):
            total = total + ref[q, : 2 * hidden, :].astype(F32)
            small = small + ref[q, at : at + GROUP, :].astype(F32)
            for n in range(w_lines // hidden):
                e = (who * (src // 2) + q) * (w_lines // hidden) + n
                line = 2 * hidden + n * hidden
                weight[pl.ds(e, hidden, stride=hidden), :] = ref[q, line : line + hidden, :].astype(F32)
        sums.append(total)
    first = jnp.where(core == 0, sums[0], sums[1])
    second = jnp.where(core == 0, sums[1], sums[0])
    projector[...] = jnp.concatenate([first, second], axis=1)
    bias[...] = small[0:1] + small[1:2]
    projector_bias[...] = (small[2:3] + small[3:4])[:, : 2 * hidden]


def shape_of(dtype, *shape):
    return jax.ShapeDtypeStruct(shape, dtype)


def whole(*shape):
    return pl.BlockSpec(shape, lambda t: (0,) * len(shape))


def call(kernel, dims, name, args, outs, scratch=(), macs=0, room=16):
    size = sum(a.size * a.dtype.itemsize for a in args)
    size += sum(o.size * jnp.dtype(o.dtype).itemsize for o in outs)
    result = pl.pallas_call(
        functools.partial(kernel, dims),
        grid=(1,),
        in_specs=[whole(*a.shape) for a in args],
        out_specs=[whole(*o.shape) for o in outs],
        out_shape=list(outs),
        scratch_shapes=[pltpu.VMEM(s, t) for s, t in scratch],
        compiler_params=pltpu.CompilerParams(
            dimension_semantics=("arbitrary",), vmem_limit_bytes=room * 2**20
        ),
        cost_estimate=pl.CostEstimate(flops=40 * macs, bytes_accessed=size, transcendentals=0),
        name=name,
    )(*args)
    return result


def swap_parts(block, cols, unit):
    swaps = [lax.ppermute(block, "col", [(i, i ^ d * unit) for i in range(cols)]) for d in range(1, STEP)]
    return [block, *swaps]


def per_device(
    homolog_features,
    presence_indicator,
    polymer_label,
    lowering_matrix,
    lowering_offset,
    outgoing_matrix,
    outgoing_offset,
    update_adjoint,
):
    seqs, places, depth = homolog_features.shape
    hidden = lowering_matrix.shape[1] // 2
    channels = outgoing_matrix.shape[1]
    row_dev = update_adjoint.shape[0]
    rows, cols = lax.axis_size("row"), lax.axis_size("col")
    pairs, half = rows // 2, channels
    dims = (rows, seqs, hidden, row_dev, places, half)
    base = seqs * hidden
    total = rows * seqs
    lines = row_dev * hidden
    w_lines = hidden * hidden // rows
    swap = [(i, i ^ 1) for i in range(rows)]
    same_core = [list(range(c, rows, 2)) for c in range(2)]

    def partner(block):
        return lax.ppermute(block, "row", swap)

    def over_pairs(block):
        return lax.all_to_all(block, "row", 0, 0, axis_index_groups=same_core, tiled=True)

    size = base + GROUP + pairs * row_dev
    normed, live, send, keep = call(
        project_kernel,
        dims,
        "project",
        (homolog_features, presence_indicator, polymer_label[None], lowering_matrix.T, lowering_offset[None]),
        (
            shape_of(BF, seqs, places, depth),
            shape_of(F32, 8, places),
            shape_of(BF, size, half),
            shape_of(BF, size, half),
        ),
        [((2 * base, half), F32), ((places, base), F32)],
        macs=100_000_000,
        room=62,
    )
    came = partner(send)
    keep = call(move_kernel, dims, "move", (keep,), (shape_of(BF, size, half),))[0]
    came, keep = lax.optimization_barrier((came, keep))

    packed = call(
        pack_forward_kernel,
        dims,
        "pack_forward",
        (keep, came),
        (shape_of(BF, pairs, 2 * (base + row_dev) + GROUP, half),),
    )[0]
    mine = over_pairs(packed)
    tree = call(
        left_rows_kernel,
        dims,
        "left_rows",
        (mine,),
        (shape_of(BF, total, half + lines),),
        [((rows * GROUP, half), F32)],
    )[0]
    leads = sorted(range(STEP, cols, STEP), key=lambda d: min(d, cols - d))
    far = [lax.ppermute(tree, "col", [(0, d)]) for d in leads]
    tree = sum(far, tree)
    near = swap_parts(tree, cols, 1)[1:]
    mine, tree = lax.optimization_barrier((mine, tree))
    other = partner(mine)
    right_cols, live_t, by_e, by_e_t = call(
        unpack_right_kernel,
        dims,
        "unpack_right",
        (mine, other, outgoing_matrix),
        (
            shape_of(BF, hidden, total, places),
            shape_of(BF, places, total),
            shape_of(BF, hidden * hidden, channels),
            shape_of(BF, channels, hidden * hidden),
        ),
        [
            ((2 * rows * base, half), F32),
            ((rows * GROUP, half), F32),
            ((hidden * hidden, channels), F32),
        ],
        macs=300_000_000,
    )

    outer_grad, scaled, divisor, left_grad, bias_grad, left_rows, left_t = call(
        first_kernel,
        dims,
        "scaled_outer_grad",
        (tree, *near, right_cols, live_t, update_adjoint, by_e),
        (
            shape_of(BF, hidden, lines, places),
            shape_of(BF, row_dev, places, channels),
            shape_of(BF, row_dev, places, channels),
            shape_of(F32, rows * row_dev, half),
            shape_of(F32, 1, channels),
            shape_of(BF, total, lines),
            shape_of(BF, lines, total),
        ),
        macs=800_000_000,
        room=32,
    )

    sent = left_grad.astype(BF)
    near = swap_parts(sent, cols, 1)[1:]
    right_keep, right_send = call(
        third_kernel,
        dims,
        "right_grad",
        (left_rows, outer_grad),
        (shape_of(F32, rows * base, half), shape_of(BF, rows * base, half)),
        [((2 * rows * base, half), F32)],
        macs=270_000_000,
        room=32,
    )
    *near, right_send = lax.optimization_barrier((*near, right_send))
    left_grad, sent = call(
        left_sum_kernel,
        dims,
        "left_sum",
        (left_grad, *near),
        (shape_of(F32, rows * row_dev, half), shape_of(BF, rows * row_dev, half)),
    )
    left_t, sent = lax.optimization_barrier((left_t, sent))
    far = [lax.ppermute(sent, "col", [(d, 0)]) for d in leads]
    w_keep, w_send = call(
        second_kernel,
        dims,
        "outer_weight_grad",
        (left_t, right_cols, scaled),
        (shape_of(F32, hidden * hidden // 2, channels), shape_of(BF, hidden * hidden // 2, channels)),
        [((hidden, lines, places), BF), ((hidden * hidden, channels), F32)],
        macs=800_000_000,
        room=26,
    )
    w_send, *far = lax.optimization_barrier((w_send, *far))
    w_came = partner(w_send)
    right_came = partner(right_send)
    packed = call(
        pack_backward_kernel,
        dims,
        "pack_backward",
        (right_keep, right_came, w_keep, w_came, left_grad, *far),
        (shape_of(BF, pairs, 2 * base + w_lines + 2 * row_dev, half),),
    )[0]
    arrived = over_pairs(packed)

    send, keep, chunk = call(
        unpack_backward_kernel,
        dims,
        "unpack_backward",
        (arrived,),
        (
            shape_of(BF, base + pairs * row_dev, half),
            shape_of(BF, base + pairs * row_dev, half),
            shape_of(BF, w_lines, half),
        ),
        [((2 * base, half), F32)],
    )
    came = partner(send)
    grads, w_keep, w_send, small = call(
        projector_kernel,
        dims,
        "projector_grad",
        (keep, came, normed, live, bias_grad),
        (
            shape_of(BF, seqs * 2 * hidden, places),
            shape_of(F32, 2 * hidden, half),
            shape_of(BF, 2 * hidden, half),
            shape_of(BF, GROUP, half),
        ),
        [((2 * base, half), F32), ((places, base), F32)],
        macs=20_000_000,
    )
    w_came = partner(w_send)
    size = 2 * hidden + w_lines + GROUP
    own = call(
        pack_column_kernel, dims, "pack_column", (w_keep, w_came, chunk, small), (shape_of(BF, size, half),)
    )[0]
    parts = swap_parts(own, cols, STEP)
    pair_increment = call(
        pair_kernel,
        dims,
        "outer_pair",
        (left_t, right_cols, divisor, by_e_t, outgoing_offset[None]),
        (shape_of(BF, row_dev, places, channels),),
        [((hidden, lines, places), BF)],
        macs=800_000_000,
        room=26,
    )[0]
    *parts, pair_increment = lax.optimization_barrier((*parts, pair_increment))
    own = call(column_sum_kernel, dims, "column_sum", parts, (shape_of(BF, size, half),))[0]
    parts = swap_parts(own, cols, 1)
    alignment_gradient = call(
        align_kernel,
        dims,
        "alignment",
        (homolog_features, grads, lowering_matrix.T),
        (shape_of(BF, seqs, places, depth),),
        macs=200_000_000,
    )[0]
    *parts, alignment_gradient = lax.optimization_barrier((*parts, alignment_gradient))
    packed = call(pack_row_kernel, dims, "pack_row", parts, (shape_of(BF, pairs, size, half),))[0]
    mine = over_pairs(packed)
    other = partner(mine)
    projector, projector_bias, weight, bias = call(
        finish_kernel,
        dims,
        "finish",
        (mine, other),
        (
            shape_of(F32, 2 * hidden, depth),
            shape_of(F32, 1, 2 * hidden),
            shape_of(F32, hidden * hidden, channels),
            shape_of(F32, 1, channels),
        ),
    )
    return (
        pair_increment,
        alignment_gradient,
        projector.T,
        projector_bias[0],
        weight,
        bias[0],
    )


def solution(mesh):
    in_specs = (
        P("row", "col", None),
        P("row", "col"),
        P("col"),
        P(),
        P(),
        P(),
        P(),
        P("row", "col", None),
    )
    out_specs = (P("row", "col", None), P("row", "col", None), P(), P(), P(), P())
    return jax.shard_map(
        per_device, mesh=mesh, in_specs=in_specs, out_specs=out_specs, check_vma=False
    )
```

```python
import functools

import jax
import jax.numpy as jnp
from jax import lax
from jax.experimental import pallas as pl
from jax.experimental.pallas import tpu as pltpu
from jax.sharding import PartitionSpec as P

PAIRED = 16
CHAINS = 4
BF = jnp.bfloat16
F32 = jnp.float32
STEP = 4
GROUP = 16
FUSE_E = 8
FUSE_I = 8


def dot(a, b, lhs, rhs):
    return lax.dot_general(a, b, (((lhs,), (rhs,)), ((), ())), preferred_element_type=F32)


def rows_at(start, size):
    return pl.ds(pl.multiple_of(start, GROUP), size)


def normal(values):
    center = values - jnp.mean(values, axis=-1, keepdims=True)
    spread = jnp.mean(center * center, axis=-1, keepdims=True)
    scale = lax.rsqrt(spread + 1e-05)
    return center * scale, scale


def project_kernel(dims, msa, present, label, weights, offset, normed, live_ref, send, keep, right, left):
    src, seqs, hidden, row_dev, places, half = dims
    pairs = src // 2
    me = lax.axis_index("row")
    core = lax.rem(me, 2)
    first = lax.axis_index("col") == 0
    seq = me * seqs + lax.broadcasted_iota(jnp.int32, (seqs, places), 0)
    chain = lax.rem(seq + (CHAINS - PAIRED % CHAINS), CHAINS)
    permitted = (seq < PAIRED) | (chain == jnp.broadcast_to(label[...], (seqs, places)))
    live = jnp.where(permitted & (present[...] == 1), 1.0, 0.0).astype(F32)
    live = jnp.concatenate([live, jnp.zeros((8 - seqs, places), F32)], axis=0)
    live_ref[...] = live
    weight = weights[...].astype(F32)
    right_w = weight[hidden:].astype(BF)
    left_w = jnp.concatenate([weight[:hidden]] * seqs, axis=0).T.astype(BF)
    lane = lax.broadcasted_iota(jnp.int32, left_w.shape, 1) // hidden
    column = jnp.broadcast_to(offset[...], (8, 2 * hidden)).T[hidden:, :1]
    total = jnp.zeros((places, seqs * hidden), F32)
    for s in range(seqs):
        value = normal(msa[s].astype(F32))[0].astype(BF)
        normed[s] = value
        out = (dot(right_w, value, 1, 1) + column) * live[s : s + 1]
        for h in range(2):
            right[pl.ds(h * seqs * hidden + s * hidden, hidden), :] = out[:, h * half : (h + 1) * half]
        total = total + dot(value, jnp.where(lane == s, left_w, jnp.zeros_like(left_w)), 1, 0)
    total = total + jnp.concatenate([offset[:, :hidden]] * seqs, axis=1)
    spot = lax.broadcasted_iota(jnp.int32, (8, seqs * hidden), 0)
    expand = jnp.where(spot == lax.broadcasted_iota(jnp.int32, (8, seqs * hidden), 1) // hidden, 1.0, 0.0)
    total = total * dot(live.T.astype(BF), expand.astype(BF), 1, 0)
    left[...] = jnp.where(first, total, 0.0)
    place = lax.broadcasted_iota(jnp.int32, (places, half), 0)
    slot = lax.broadcasted_iota(jnp.int32, (places, half), 1)
    base = seqs * hidden
    for ref, to in ((send, 1 - core), (keep, core)):
        pick = jnp.where(place == slot // row_dev * 2 * row_dev + to * row_dev + lax.rem(slot, row_dev), 1.0, 0.0)
        band = dot(live.astype(BF), pick.astype(BF), 1, 0)[:seqs]
        band = jnp.where(first, band, 0.0)
        own = jnp.where(to == 0, live[:seqs, :half], live[:seqs, half:])
        flags = jnp.concatenate([own, band, jnp.zeros((GROUP - 2 * seqs, half), F32)], axis=0)
        ref[pl.ds(0, base), :] = right[rows_at(to * base, base), :].astype(BF)
        ref[pl.ds(base, GROUP), :] = flags.astype(BF)
        for q in range(pairs):
            ref[pl.ds(base + GROUP + q * row_dev, row_dev), :] = left[
                rows_at(q * 2 * row_dev + to * row_dev, row_dev), :
            ].astype(BF)


def move_kernel(dims, block, out):
    out[...] = block[...]


def pack_forward_kernel(dims, keep, came, out):
    src, seqs, hidden, row_dev, places, half = dims
    core = lax.rem(lax.axis_index("row"), 2)
    base = seqs * hidden
    own, partner = [ref[pl.ds(base, GROUP), :].astype(F32)[: GROUP // 2] for ref in (keep, came)]
    flags = jnp.where(
        core == 0, jnp.concatenate([own, partner], axis=0), jnp.concatenate([partner, own], axis=0)
    ).astype(BF)
    for q in range(src // 2):
        out[q, pl.ds(2 * base, GROUP), :] = flags
    for ref, who in ((keep, core), (came, 1 - core)):
        value = ref[pl.ds(0, base), :]
        for q in range(src // 2):
            out[q, rows_at(who * base, base), :] = value
            out[q, rows_at(2 * base + GROUP + who * row_dev, row_dev), :] = ref[
                pl.ds(base + GROUP + q * row_dev, row_dev), :
            ]


def left_rows_kernel(dims, mine, out, tiles):
    src, seqs, hidden, row_dev, places, half = dims
    first = 2 * seqs * hidden
    for q in range(src // 2):
        tiles[pl.ds(q * GROUP, GROUP), :] = mine[q, first : first + GROUP, :].astype(F32)
    rows = [tiles[pl.ds(seqs + s, src, stride=GROUP // 2), :] for s in range(seqs)]
    blocks = [jnp.concatenate(rows, axis=0)]
    for q in range(src // 2):
        tiles[pl.ds(q * 2 * row_dev, 2 * row_dev), :] = mine[q, first + GROUP :, :].astype(F32)
    for i in range(row_dev):
        tile = tiles[pl.ds(i, src, stride=row_dev), :]
        blocks.append(jnp.concatenate([tile[:, s * hidden : (s + 1) * hidden] for s in range(seqs)], axis=0))
    out[...] = jnp.concatenate(blocks, axis=1).astype(BF)


def unpack_right_kernel(dims, mine, other, weights, r_ref, live_t_ref, by_e, by_e_t, r_all, flags, w_all):
    src, seqs, hidden, row_dev, places, half = dims
    base = seqs * hidden
    lines = src * base
    core = lax.rem(lax.axis_index("row"), 2)
    for ref, h in ((mine, core), (other, 1 - core)):
        for q in range(src // 2):
            r_all[rows_at(h * lines + q * 2 * base, 2 * base), :] = ref[q, : 2 * base, :].astype(F32)
            flags[rows_at((h * src // 2 + q) * GROUP, GROUP), :] = ref[
                q, 2 * base : 2 * base + GROUP, :
            ].astype(F32)
    w_all[...] = weights[...].astype(F32)
    for e in range(hidden):
        for h in range(2):
            rows = [r_all[pl.ds(h * lines + s * hidden + e, src, stride=base), :] for s in range(seqs)]
            r_ref[e, :, pl.ds(h * half, half)] = jnp.concatenate(rows, axis=0).astype(BF)
    for e in range(0, hidden, 4):
        rows = [w_all[pl.ds(e + n, hidden, stride=hidden), :] for n in range(4)]
        part = jnp.concatenate(rows, axis=0)
        by_e[pl.ds(e * hidden, 4 * hidden), :] = part.astype(BF)
        by_e_t[:, pl.ds(e * hidden, 4 * hidden)] = part.T.astype(BF)
    for h in range(2):
        rows = [flags[pl.ds(h * src * GROUP // 2 + s, src, stride=GROUP // 2), :] for s in range(seqs)]
        live_t_ref[pl.ds(h * half, half), :] = jnp.concatenate(rows, axis=0).T.astype(BF)


def first_kernel(dims, tree, near_1, near_2, near_3, r_ref, live_t, adjoint, weights, g_ref, s_ref, d_ref, left_ref, bias_ref, left_out, left_t):
    src, seqs, hidden, row_dev, places, half = dims
    pair = lax.axis_index("row") // 2
    spread = tree[...].astype(F32) + near_1[...].astype(F32) + near_2[...].astype(F32) + near_3[...].astype(F32)
    band = spread[:, :half].astype(BF)
    left = spread[:, half:]
    left_out[...] = left.astype(BF)
    left_t[...] = left.T.astype(BF)
    spot = lax.broadcasted_iota(jnp.int32, (half, half), 0) - pair * row_dev
    bias = jnp.zeros((1, half), F32)
    for i in range(row_dev):
        column = dot(band, jnp.where(spot == i, 1.0, 0.0).astype(BF), 1, 0).astype(BF)
        divisor = jnp.maximum(dot(live_t[...], column, 1, 0), 1.0)
        scaled = (adjoint[i].astype(F32) / divisor).astype(BF)
        d_ref[i] = divisor.astype(BF)
        s_ref[i] = scaled
        bias = bias + jnp.sum(scaled.astype(F32), axis=0, keepdims=True)
    bias_ref[...] = bias
    for i in range(row_dev):
        g = dot(weights[...], s_ref[i], 1, 1).astype(BF)
        g_ref[:, pl.ds(i * hidden, hidden), :] = g.reshape(hidden, hidden, places)
    acc = jnp.zeros((src * seqs, row_dev * hidden), F32)
    for e in range(0, hidden, FUSE_E):
        right = jnp.concatenate([r_ref[e + n] for n in range(FUSE_E)], axis=1)
        grad = jnp.concatenate([g_ref[e + n] for n in range(FUSE_E)], axis=1)
        acc = acc + dot(right, grad, 1, 1)
    for i in range(row_dev):
        block = acc[:, i * hidden : (i + 1) * hidden]
        left_ref[pl.ds(i, src, stride=row_dev), :] = jnp.concatenate(
            [block[s * src : (s + 1) * src] for s in range(seqs)], axis=1
        )


def outer_of(left_t, r_ref, outer):
    for e in range(outer.shape[0]):
        outer[e] = dot(left_t[...], r_ref[e], 1, 0).astype(BF)


def outer_row(outer, i, hidden):
    return outer[:, pl.ds(i * hidden, hidden), :].reshape(hidden * hidden, outer.shape[2])


def second_kernel(dims, left_t, r_ref, s_ref, keep, send, outer, held):
    src, seqs, hidden, row_dev, places, half = dims
    outer_of(left_t, r_ref, outer)
    acc = jnp.zeros((hidden * hidden, half), F32)
    for i in range(0, row_dev, FUSE_I):
        blocks = [outer_row(outer, i + n, hidden) for n in range(FUSE_I)]
        scaled = s_ref[pl.ds(i, FUSE_I)].reshape(FUSE_I * places, half)
        acc = acc + dot(jnp.concatenate(blocks, axis=1), scaled, 1, 0)
    held[...] = acc
    core = lax.rem(lax.axis_index("row"), 2)
    lines = hidden * hidden // 2
    keep[...] = held[rows_at(core * lines, lines), :]
    send[...] = held[rows_at((1 - core) * lines, lines), :].astype(BF)


def pair_kernel(dims, left_t, r_ref, d_ref, weights_t, offset, pair_ref, outer):
    src, seqs, hidden, row_dev, places, half = dims
    outer_of(left_t, r_ref, outer)
    for i in range(row_dev):
        before = dot(weights_t[...], outer_row(outer, i, hidden), 1, 0)
        pair_ref[i] = ((before.T + offset[...]) / d_ref[i].astype(F32)).astype(BF)


def third_kernel(dims, left, g_ref, keep, send, held):
    src, seqs, hidden, row_dev, places, half = dims
    base = seqs * hidden
    lines = src * base
    for e in range(hidden):
        grad = dot(left[...], g_ref[e], 1, 0)
        for h in range(2):
            for s in range(seqs):
                held[pl.ds(h * lines + s * hidden + e, src, stride=base), :] = grad[
                    s * src : (s + 1) * src, h * half : (h + 1) * half
                ]
    core = lax.rem(lax.axis_index("row"), 2)
    keep[...] = held[rows_at(core * lines, lines), :]
    send[...] = held[rows_at((1 - core) * lines, lines), :].astype(BF)


def pack_backward_kernel(dims, keep, came, w_keep, w_came, left, far_1, far_2, far_3, out):
    src, seqs, hidden, row_dev, places, half = dims
    pairs = src // 2
    lines = 2 * seqs * hidden
    w_lines = hidden * hidden // src
    total = left[...] + far_1[...].astype(F32) + far_2[...].astype(F32) + far_3[...].astype(F32)
    total = jnp.where(lax.axis_index("col") == 0, total, 0.0).astype(BF)
    for q in range(pairs):
        span = pl.ds(q * lines, lines)
        out[q, pl.ds(0, lines), :] = (keep[span, :] + came[span, :].astype(F32)).astype(BF)
        span = pl.ds(q * w_lines, w_lines)
        out[q, pl.ds(lines, w_lines), :] = (w_keep[span, :] + w_came[span, :].astype(F32)).astype(BF)
        out[q, pl.ds(lines + w_lines, 2 * row_dev), :] = total[q * 2 * row_dev : (q + 1) * 2 * row_dev]


def unpack_backward_kernel(dims, arrived, send, keep, chunk, held):
    src, seqs, hidden, row_dev, places, half = dims
    pairs = src // 2
    base = seqs * hidden
    w_lines = hidden * hidden // src
    core = lax.rem(lax.axis_index("row"), 2)
    total = arrived[0, : 2 * base + w_lines, :].astype(F32)
    for q in range(1, pairs):
        total = total + arrived[q, : 2 * base + w_lines, :].astype(F32)
    held[...] = total[: 2 * base]
    chunk[...] = total[2 * base :].astype(BF)
    for ref, to in ((send, 1 - core), (keep, core)):
        ref[pl.ds(0, base), :] = held[rows_at(to * base, base), :].astype(BF)
        for q in range(pairs):
            ref[pl.ds(base + q * row_dev, row_dev), :] = arrived[
                q, rows_at(2 * base + w_lines + to * row_dev, row_dev), :
            ]


def projector_kernel(dims, keep, came, normed, live, bias, grads, w_keep, w_send, small, right, left):
    src, seqs, hidden, row_dev, places, half = dims
    base = seqs * hidden
    core = lax.rem(lax.axis_index("row"), 2)
    for ref, who in ((keep, core), (came, 1 - core)):
        right[rows_at(who * base, base), :] = ref[pl.ds(0, base), :].astype(F32)
        for q in range(src // 2):
            left[rows_at(q * 2 * row_dev + who * row_dev, row_dev), :] = ref[
                pl.ds(base + q * row_dev, row_dev), :
            ].astype(F32)
    left_t = left[...].T
    weight = jnp.zeros((2 * hidden, places), F32)
    sums = jnp.zeros((8, 2 * hidden), F32)
    for s in range(seqs):
        span = slice(s * hidden, (s + 1) * hidden)
        right_s = jnp.concatenate([right[span, :], right[base + s * hidden : base + (s + 1) * hidden, :]], axis=1)
        grad = (jnp.concatenate([left_t[span], right_s], axis=0) * live[s : s + 1, :]).astype(BF)
        grads[pl.ds(s * 2 * hidden, 2 * hidden), :] = grad
        weight = weight + dot(grad, normed[s], 1, 0)
        sums = sums + dot(jnp.ones((8, places), BF), grad, 1, 1)
    low, high = weight[:, :half], weight[:, half:]
    w_keep[...] = jnp.where(core == 0, low, high)
    w_send[...] = jnp.where(core == 0, high, low).astype(BF)
    row = jnp.concatenate([sums[:1], jnp.zeros((1, half - 2 * hidden), F32)], axis=1)
    small[...] = bias_block(bias[...], row, half)


def bias_block(first, second, half):
    first_high, second_high = first.astype(BF).astype(F32), second.astype(BF).astype(F32)
    rows = [first_high, first - first_high, second_high, second - second_high]
    return jnp.concatenate(rows + [jnp.zeros((GROUP - 4, half), F32)], axis=0).astype(BF)


def align_kernel(dims, msa, grads, weights, out):
    src, seqs, hidden, row_dev, places, half = dims
    for s in range(seqs):
        grad = grads[pl.ds(s * 2 * hidden, 2 * hidden), :].astype(F32).T.astype(BF)
        grad = dot(grad, weights[...], 1, 0)
        value, scale = normal(msa[s].astype(F32))
        shift = jnp.mean(grad, axis=-1, keepdims=True)
        slope = jnp.mean(grad * value, axis=-1, keepdims=True)
        out[s] = (scale * (grad - shift - value * slope)).astype(BF)


def pack_column_kernel(dims, w_keep, w_came, chunk, small, out):
    weight = (w_keep[...] + w_came[...].astype(F32)).astype(BF)
    at = weight.shape[0]
    size = chunk.shape[0]
    out[pl.ds(0, at), :] = weight
    out[pl.ds(at, size), :] = chunk[...]
    out[pl.ds(at + size, GROUP), :] = small[...]


def sum_of_four(part_0, part_1, part_2, part_3):
    parts = [p[...].astype(F32) for p in (part_0, part_1, part_2, part_3)]
    total = (parts[0] + parts[1]) + (parts[2] + parts[3])
    at = total.shape[0] - GROUP
    last = total[at:]
    small = bias_block(last[0:1] + last[1:2], last[2:3] + last[3:4], last.shape[1])
    return total[:at].astype(BF), small


def column_sum_kernel(dims, part_0, part_1, part_2, part_3, out):
    total, small = sum_of_four(part_0, part_1, part_2, part_3)
    out[pl.ds(0, total.shape[0]), :] = total
    out[pl.ds(total.shape[0], GROUP), :] = small


def left_sum_kernel(dims, left, near_1, near_2, near_3, total, sent):
    value = left[...] + near_1[...].astype(F32) + near_2[...].astype(F32) + near_3[...].astype(F32)
    total[...] = value
    sent[...] = value.astype(BF)


def pack_row_kernel(dims, part_0, part_1, part_2, part_3, out):
    total, small = sum_of_four(part_0, part_1, part_2, part_3)
    for q in range(out.shape[0]):
        out[q, pl.ds(0, total.shape[0]), :] = total
        out[q, pl.ds(total.shape[0], GROUP), :] = small


def finish_kernel(dims, mine, other, projector, projector_bias, weight, bias):
    src, seqs, hidden, row_dev, places, half = dims
    core = lax.rem(lax.axis_index("row"), 2)
    w_lines = hidden * hidden // src
    at = 2 * hidden + w_lines
    sums = []
    small = jnp.zeros((GROUP, half), F32)
    for ref, who in ((mine, core), (other, 1 - core)):
        total = jnp.zeros((2 * hidden, half), F32)
        for q in range(src // 2):
            total = total + ref[q, : 2 * hidden, :].astype(F32)
            small = small + ref[q, at : at + GROUP, :].astype(F32)
            for n in range(w_lines // hidden):
                e = (who * (src // 2) + q) * (w_lines // hidden) + n
                line = 2 * hidden + n * hidden
                weight[pl.ds(e, hidden, stride=hidden), :] = ref[q, line : line + hidden, :].astype(F32)
        sums.append(total)
    first = jnp.where(core == 0, sums[0], sums[1])
    second = jnp.where(core == 0, sums[1], sums[0])
    projector[...] = jnp.concatenate([first, second], axis=1)
    bias[...] = small[0:1] + small[1:2]
    projector_bias[...] = (small[2:3] + small[3:4])[:, : 2 * hidden]


def shape_of(dtype, *shape):
    return jax.ShapeDtypeStruct(shape, dtype)


def whole(*shape):
    return pl.BlockSpec(shape, lambda t: (0,) * len(shape))


def call(kernel, dims, name, args, outs, scratch=(), macs=0, room=16):
    size = sum(a.size * a.dtype.itemsize for a in args)
    size += sum(o.size * jnp.dtype(o.dtype).itemsize for o in outs)
    result = pl.pallas_call(
        functools.partial(kernel, dims),
        grid=(1,),
        in_specs=[whole(*a.shape) for a in args],
        out_specs=[whole(*o.shape) for o in outs],
        out_shape=list(outs),
        scratch_shapes=[pltpu.VMEM(s, t) for s, t in scratch],
        compiler_params=pltpu.CompilerParams(
            dimension_semantics=("arbitrary",), vmem_limit_bytes=room * 2**20
        ),
        cost_estimate=pl.CostEstimate(flops=40 * macs, bytes_accessed=size, transcendentals=0),
        name=name,
    )(*args)
    return result


def swap_parts(block, cols, unit):
    order = sorted(range(1, STEP), key=lambda d: min(d * unit, cols - d * unit))
    swaps = [lax.ppermute(block, "col", [(i, i ^ d * unit) for i in range(cols)]) for d in order]
    return [block, *swaps]


def per_device(
    homolog_features,
    presence_indicator,
    polymer_label,
    lowering_matrix,
    lowering_offset,
    outgoing_matrix,
    outgoing_offset,
    update_adjoint,
):
    seqs, places, depth = homolog_features.shape
    hidden = lowering_matrix.shape[1] // 2
    channels = outgoing_matrix.shape[1]
    row_dev = update_adjoint.shape[0]
    rows, cols = lax.axis_size("row"), lax.axis_size("col")
    pairs, half = rows // 2, channels
    dims = (rows, seqs, hidden, row_dev, places, half)
    base = seqs * hidden
    total = rows * seqs
    lines = row_dev * hidden
    w_lines = hidden * hidden // rows
    swap = [(i, i ^ 1) for i in range(rows)]
    same_core = [list(range(c, rows, 2)) for c in range(2)]

    def partner(block):
        return lax.ppermute(block, "row", swap)

    def over_pairs(block):
        return lax.all_to_all(block, "row", 0, 0, axis_index_groups=same_core, tiled=True)

    size = base + GROUP + pairs * row_dev
    normed, live, send, keep = call(
        project_kernel,
        dims,
        "project",
        (homolog_features, presence_indicator, polymer_label[None], lowering_matrix.T, lowering_offset[None]),
        (
            shape_of(BF, seqs, places, depth),
            shape_of(F32, 8, places),
            shape_of(BF, size, half),
            shape_of(BF, size, half),
        ),
        [((2 * base, half), F32), ((places, base), F32)],
        macs=100_000_000,
        room=62,
    )
    came = partner(send)
    keep = call(move_kernel, dims, "move", (keep,), (shape_of(BF, size, half),))[0]
    came, keep = lax.optimization_barrier((came, keep))

    packed = call(
        pack_forward_kernel,
        dims,
        "pack_forward",
        (keep, came),
        (shape_of(BF, pairs, 2 * (base + row_dev) + GROUP, half),),
    )[0]
    mine = over_pairs(packed)
    tree = call(
        left_rows_kernel,
        dims,
        "left_rows",
        (mine,),
        (shape_of(BF, total, half + lines),),
        [((rows * GROUP, half), F32)],
    )[0]
    leads = sorted(range(STEP, cols, STEP), key=lambda d: min(d, cols - d))
    far = [lax.ppermute(tree, "col", [(0, d)]) for d in leads]
    tree = sum(far, tree)
    near = swap_parts(tree, cols, 1)[1:]
    mine, tree = lax.optimization_barrier((mine, tree))
    other = partner(mine)
    right_cols, live_t, by_e, by_e_t = call(
        unpack_right_kernel,
        dims,
        "unpack_right",
        (mine, other, outgoing_matrix),
        (
            shape_of(BF, hidden, total, places),
            shape_of(BF, places, total),
            shape_of(BF, hidden * hidden, channels),
            shape_of(BF, channels, hidden * hidden),
        ),
        [
            ((2 * rows * base, half), F32),
            ((rows * GROUP, half), F32),
            ((hidden * hidden, channels), F32),
        ],
        macs=300_000_000,
    )

    outer_grad, scaled, divisor, left_grad, bias_grad, left_rows, left_t = call(
        first_kernel,
        dims,
        "scaled_outer_grad",
        (tree, *near, right_cols, live_t, update_adjoint, by_e),
        (
            shape_of(BF, hidden, lines, places),
            shape_of(BF, row_dev, places, channels),
            shape_of(BF, row_dev, places, channels),
            shape_of(F32, rows * row_dev, half),
            shape_of(F32, 1, channels),
            shape_of(BF, total, lines),
            shape_of(BF, lines, total),
        ),
        macs=800_000_000,
        room=32,
    )

    sent = left_grad.astype(BF)
    near = swap_parts(sent, cols, 1)[1:]
    right_keep, right_send = call(
        third_kernel,
        dims,
        "right_grad",
        (left_rows, outer_grad),
        (shape_of(F32, rows * base, half), shape_of(BF, rows * base, half)),
        [((2 * rows * base, half), F32)],
        macs=270_000_000,
        room=32,
    )
    *near, right_send = lax.optimization_barrier((*near, right_send))
    left_grad, sent = call(
        left_sum_kernel,
        dims,
        "left_sum",
        (left_grad, *near),
        (shape_of(F32, rows * row_dev, half), shape_of(BF, rows * row_dev, half)),
    )
    left_t, sent = lax.optimization_barrier((left_t, sent))
    far = [lax.ppermute(sent, "col", [(d, 0)]) for d in leads]
    w_keep, w_send = call(
        second_kernel,
        dims,
        "outer_weight_grad",
        (left_t, right_cols, scaled),
        (shape_of(F32, hidden * hidden // 2, channels), shape_of(BF, hidden * hidden // 2, channels)),
        [((hidden, lines, places), BF), ((hidden * hidden, channels), F32)],
        macs=800_000_000,
        room=26,
    )
    w_send, *far = lax.optimization_barrier((w_send, *far))
    w_came = partner(w_send)
    right_came = partner(right_send)
    packed = call(
        pack_backward_kernel,
        dims,
        "pack_backward",
        (right_keep, right_came, w_keep, w_came, left_grad, *far),
        (shape_of(BF, pairs, 2 * base + w_lines + 2 * row_dev, half),),
    )[0]
    arrived = over_pairs(packed)

    send, keep, chunk = call(
        unpack_backward_kernel,
        dims,
        "unpack_backward",
        (arrived,),
        (
            shape_of(BF, base + pairs * row_dev, half),
            shape_of(BF, base + pairs * row_dev, half),
            shape_of(BF, w_lines, half),
        ),
        [((2 * base, half), F32)],
    )
    came = partner(send)
    grads, w_keep, w_send, small = call(
        projector_kernel,
        dims,
        "projector_grad",
        (keep, came, normed, live, bias_grad),
        (
            shape_of(BF, seqs * 2 * hidden, places),
            shape_of(F32, 2 * hidden, half),
            shape_of(BF, 2 * hidden, half),
            shape_of(BF, GROUP, half),
        ),
        [((2 * base, half), F32), ((places, base), F32)],
        macs=20_000_000,
    )
    w_came = partner(w_send)
    size = 2 * hidden + w_lines + GROUP
    own = call(
        pack_column_kernel, dims, "pack_column", (w_keep, w_came, chunk, small), (shape_of(BF, size, half),)
    )[0]
    parts = swap_parts(own, cols, STEP)
    pair_increment = call(
        pair_kernel,
        dims,
        "outer_pair",
        (left_t, right_cols, divisor, by_e_t, outgoing_offset[None]),
        (shape_of(BF, row_dev, places, channels),),
        [((hidden, lines, places), BF)],
        macs=800_000_000,
        room=26,
    )[0]
    *parts, pair_increment = lax.optimization_barrier((*parts, pair_increment))
    own = call(column_sum_kernel, dims, "column_sum", parts, (shape_of(BF, size, half),))[0]
    parts = swap_parts(own, cols, 1)
    alignment_gradient = call(
        align_kernel,
        dims,
        "alignment",
        (homolog_features, grads, lowering_matrix.T),
        (shape_of(BF, seqs, places, depth),),
        macs=200_000_000,
    )[0]
    *parts, alignment_gradient = lax.optimization_barrier((*parts, alignment_gradient))
    packed = call(pack_row_kernel, dims, "pack_row", parts, (shape_of(BF, pairs, size, half),))[0]
    mine = over_pairs(packed)
    other = partner(mine)
    projector, projector_bias, weight, bias = call(
        finish_kernel,
        dims,
        "finish",
        (mine, other),
        (
            shape_of(F32, 2 * hidden, depth),
            shape_of(F32, 1, 2 * hidden),
            shape_of(F32, hidden * hidden, channels),
            shape_of(F32, 1, channels),
        ),
    )
    return (
        pair_increment,
        alignment_gradient,
        projector.T,
        projector_bias[0],
        weight,
        bias[0],
    )


def solution(mesh):
    in_specs = (
        P("row", "col", None),
        P("row", "col"),
        P("col"),
        P(),
        P(),
        P(),
        P(),
        P("row", "col", None),
    )
    out_specs = (P("row", "col", None), P("row", "col", None), P(), P(), P(), P())
    return jax.shard_map(
        per_device, mesh=mesh, in_specs=in_specs, out_specs=out_specs, check_vma=False
    )
```
